32 devices in a mesh: dp: 8 (over z, x), head: 4 (over y, core).
Axes of the slice: x: 2, y: 2, z: 4, core: 2. Of those that a mesh axis runs over, the one named last changes fastest.
Arguments:
- post_in: float32 [16384, 512], P(('dp', 'head')), may hold values from -6 to 6
- dual_in: float32 [16384, 512], P(('dp', 'head')), may hold values from -6 to 6
- segment_ids: int32 [8, 2048], P('dp'), may hold values from 0 to 7, never falling along the last dimension, each value on 1 to 1024 neighbouring positions
- post_cot: float32 [16384, 512], P(('dp', 'head')), may hold values from -6 to 6
- dual_cot: float32 [16384, 512], P(('dp', 'head')), may hold values from -6 to 6
- attend_weight: float32 [512, 1536], P('dp', 'head'), may hold values from -0.25 to 0.25
- output_weight: float32 [512, 512], P('head', 'dp'), may hold values from -1 to 1
- expand_weight: float32 [512, 2048], P('dp', 'head'), may hold values from -0.25 to 0.25
- contract_weight: float32 [2048, 512], P('head', 'dp'), may hold values from -0.125 to 0.125
- head_bias: float32 [8, 384], P('head', 'dp'), may hold values from -4 to 4
- norm_params: float32 [6, 512], replicated, may hold values from -1.2 to 1.6, as said below
- attend_momentum: float32 [512, 1536], P('dp', 'head'), may hold values from -0.0048828125 to 0.0048828125
- output_momentum: float32 [512, 512], P('head', 'dp'), may hold values from -0.0048828125 to 0.0048828125
- expand_momentum: float32 [512, 2048], P('dp', 'head'), may hold values from -0.0048828125 to 0.0048828125
- contract_momentum: float32 [2048, 512], P('head', 'dp'), may hold values from -0.0048828125 to 0.0048828125
- bias_momentum: float32 [8, 384], P('head', 'dp'), may hold values from -0.01953125 to 0.01953125
- norm_momentum: float32 [6, 512], replicated, may hold values from -0.0048828125 to 0.0048828125
- attend_variance: float32 [512, 1536], P('dp', 'head'), may hold values from 7.138615e-07 to 2.855446e-06
- output_variance: float32 [512, 512], P('head', 'dp'), may hold values from 7.138615e-07 to 2.855446e-06
- expand_variance: float32 [512, 2048], P('dp', 'head'), may hold values from 7.138615e-07 to 2.855446e-06
- contract_variance: float32 [2048, 512], P('head', 'dp'), may hold values from 7.138615e-07 to 2.855446e-06
- bias_variance: float32 [8, 384], P('head', 'dp'), may hold values from 1.1421784e-05 to 4.5687135e-05
- norm_variance: float32 [6, 512], replicated, may hold values from 3.1727177e-07 to 1.2690871e-06
- clip_limit: float32 [1], replicated, may hold values from 1 to 2
Outputs:
- post_out: float32 [16384, 512], P(('dp', 'head'))
- dual_out: float32 [16384, 512], P(('dp', 'head'))
- post_grad: float32 [16384, 512], P(('dp', 'head'))
- grad_norm: float32 [1], replicated
- attend_momentum_new: float32 [512, 1536], P('dp', 'head')
- attend_variance_new: float32 [512, 1536], P('dp', 'head')
- attend_master_new: float32 [512, 1536], P('dp', 'head')
- attend_copy_new: bfloat16 [512, 1536], P('dp', 'head')
- output_momentum_new: float32 [512, 512], P('head', 'dp')
- output_variance_new: float32 [512, 512], P('head', 'dp')
- output_master_new: float32 [512, 512], P('head', 'dp')
- output_copy_new: bfloat16 [512, 512], P('head', 'dp')
- expand_momentum_new: float32 [512, 2048], P('dp', 'head')
- expand_variance_new: float32 [512, 2048], P('dp', 'head')
- expand_master_new: float32 [512, 2048], P('dp', 'head')
- expand_copy_new: bfloat16 [512, 2048], P('dp', 'head')
- contract_momentum_new: float32 [2048, 512], P('head', 'dp')
- contract_variance_new: float32 [2048, 512], P('head', 'dp')
- contract_master_new: float32 [2048, 512], P('head', 'dp')
- contract_copy_new: bfloat16 [2048, 512], P('head', 'dp')
- bias_momentum_new: float32 [8, 384], P('head', 'dp')
- bias_variance_new: float32 [8, 384], P('head', 'dp')
- bias_master_new: float32 [8, 384], P('head', 'dp')
- bias_copy_new: bfloat16 [8, 384], P('head', 'dp')
- norm_momentum_new: float32 [6, 512], replicated
- norm_variance_new: float32 [6, 512], replicated
- norm_master_new: float32 [6, 512], replicated
- norm_clipped: float32 [6, 512], replicated
The draws below stay inside these ranges and needn't reach their ends.
Inputs may be any that keep to these rules, and one draw needn't show every extreme that they name: `segment_ids`: within each group the document numbers never fall; each document has 1 to 1024 tokens, and one has exactly 1024. `norm_params`: rows 0 and 3 are gains near 1; the other rows are biases near 0.
All inputs are finite; a program needn't handle non-finite values.
Results may differ from the reference program's by a relative error of at most 0.035.
The reference program's roundings to bfloat16 on the way count: a program that leaves them out, or rounds other values in their place, can miss the bound.
Values may be sent and summed in bfloat16 or wider, within the bound.
No kernel may reach another device: no remote copies, remote signals or barrier semaphores. Data moves between devices by JAX's collectives and lax.ppermute only.
A program may use at most 128 MiB of HBM per device.

```python
import math
import jax
import jax.numpy as jnp
import numpy as np
from jax import lax

D = 512
HEADS = 8
FF = 2048
HB = 384
TOK_DP = 2048
SEQ_MOST = 1024
SEGS = 8
QBLK = 512
GROUPS = 8
TOKENS = 16384


def draw_norm_params(key, part):
    noise = jnp.clip(jax.random.normal(key, (6, D), jnp.float32), -4.0, 4.0)
    row_index = jnp.arange(6)[:, None]
    is_gain = (row_index % 3 == 0).astype(jnp.float32)
    return is_gain * (1.0 + 0.15 * noise) + (1.0 - is_gain) * (0.3 * noise)


def shard_levels(rng, extent, cuts, smallest, largest):
    gain, own = 1.0, jax.random.fold_in(rng, 6)
    for axis_at, shards_of in cuts:
        draws = jnp.exp(jax.random.uniform(jax.random.fold_in(own, axis_at), (shards_of,), jnp.float32, smallest / len(cuts), largest / len(cuts)))
        gain = gain * jnp.repeat(draws, extent[axis_at] // shards_of).reshape([-1 if axis == axis_at else 1 for axis in range(len(extent))])
    return gain


def split_up(amount, total, most, skew):
    weights = [(1 << 20) // math.isqrt(rank ** skew) + 1 for rank in range(2, amount + 1)]
    surplus, counts = total - most - (amount - 1), [1] * (amount - 1)
    while surplus > 0:
        free = [i for i in range(amount - 1) if counts[i] < most]
        pool, left = sum([weights[i] for i in free]), surplus
        for i in free:
            more = min(most - counts[i], max(1, left * weights[i] // pool), surplus)
            counts[i] = counts[i] + more
            surplus = surplus - more
    return np.array([most] + counts)


def ragged(rng, count, total, limit, skew):
    if count == 2:
        one = jax.random.randint(rng, (), max(1, total - limit), min(limit, total - 1) + 1)
        return jnp.stack([one, total - one])
    sizes = jnp.asarray(split_up(count, total, limit, skew), jnp.int32)
    couples = (count - 1) // 2
    giver, taker = sizes[1:1 + 2 * couples:2], sizes[2:2 + 2 * couples:2]
    margin = jnp.minimum(giver - 1, limit - taker)
    moved = jax.random.randint(jax.random.fold_in(rng, 1), (couples,), 0, 1 << 20) % (margin + 1)
    sizes = sizes.at[1:1 + 2 * couples:2].set(giver - moved).at[2:2 + 2 * couples:2].set(taker + moved)
    return sizes[jax.random.permutation(jax.random.fold_in(rng, 2), count)]


def scatter_about(rng, extent, spread, most, cuts=(), held_as=jnp.bfloat16):
    values = spread * jax.random.normal(rng, extent, jnp.float32)
    if cuts:
        values = values * shard_levels(rng, extent, cuts, -0.22, 0.18)
    return jnp.clip(values, -most, most).astype(held_as)


def setup_inputs(seed: int = 0) -> dict:
    keys = jax.random.split(jax.random.key(seed), 25)
    return {
        "post_in": scatter_about(keys[0], (TOKENS, D), 1.0, 6.0, ((0, 32),), jnp.float32),
        "dual_in": scatter_about(keys[1], (TOKENS, D), 1.0, 6.0, ((0, 32),), jnp.float32),
        "segment_ids": jax.vmap(lambda own: jnp.searchsorted(jnp.cumsum(ragged(own, SEGS, TOK_DP, SEQ_MOST, 2)), jnp.arange(TOK_DP), side="right"))(jax.random.split(keys[2], GROUPS)).reshape((GROUPS, TOK_DP)).astype(jnp.int32),
        "post_cot": scatter_about(keys[3], (TOKENS, D), 1.0, 6.0, ((0, 32),), jnp.float32),
        "dual_cot": scatter_about(keys[4], (TOKENS, D), 1.0, 6.0, ((0, 32),), jnp.float32),
        "attend_weight": scatter_about(keys[5], (D, 3 * D), D ** -0.5, 0.25, ((0, 8), (1, 4)), jnp.float32),
        "output_weight": scatter_about(keys[6], (D, D), (D // 16) ** -0.5, 1.0, ((0, 4), (1, 8)), jnp.float32),
        "expand_weight": scatter_about(keys[7], (D, FF), D ** -0.5, 0.25, ((0, 8), (1, 4)), jnp.float32),
        "contract_weight": scatter_about(keys[8], (FF, D), FF ** -0.5, 0.125, ((0, 4), (1, 8)), jnp.float32),
        "head_bias": scatter_about(keys[9], (HEADS, HB), 0.3, 4.0, ((0, 4), (1, 8)), jnp.float32),
        "norm_params": draw_norm_params(jax.random.fold_in(keys[24], 71), 0),
        "attend_momentum": scatter_about(keys[11], (D, 3 * D), (1.5 * (4 * D * D + 2 * D * FF + 8 * D + FF) ** -0.5), 0.0048828125, ((0, 8), (1, 4)), jnp.float32),
        "output_momentum": scatter_about(keys[12], (D, D), (1.5 * (4 * D * D + 2 * D * FF + 8 * D + FF) ** -0.5), 0.0048828125, ((0, 4), (1, 8)), jnp.float32),
        "expand_momentum": scatter_about(keys[13], (D, FF), (1.5 * (4 * D * D + 2 * D * FF + 8 * D + FF) ** -0.5), 0.0048828125, ((0, 8), (1, 4)), jnp.float32),
        "contract_momentum": scatter_about(keys[14], (FF, D), (1.5 * (4 * D * D + 2 * D * FF + 8 * D + FF) ** -0.5), 0.0048828125, ((0, 4), (1, 8)), jnp.float32),
        "bias_momentum": scatter_about(keys[15], (HEADS, HB), (6.0 * (4 * D * D + 2 * D * FF + 8 * D + FF) ** -0.5), 0.01953125, ((0, 4), (1, 8)), jnp.float32),
        "norm_momentum": scatter_about(keys[16], (6, D), (1.5 * (4 * D * D + 2 * D * FF + 8 * D + FF) ** -0.5), 0.0048828125, (), jnp.float32),
        "attend_variance": jnp.clip(jnp.exp(math.log(2.8554459277074784e-06) - 1.3862944 * jax.random.uniform(keys[17], (D, 3 * D), jnp.float32) ** shard_levels(keys[17], (D, 3 * D), ((0, 8), (1, 4)), -0.2, 0.2)), 7.138614819268696e-07, 2.8554459277074784e-06),
        "output_variance": jnp.clip(jnp.exp(math.log(2.8554459277074784e-06) - 1.3862944 * jax.random.uniform(keys[18], (D, D), jnp.float32) ** shard_levels(keys[18], (D, D), ((0, 4), (1, 8)), -0.2, 0.2)), 7.138614819268696e-07, 2.8554459277074784e-06),
        "expand_variance": jnp.clip(jnp.exp(math.log(2.8554459277074784e-06) - 1.3862944 * jax.random.uniform(keys[19], (D, FF), jnp.float32) ** shard_levels(keys[19], (D, FF), ((0, 8), (1, 4)), -0.2, 0.2)), 7.138614819268696e-07, 2.8554459277074784e-06),
        "contract_variance": jnp.clip(jnp.exp(math.log(2.8554459277074784e-06) - 1.3862944 * jax.random.uniform(keys[20], (FF, D), jnp.float32) ** shard_levels(keys[20], (FF, D), ((0, 4), (1, 8)), -0.2, 0.2)), 7.138614819268696e-07, 2.8554459277074784e-06),
        "bias_variance": jnp.clip(jnp.exp(math.log(4.5687134843319654e-05) - 1.3862944 * jax.random.uniform(keys[21], (HEADS, HB), jnp.float32) ** shard_levels(keys[21], (HEADS, HB), ((0, 4), (1, 8)), -0.2, 0.2)), 1.1421783710829914e-05, 4.5687134843319654e-05),
        "norm_variance": jnp.clip(jnp.exp(jax.random.uniform(keys[22], (6, D), jnp.float32, math.log(3.172717697452754e-07), math.log(1.2690870789811015e-06))), 3.172717697452754e-07, 1.2690870789811015e-06),
        "clip_limit": jnp.clip(jax.random.uniform(keys[23], (1,), jnp.float32, 1.0, 2.0), 1.0, 2.0),
    }


EPS_NORM = 1e-05
NEG_LARGE = -1e+30
PRECISE = lax.Precision.HIGHEST
RATE_TABLE = (0.04, 0.12, 0.04, 0.04, 0.16, 0.3)
DECAY = 0.01
ADAM_EPS = 1e-08
BETA = 0.5
BIAS_CORRECTION = 0.875

@jax.custom_vjp
def low(v):
    return lax.optimization_barrier(v.astype(jnp.bfloat16)).astype(jnp.float32)

@jax.custom_vjp
def low_back(v):
    return v

def low_keep(v):
    return (low(v), None)

def low_pass(kept, grad):
    return (grad,)

def back_keep(v):
    return (v, None)

def back_low(kept, grad):
    return (low(grad),)
low.defvjp(low_keep, low_pass)
low_back.defvjp(back_keep, back_low)

def layer_norm(stream_rows, gain_row, shift_row):
    row_mean = lax.optimization_barrier(jnp.mean(stream_rows, axis=-1, keepdims=True))
    centered = stream_rows - row_mean
    row_var = lax.optimization_barrier(jnp.mean(centered * centered, axis=-1, keepdims=True))
    return centered * lax.rsqrt(row_var + EPS_NORM) * gain_row + shift_row

def group_layer(params, post_rows, dual_rows, segment):
    attend_w, output_w, expand_w, contract_w, bias_w, norm_w = params
    row_count = post_rows.shape[0]
    head_dim = D // HEADS
    copy_attend = low(attend_w)
    copy_output = low(output_w)
    copy_expand = low(expand_w)
    copy_contract = low(contract_w)
    copy_bias = low(bias_w)
    inputs = low(post_rows)
    qkv_rows = jnp.dot(inputs, copy_attend, precision=PRECISE).reshape(row_count, HEADS, 3, head_dim)
    queries = low_back(low(qkv_rows[:, :, 0] + copy_bias[:, :head_dim]))
    key_rows = low_back(low(qkv_rows[:, :, 1]))
    values = low_back(low(qkv_rows[:, :, 2] + copy_bias[:, head_dim:2 * head_dim]))
    score_scale = 1.0 / math.sqrt(head_dim)
    positions = jnp.arange(row_count, dtype=jnp.int32)

    def attend_block(offset):
        query_block = lax.dynamic_slice_in_dim(queries, offset, QBLK, 0)
        query_seg = lax.dynamic_slice_in_dim(segment, offset, QBLK, 0)
        query_pos = offset + jnp.arange(QBLK, dtype=jnp.int32)
        scores = low_back(jnp.einsum('qhe,khe->hqk', query_block, key_rows, precision=PRECISE) * score_scale)
        allowed = (query_seg[:, None] == segment[None, :]) & (positions[None, :] <= query_pos[:, None])
        scores = jnp.where(allowed[None], scores, NEG_LARGE)
        row_top = lax.optimization_barrier(jnp.max(scores, axis=-1, keepdims=True))
        exponent = jnp.exp(scores - row_top)
        attn_probs = low(exponent / lax.optimization_barrier(jnp.sum(exponent, axis=-1, keepdims=True)))
        return jnp.einsum('hqk,khe->qhe', attn_probs, values, precision=PRECISE)
    starts = jnp.arange(row_count // QBLK, dtype=jnp.int32) * QBLK
    attended = lax.map(jax.checkpoint(attend_block), starts)
    attn_mixed = low_back(low(attended.reshape(row_count, D)))
    attn_out = low_back(jnp.dot(attn_mixed, copy_output, precision=PRECISE)) + norm_w[2]
    post_norm = layer_norm(post_rows + attn_out, norm_w[0], norm_w[1])
    inner_bias = copy_bias[:, 2 * head_dim:].reshape(FF)
    hidden_pre = low_back(jnp.dot(low(post_norm), copy_expand, precision=PRECISE) + inner_bias)
    hidden = low(jnp.where(hidden_pre > 0, hidden_pre, 0.0))
    ffn_out = low_back(jnp.dot(hidden, copy_contract, precision=PRECISE)) + norm_w[5]
    post_out = layer_norm(post_norm + ffn_out, norm_w[3], norm_w[4])
    dual_out = dual_rows + attn_out + ffn_out
    return (post_out, dual_out)

def adam_update(master, momentum, variance, gradient, factor, correction, rate):
    clipped = factor * gradient
    momentum_new = BETA * momentum + (1.0 - BETA) * clipped
    variance_new = BETA * variance + (1.0 - BETA) * clipped * clipped
    master_new = master - rate * (momentum_new / correction / (jnp.sqrt(variance_new / correction) + ADAM_EPS) + DECAY * master)
    return (momentum_new, variance_new, master_new)

def reference(post_in, dual_in, segment_ids, post_cot, dual_cot, attend_weight, output_weight, expand_weight, contract_weight, head_bias, norm_params, attend_momentum, output_momentum, expand_momentum, contract_momentum, bias_momentum, norm_momentum, attend_variance, output_variance, expand_variance, contract_variance, bias_variance, norm_variance, clip_limit):
    params = (attend_weight, output_weight, expand_weight, contract_weight, head_bias, norm_params)

    def grouped(array_rows):
        return array_rows.reshape(GROUPS, TOK_DP, D)

    def group_step(running, group_batch):
        post_rows, dual_rows, segment, cot_post, cot_dual = group_batch

        def layer_fn(param_set, rows_in):
            return group_layer(param_set, rows_in, dual_rows, segment)
        outputs, pullback = jax.vjp(layer_fn, params, post_rows)
        param_grads, row_grads = pullback((cot_post, cot_dual))
        running = jax.tree.map(lambda accum, addend: accum + addend, running, param_grads)
        return (running, (outputs[0], outputs[1], row_grads))
    zero_grads = jax.tree.map(jnp.zeros_like, params)
    grad_sums, (post_out, dual_out, post_grad) = lax.scan(group_step, zero_grads, (grouped(post_in), grouped(dual_in), segment_ids, grouped(post_cot), grouped(dual_cot)))
    post_out = post_out.reshape(TOKENS, D)
    dual_out = dual_out.reshape(TOKENS, D)
    post_grad = post_grad.reshape(TOKENS, D)
    squares = jnp.sum(grad_sums[0] * grad_sums[0]) + jnp.sum(grad_sums[1] * grad_sums[1]) + jnp.sum(grad_sums[2] * grad_sums[2]) + jnp.sum(grad_sums[3] * grad_sums[3]) + jnp.sum(grad_sums[4] * grad_sums[4]) + jnp.sum(grad_sums[5] * grad_sums[5])
    total_norm = jnp.sqrt(squares)
    factor = clip_limit[0] / jnp.maximum(total_norm, clip_limit[0])
    correction = BIAS_CORRECTION
    moments = (attend_momentum, output_momentum, expand_momentum, contract_momentum, bias_momentum, norm_momentum)
    variances = (attend_variance, output_variance, expand_variance, contract_variance, bias_variance, norm_variance)
    results = []
    for index in range(6):
        momentum_new, variance_new, master_new = adam_update(params[index], moments[index], variances[index], grad_sums[index], factor, correction, RATE_TABLE[index])
        results.append(momentum_new)
        results.append(variance_new)
        results.append(master_new)
        if index < 5:
            results.append(master_new.astype(jnp.bfloat16))
    norm_clipped = factor * grad_sums[5]
    return (post_out, dual_out, post_grad, total_norm.reshape(1), results[0], results[1], results[2], results[3], results[4], results[5], results[6], results[7], results[8], results[9], results[10], results[11], results[12], results[13], results[14], results[15], results[16], results[17], results[18], results[19], results[20], results[21], results[22], norm_clipped)
```

```python
import functools

import jax
import jax.numpy as jnp
from jax import lax
from jax.experimental import pallas as pl
from jax.experimental.pallas import tpu as pltpu
from jax.sharding import PartitionSpec as P

D = 512
HEADS = 8
HD = 64
TQ = 256
TK = 256
SEQ_MOST = 1024
KEY_BLOCKS = SEQ_MOST // TK + 1
CH = 64

EPS_NORM = 1e-05
NEG_LARGE = -1e30
LOG2E = 1.4426950408889634
SCORE_SCALE = HD ** (-0.5)
RATE_ATTEND = 0.04
RATE_OUTPUT = 0.12
RATE_EXPAND = 0.04
RATE_CONTRACT = 0.04
RATE_BIAS = 0.16
RATE_NORM = 0.3
DECAY = 0.01
ADAM_EPS = 1e-08
BETA = 0.5
BIAS_CORRECTION = 0.875
BF = jnp.bfloat16
F32 = jnp.float32
VMEM = pl.BlockSpec(memory_space=pltpu.VMEM)
SMEM = pl.BlockSpec(memory_space=pltpu.SMEM)


def dot(a, b, ca, cb):
    return lax.dot_general(a, b, (((ca,), (cb,)), ((), ())), preferred_element_type=F32)


def bits_of(count):
    bits = []
    while count > 1:
        count //= 2
        bits.append(count)
    return bits


def swap(v, step):
    axis, bit = step
    count = lax.axis_size(axis)
    return lax.ppermute(v, axis, [(i, i ^ bit) for i in range(count)])


def offsets(steps, axis):
    offs = [0]
    for name, bit in steps:
        offs = offs + [o ^ (bit if name == axis else 0) for o in offs]
    return offs


def gather_steps(v, steps):
    acc = v[None]
    for step in steps:
        acc = jnp.concatenate([acc, swap(acc, step)], axis=0)
    return acc


def place(steps, axis, off):
    pos = 0
    for k, (name, bit) in enumerate(steps):
        if name == axis:
            pos = pos + ((off // bit) % 2) * (1 << k)
    return pos


def scatter_steps(keep, send, steps):
    for step in reversed(steps):
        got = swap(send, step)
        half = keep.shape[0] // 2
        if half == 0:
            return keep, got
        total = keep.astype(F32) + got.astype(F32)
        send = total[half:].astype(BF)
        keep = total[:half].astype(BF)
    return keep, send


def lane_mask_stack(v, lh):
    if lh == 1:
        return v
    lane = lax.broadcasted_iota(jnp.int32, v.shape, 1)
    zero = jnp.zeros_like(v)
    return jnp.concatenate(
        [jnp.where((lane >= l * HD) & (lane < (l + 1) * HD), v, zero) for l in range(lh)], axis=0
    )


def head_rows_merge(vt, lh):
    return jnp.concatenate(
        [vt[l * HD : (l + 1) * HD, l * TQ : (l + 1) * TQ] for l in range(lh)], axis=0
    )


def attend_kernel(lh, n_dp, n_h, dp_offs, idx_ref, lo_ref, start_ref, w_ref, *refs):
    rows = refs[:n_h]
    pieces = refs[n_h : 2 * n_h]
    q_ref, k_ref, v_ref, o_ref, lse_ref, wg_ref, w_s, b_s, vt_s, s_s, acc_s = refs[2 * n_h :]
    g, h = idx_ref[0], idx_ref[1]
    width = lh * HD
    ds_rows = D // n_dp
    rw = rows[0].shape[0]
    shares = b_s.shape[1] // lh
    for p in range(n_dp):
        block = g ^ dp_offs[p]
        w_s[pl.ds(pl.multiple_of(block * ds_rows, ds_rows), ds_rows), :] = w_ref[p, :ds_rows, :]
        b_s[pl.ds(block, 1), :] = w_ref[p, ds_rows : ds_rows + 16, : lh * shares][:1].astype(F32)
    wide = w_s[...].astype(F32)
    wg = jnp.concatenate(
        [
            wide[:, l * 3 * HD + kind * HD : l * 3 * HD + (kind + 1) * HD]
            for kind in range(3)
            for l in range(lh)
        ],
        axis=1,
    ).astype(BF)
    wg_ref[...] = wg
    per_head = [
        jnp.concatenate([b_s[b : b + 1, l * shares : (l + 1) * shares] for b in range(n_dp)], axis=1)
        for l in range(lh)
    ]
    q_bias = jnp.concatenate([r[:, :HD] for r in per_head], axis=1)
    v_bias = jnp.concatenate([r[:, HD : 2 * HD] for r in per_head], axis=1)
    inner = jnp.concatenate([r[:, 2 * HD :] for r in per_head], axis=1)
    inner_rows = jnp.concatenate(
        [inner[:, i * width : (i + 1) * width] for i in range(inner.shape[1] // width)]
        + [jnp.zeros((16 - inner.shape[1] // width, width), F32)],
        axis=0,
    ).astype(BF)
    for off in range(n_h):
        base = pl.multiple_of((h ^ off) * rw, rw)
        qkv = dot(rows[off][...], wg_ref[...], 1, 0)
        q_ref[pl.ds(base, rw), :] = (qkv[:, :width] + q_bias).astype(BF)
        k_ref[pl.ds(base, rw), :] = qkv[:, width : 2 * width].astype(BF)
        v_ref[pl.ds(base, rw), :] = (qkv[:, 2 * width :] + v_bias).astype(BF)
        pieces[off][pl.ds(rw, 16), :] = inner_rows
    n_rows = q_ref.shape[0]
    vt_s[:width, :] = v_ref[...].T
    vt_s[width:, :] = jnp.ones((16, n_rows), BF)
    factor = SCORE_SCALE * LOG2E
    cols = lh * TQ

    def query_block(qb, carry):
        r0 = pl.multiple_of(qb * TQ, TQ)
        q2 = lane_mask_stack(q_ref[pl.ds(r0, TQ), :], lh)
        start = jnp.concatenate([start_ref[:, pl.ds(r0, TQ)]] * lh, axis=1)
        lo = lo_ref[qb]
        column = lax.broadcasted_iota(jnp.int32, (1, cols), 1) % TQ

        def scores(kb, top):
            c0 = pl.multiple_of(kb * TK, TK)
            s = dot(k_ref[pl.ds(c0, TK), :], q2, 1, 1)
            key = lax.broadcasted_iota(jnp.int32, (TK, cols), 0)
            ok = (key >= start - c0) & (key <= column + (r0 - c0))
            s = jnp.where(ok, s, NEG_LARGE)
            s_s[kb - lo] = s
            return jnp.maximum(top, jnp.max(s.reshape(TK // 8, 8, cols), axis=0))

        top = lax.fori_loop(lo, qb + 1, scores, jnp.full((8, cols), NEG_LARGE, F32))
        top = jnp.max(top, axis=0, keepdims=True)
        acc_s[...] = jnp.zeros_like(acc_s)

        def mix(kb, carry):
            c0 = pl.multiple_of(kb * TK, TK)
            p = jnp.exp2((s_s[kb - lo] - top) * factor).astype(BF)
            acc_s[...] += dot(vt_s[:, pl.ds(c0, TK)], p, 1, 0)
            return carry

        lax.fori_loop(lo, qb + 1, mix, 0)
        total = acc_s[width : width + 1, :]
        out_t = head_rows_merge(acc_s[:width, :] / total, lh)
        o_ref[pl.ds(r0, TQ), :] = out_t.T.astype(BF)
        lse_ref[qb] = jnp.broadcast_to(top * factor + jnp.log2(total), (8, cols))
        return carry

    lax.fori_loop(0, n_rows // TQ, query_block, 0)
    for off in range(n_h):
        base = pl.multiple_of((h ^ off) * rw, rw)
        pieces[off][:rw, :] = o_ref[pl.ds(base, rw), :]


def norm_back(grad, xhat, rstd, gain):
    g = grad * gain
    return rstd * (
        g - jnp.mean(g, axis=-1, keepdims=True) - xhat * jnp.mean(g * xhat, axis=-1, keepdims=True)
    )


def fold(v):
    return jnp.sum(v.reshape(v.shape[0] // 8, 8, v.shape[1]), axis=0)


def middle_kernel(lh, n_dp, n_h, e_steps, c_steps, idx_ref, norm_ref, *refs):
    width = lh * HD
    mixed = refs[:n_h]
    e_ref, c_ref, post_in, dual_in, post_cot, dual_cot = refs[n_h : n_h + 6]
    outs = refs[n_h + 6 :]
    post_out, dual_out, gmid1_ref = outs[:3]
    gm = outs[3 : 3 + n_h]
    ge_keep, ge_send, gc_keep, gc_send, small_ref = outs[3 + n_h : 8 + n_h]
    (e_s, c_s, o_s, mix_s, bias_s, hid_s, acc_s, xh_s, rs_s, pn_s, xb_s, xt_s, gb_s, gmid2_s, ffb_s) = outs[
        8 + n_h :
    ]
    g, h = idx_ref[0], idx_ref[1]
    rw = post_in.shape[0]
    ds_rows = D // n_dp
    units = hid_s.shape[2]
    row = lambda i: norm_ref[i : i + 1, :]

    e_dp, e_h = offsets(e_steps, "dp"), offsets(e_steps, "head")
    c_dp, c_h = offsets(c_steps, "dp"), offsets(c_steps, "head")
    for p in range(n_dp * n_h):
        at = pl.ds(pl.multiple_of((g ^ e_dp[p]) * ds_rows, ds_rows), ds_rows)
        e_s[e_h[p], at, :] = e_ref[p]
        at = pl.ds(pl.multiple_of((g ^ c_dp[p]) * ds_rows, ds_rows), ds_rows)
        c_s[c_h[p], at, :] = c_ref[p, :, :units]
        o_s[at, c_h[p] * width : (c_h[p] + 1) * width] = c_ref[p, :, units:]
    for off in range(n_h):
        mix_s[:, off * width : (off + 1) * width] = mixed[off][:rw, :]
        tail = mixed[off][rw : rw + 16, :].astype(F32)
        bias_s[off] = jnp.concatenate([tail[i : i + 1, :] for i in range(units // width)], axis=1)

    acc_s[...] = dot(mix_s[...], o_s[...], 1, 1)

    def chunk_one(i, carry):
        at = pl.ds(pl.multiple_of(i * CH, CH), CH)
        attn_out = acc_s[at, :] + row(2)
        v = post_in[at, :] + attn_out
        centered = v - jnp.mean(v, axis=-1, keepdims=True)
        rstd = lax.rsqrt(jnp.mean(centered * centered, axis=-1, keepdims=True) + EPS_NORM)
        xhat = centered * rstd
        pn = xhat * row(0) + row(1)
        xh_s[at, :] = xhat
        rs_s[at, :] = jnp.broadcast_to(rstd, (CH, 128))
        pn_s[at, :] = pn
        xb_s[at, :] = pn.astype(BF)
        dual_out[at, :] = dual_in[at, :] + attn_out
        return carry

    lax.fori_loop(0, rw // CH, chunk_one, 0)
    xt_s[...] = xb_s[...].T
    acc_s[...] = jnp.zeros_like(acc_s)

    def inner(oh, carry):
        pre = dot(xb_s[...], e_s[oh], 1, 0) + bias_s[oh]
        hid = jnp.maximum(pre, 0.0).astype(BF)
        hid_s[oh] = hid
        acc_s[...] += dot(hid, c_s[oh], 1, 1)
        return carry

    lax.fori_loop(0, n_h, inner, 0)

    def chunk_two(i, carry):
        gain_sum, shift_sum, ffn_sum = carry
        at = pl.ds(pl.multiple_of(i * CH, CH), CH)
        ffn_out = acc_s[at, :] + row(5)
        v = pn_s[at, :] + ffn_out
        centered = v - jnp.mean(v, axis=-1, keepdims=True)
        rstd = lax.rsqrt(jnp.mean(centered * centered, axis=-1, keepdims=True) + EPS_NORM)
        xhat = centered * rstd
        post_out[at, :] = xhat * row(3) + row(4)
        dual_out[at, :] = dual_out[at, :] + ffn_out
        cot = post_cot[at, :]
        gmid2 = norm_back(cot, xhat, rstd, row(3))
        gffn = gmid2 + dual_cot[at, :]
        gmid2_s[at, :] = gmid2
        gb_s[at, :] = gffn.astype(BF)
        return gain_sum + fold(cot * xhat), shift_sum + fold(cot), ffn_sum + fold(gffn)

    zero = jnp.zeros((8, D), F32)
    gain2, shift2, ffn_sum = lax.fori_loop(0, rw // CH, chunk_two, (zero, zero, zero))
    acc_s[...] = jnp.zeros_like(acc_s)
    gt = gb_s[...].T
    hid_t = gt

    def inner_back(pair, carry):
        for low in range(2):
            oh = pair * 2 + low
            ge, gc = (ge_keep, gc_keep) if low == 0 else (ge_send, gc_send)
            hid = hid_s[oh]
            gh = dot(gb_s[...], c_s[oh], 1, 0)
            gp = jnp.where(hid > 0, gh, 0.0).astype(BF)
            ffb_s[oh] = jnp.sum(gp.astype(F32), axis=0, keepdims=True)
            acc_s[...] += dot(gp, e_s[oh], 1, 1)
            grad_c = dot(hid_t, hid, 1, 0).astype(BF)
            grad_e = dot(xt_s[...], gp, 1, 0).astype(BF)
            for b in range(n_dp):
                ge[place(e_steps, "dp", b ^ g) + place(e_steps, "head", oh - low)] = grad_e[
                    b * ds_rows : (b + 1) * ds_rows
                ]
                gc[place(c_steps, "dp", b ^ g) + place(c_steps, "head", oh - low), :, :units] = grad_c[
                    b * ds_rows : (b + 1) * ds_rows
                ]
        return carry

    lax.fori_loop(0, n_h // 2, inner_back, 0)

    def chunk_three(i, carry):
        gain_sum, shift_sum, attn_sum = carry
        at = pl.ds(pl.multiple_of(i * CH, CH), CH)
        grad = gmid2_s[at, :] + acc_s[at, :]
        xhat = xh_s[at, :]
        gmid1 = norm_back(grad, xhat, rs_s[at, :1], row(0))
        gmid1_ref[at, :] = gmid1
        gattn = gmid1 + dual_cot[at, :]
        gb_s[at, :] = gattn.astype(BF)
        return gain_sum + fold(grad * xhat), shift_sum + fold(grad), attn_sum + fold(gattn)

    gain1, shift1, attn_sum = lax.fori_loop(0, rw // CH, chunk_three, (zero, zero, zero))
    grad_mixed = dot(gb_s[...], o_s[...], 1, 0).astype(BF)
    for off in range(n_h):
        gm[off][...] = grad_mixed[:, off * width : (off + 1) * width]
    grad_o = dot(gb_s[...].T, mix_s[...], 1, 0).astype(BF)
    for oh in range(n_h):
        gc = gc_keep if oh % 2 == 0 else gc_send
        for b in range(n_dp):
            gc[place(c_steps, "dp", b ^ g) + place(c_steps, "head", oh - oh % 2), :, units:] = grad_o[
                b * ds_rows : (b + 1) * ds_rows, oh * width : (oh + 1) * width
            ]
    for i, part in enumerate((gain1, shift1, attn_sum, gain2, shift2, ffn_sum)):
        line = jnp.sum(part, axis=0, keepdims=True)
        for j in range(D // 128):
            small_ref[4 * i + j : 4 * i + j + 1, :] = line[:, j * 128 : (j + 1) * 128]
    for oh in range(n_h):
        first = 24 + (h ^ oh) * (units // 128)
        for j in range(units // 128):
            small_ref[pl.ds(first + j, 1), :] = ffb_s[oh, :, j * 128 : (j + 1) * 128]


def attend_back_kernel(lh, n_h, idx_ref, lo_ref, start_ref, q_ref, k_ref, v_ref, o_ref, lse_ref, small_in, *refs):
    gm = refs[:n_h]
    gqkv_ref, small_ref, do_s, kt_s, dk_s, dv_s, dq_s = refs[n_h:]
    h = idx_ref[1]
    width = lh * HD
    rw = gm[0].shape[0]
    n_rows = q_ref.shape[0]
    cols = lh * TQ
    factor = SCORE_SCALE * LOG2E
    for off in range(n_h):
        do_s[pl.ds(pl.multiple_of((h ^ off) * rw, rw), rw), :] = gm[off][...]
    kt_s[...] = k_ref[...].T
    dk_s[...] = jnp.zeros_like(dk_s)
    dv_s[...] = jnp.zeros_like(dv_s)

    def query_block(qb, q_sum):
        r0 = pl.multiple_of(qb * TQ, TQ)
        at = pl.ds(r0, TQ)
        q2 = lane_mask_stack(q_ref[at, :], lh)
        do = do_s[at, :]
        do2 = lane_mask_stack(do, lh)
        prod = (do.astype(F32) * o_ref[at, :].astype(F32)).T
        delta = jnp.concatenate(
            [jnp.sum(prod[l * HD : (l + 1) * HD, :], axis=0, keepdims=True) for l in range(lh)], axis=1
        )
        lse = lse_ref[qb][:1]
        start = jnp.concatenate([start_ref[:, at]] * lh, axis=1)
        lo = lo_ref[qb]
        column = lax.broadcasted_iota(jnp.int32, (1, cols), 1) % TQ
        dq_s[...] = jnp.zeros_like(dq_s)

        def pair(kb, carry):
            c0 = pl.multiple_of(kb * TK, TK)
            keys = pl.ds(c0, TK)
            s = dot(k_ref[keys, :], q2, 1, 1)
            key = lax.broadcasted_iota(jnp.int32, (TK, cols), 0)
            ok = (key >= start - c0) & (key <= column + (r0 - c0))
            p = jnp.exp2(jnp.where(ok, s, NEG_LARGE) * factor - lse)
            dp = dot(v_ref[keys, :], do2, 1, 1)
            grad = (p * (dp - delta)).astype(BF)
            dv_s[keys, :] += dot(p.astype(BF), do2, 1, 0)
            dk_s[keys, :] += dot(grad, q2, 1, 0)
            dq_s[...] += dot(kt_s[:, keys], grad, 1, 0)
            return carry

        lax.fori_loop(lo, qb + 1, pair, 0)
        dq = (head_rows_merge(dq_s[...], lh) * SCORE_SCALE).T.astype(BF)
        gqkv_ref[at, :width] = dq
        return q_sum + jnp.sum(dq.astype(F32), axis=0, keepdims=True)

    q_sum = lax.fori_loop(0, n_rows // TQ, query_block, jnp.zeros((1, width), F32))
    gqkv_ref[:, width : 2 * width] = (dk_s[...] * SCORE_SCALE).astype(BF)
    dv = dv_s[...].astype(BF)
    gqkv_ref[:, 2 * width :] = dv
    v_sum = jnp.sum(dv.astype(F32), axis=0, keepdims=True)
    small_ref[:40, :] = small_in[...]
    small_ref[40:, :] = jnp.zeros((8, 128), F32)
    for l in range(lh):
        small_ref[pl.ds(40 + h * lh + l, 1), :] = jnp.concatenate(
            [q_sum[:, l * HD : (l + 1) * HD], v_sum[:, l * HD : (l + 1) * HD]], axis=1
        )


def rows_back_kernel(n_h, idx_ref, gqkv_ref, wg_ref, *outs):
    h = idx_ref[1]
    rw = outs[0].shape[0]
    for off in range(n_h):
        at = pl.ds(pl.multiple_of((h ^ off) * rw, rw), rw)
        outs[off][...] = dot(gqkv_ref[at, :], wg_ref[...], 1, 1).astype(BF)


def attend_grad_kernel(lh, n_dp, n_h, steps, idx_ref, gqkv_ref, *refs):
    rows = refs[:n_h]
    out_ref, acc_s = refs[n_h:]
    g, h = idx_ref[0], idx_ref[1]
    rw = rows[0].shape[0]
    ds_rows = D // n_dp
    width = lh * HD
    for off in range(n_h):
        at = pl.ds(pl.multiple_of((h ^ off) * rw, rw), rw)
        part = dot(rows[off][...], gqkv_ref[at, :], 0, 0)
        acc_s[...] = part if off == 0 else acc_s[...] + part
    full = acc_s[...]
    full = jnp.concatenate(
        [full[:, kind * width + l * HD : kind * width + (l + 1) * HD] for l in range(lh) for kind in range(3)],
        axis=1,
    ).astype(BF)
    for b in range(n_dp):
        out_ref[place(steps, "dp", b ^ g)] = full[b * ds_rows : (b + 1) * ds_rows]


def call(body, outs, scratch, n_smem, args, limit, flops, nbytes):
    return pl.pallas_call(
        body,
        out_shape=outs,
        in_specs=[SMEM] * n_smem + [VMEM] * (len(args) - n_smem),
        out_specs=jax.tree.map(lambda _: VMEM, outs),
        scratch_shapes=scratch,
        compiler_params=pltpu.CompilerParams(vmem_limit_bytes=limit << 20),
        cost_estimate=pl.CostEstimate(flops=int(flops), bytes_accessed=int(nbytes), transcendentals=0),
    )(*args)


def sds(shape, dtype):
    return jax.ShapeDtypeStruct(shape, dtype)


def adam_update(master, momentum, variance, gradient, factor, rate):
    clipped = factor * gradient
    momentum_new = BETA * momentum + (1.0 - BETA) * clipped
    variance_new = BETA * variance + (1.0 - BETA) * clipped * clipped
    master_new = master - rate * (
        momentum_new / BIAS_CORRECTION / (jnp.sqrt(variance_new / BIAS_CORRECTION) + ADAM_EPS)
        + DECAY * master
    )
    return (momentum_new, variance_new, master_new)


def per_device(
    post_in,
    dual_in,
    segment_ids,
    post_cot,
    dual_cot,
    attend_weight,
    output_weight,
    expand_weight,
    contract_weight,
    head_bias,
    norm_params,
    attend_momentum,
    output_momentum,
    expand_momentum,
    contract_momentum,
    bias_momentum,
    norm_momentum,
    attend_variance,
    output_variance,
    expand_variance,
    contract_variance,
    bias_variance,
    norm_variance,
    clip_limit,
):
    n_dp, n_h = lax.axis_size("dp"), lax.axis_size("head")
    g, h = lax.axis_index("dp"), lax.axis_index("head")
    idx = jnp.stack([g, h]).astype(jnp.int32)
    rw = post_in.shape[0]
    n_rows = rw * n_h
    lh = HEADS // n_h
    width = lh * HD
    ds_rows = attend_weight.shape[0]
    a_cols = attend_weight.shape[1]
    units = expand_weight.shape[1]
    shares = head_bias.shape[1]
    dp_bits, h_bits = bits_of(n_dp), bits_of(n_h)
    a_steps = [("dp", b) for b in dp_bits]
    e_steps = [("dp", b) for b in dp_bits] + [("head", b) for b in h_bits]
    c_steps = (
        [("dp", b) for b in dp_bits[:-1]]
        + [("head", b) for b in h_bits[:-1]]
        + [("dp", dp_bits[-1])]
        + [("head", h_bits[-1])]
    )

    rows_own = post_in.astype(BF)
    bias_block = jnp.pad(
        head_bias.astype(BF).reshape(1, lh * shares), ((0, 15), (0, a_cols - lh * shares))
    )
    a_msg = jnp.concatenate([attend_weight.astype(BF), bias_block], axis=0)
    e_msg = expand_weight.astype(BF)
    c_msg = jnp.concatenate([contract_weight.T.astype(BF), output_weight.T.astype(BF)], axis=1)

    rows = {0: rows_own}
    for bit in h_bits:
        for off in list(rows):
            rows[off ^ bit] = swap(rows[off], ("head", bit))
    rows = [rows[off] for off in range(n_h)]
    a_all = gather_steps(a_msg, a_steps)
    e_all = gather_steps(e_msg, e_steps)
    c_all = gather_steps(c_msg, c_steps)

    segment = segment_ids[0]
    start = jnp.zeros_like(segment)
    for s in range(HEADS):
        start = start + jnp.where(segment > s, jnp.sum((segment == s).astype(jnp.int32)), 0)
    lo = start[::TQ] // TK
    start = start[None]

    n_q = n_rows // TQ
    cols = lh * TQ
    attend_out = call(
        functools.partial(attend_kernel, lh, n_dp, n_h, offsets(a_steps, "dp")),
        [sds((rw + 16, width), BF)] * n_h
        + [sds((n_rows, width), BF)] * 4
        + [sds((n_q, 8, cols), F32), sds((D, 3 * width), BF)],
        [
            pltpu.VMEM((D, a_cols), BF),
            pltpu.VMEM((n_dp, lh * shares), F32),
            pltpu.VMEM((width + 16, n_rows), BF),
            pltpu.VMEM((KEY_BLOCKS, TK, cols), F32),
            pltpu.VMEM((width + 16, cols), F32),
        ],
        2,
        [idx, lo, start, a_all] + rows,
        32,
        3e9,
        6e6,
    )
    pieces = attend_out[:n_h]
    q, k, v, o, lse, wg = attend_out[n_h:]
    mixed = [pieces[0]] + [
        lax.ppermute(pieces[off], "head", [(i, i ^ off) for i in range(n_h)]) for off in range(1, n_h)
    ]

    half = n_dp * n_h // 2
    middle_out = call(
        functools.partial(middle_kernel, lh, n_dp, n_h, e_steps, c_steps),
        [sds((rw, D), F32)] * 3
        + [sds((rw, width), BF)] * n_h
        + [sds((half, ds_rows, units), BF)] * 2
        + [sds((half, ds_rows, units + width), BF)] * 2
        + [sds((40, 128), F32)],
        [
            pltpu.VMEM((n_h, D, units), BF),
            pltpu.VMEM((n_h, D, units), BF),
            pltpu.VMEM((D, n_h * width), BF),
            pltpu.VMEM((rw, n_h * width), BF),
            pltpu.VMEM((n_h, 1, units), F32),
            pltpu.VMEM((n_h, rw, units), BF),
            pltpu.VMEM((rw, D), F32),
            pltpu.VMEM((rw, D), F32),
            pltpu.VMEM((rw, 128), F32),
            pltpu.VMEM((rw, D), F32),
            pltpu.VMEM((rw, D), BF),
            pltpu.VMEM((D, rw), BF),
            pltpu.VMEM((rw, D), BF),
            pltpu.VMEM((rw, D), F32),
            pltpu.VMEM((n_h, 1, units), F32),
        ],
        1,
        [idx, norm_params] + mixed + [e_all, c_all, post_in, dual_in, post_cot, dual_cot],
        52,
        8e9,
        16e6,
    )
    post_out, dual_out, grad_mid1 = middle_out[:3]
    gm = middle_out[3 : 3 + n_h]
    ge_keep, ge_send, gc_keep, gc_send, small_mid = middle_out[3 + n_h :]
    gm = [gm[0]] + [
        lax.ppermute(gm[off], "head", [(i, i ^ off) for i in range(n_h)]) for off in range(1, n_h)
    ]
    ge = scatter_steps(ge_keep, ge_send, e_steps)
    gc = scatter_steps(gc_keep, gc_send, c_steps)

    gqkv, small = call(
        functools.partial(attend_back_kernel, lh, n_h),
        [sds((n_rows, 3 * width), BF), sds((48, 128), F32)],
        [
            pltpu.VMEM((n_rows, width), BF),
            pltpu.VMEM((width, n_rows), BF),
            pltpu.VMEM((n_rows, width), F32),
            pltpu.VMEM((n_rows, width), F32),
            pltpu.VMEM((width, cols), F32),
        ],
        2,
        [idx, lo, start, q, k, v, o, lse, small_mid] + gm,
        32,
        4e9,
        6e6,
    )
    back = call(
        functools.partial(rows_back_kernel, n_h),
        [sds((rw, D), BF)] * n_h,
        [],
        1,
        [idx, gqkv, wg],
        24,
        8e8,
        4e6,
    )
    ga = call(
        functools.partial(attend_grad_kernel, lh, n_dp, n_h, a_steps),
        sds((n_dp, ds_rows, a_cols), BF),
        [pltpu.VMEM((D, 3 * width), F32)],
        1,
        [idx, gqkv] + rows,
        24,
        8e8,
        4e6,
    )
    ga = scatter_steps(ga[: n_dp // 2], ga[n_dp // 2 :], a_steps)
    back = {off: [back[off]] for off in range(n_h)}
    for bit in reversed(h_bits):
        sent = [off for off in back if off & bit]
        for off in sent:
            parts = back.pop(off)
            total = functools.reduce(lambda a, b: a + b, [p.astype(F32) for p in parts]).astype(BF)
            back[off ^ bit].append(swap(total, ("head", bit)))
    post_grad = functools.reduce(lambda a, b: a + b, [p.astype(F32) for p in back[0]], grad_mid1)

    for step in [("head", b) for b in reversed(h_bits)] + [("dp", b) for b in reversed(dp_bits)]:
        small = small + swap(small, step)

    join = lambda pair: (pair[0][0].astype(F32) + pair[1][0].astype(F32))
    share_attend = join(ga)
    share_expand = join(ge)
    share_co = join(gc)
    share_contract = share_co[:, :units].T
    share_output = share_co[:, units:].T
    norm_grads = small[:24].reshape(6, D)
    bias_full = jnp.concatenate(
        [
            lax.dynamic_slice_in_dim(small, 40 + h * lh, lh, 0),
            lax.dynamic_slice_in_dim(small, 24 + h * 2 * lh, 2 * lh, 0).reshape(lh, 256),
        ],
        axis=1,
    )
    share_bias = lax.dynamic_slice_in_dim(bias_full, g * shares, shares, 1)
    squares = jnp.sum(share_attend * share_attend) + jnp.sum(share_expand * share_expand) + jnp.sum(share_co * share_co)
    squares = jnp.full((8, 128), squares)
    for step in [("head", b) for b in reversed(h_bits)] + [("dp", b) for b in reversed(dp_bits)]:
        squares = squares + swap(squares, step)
    total_norm = jnp.sqrt(squares[0, 0] + jnp.sum(small * small))
    factor = clip_limit[0] / jnp.maximum(total_norm, clip_limit[0])
    results = []
    for w, m, va, gr, rate, low in (
        (attend_weight, attend_momentum, attend_variance, share_attend, RATE_ATTEND, True),
        (output_weight, output_momentum, output_variance, share_output, RATE_OUTPUT, True),
        (expand_weight, expand_momentum, expand_variance, share_expand, RATE_EXPAND, True),
        (contract_weight, contract_momentum, contract_variance, share_contract, RATE_CONTRACT, True),
        (head_bias, bias_momentum, bias_variance, share_bias, RATE_BIAS, True),
        (norm_params, norm_momentum, norm_variance, norm_grads, RATE_NORM, False),
    ):
        m_new, v_new, w_new = adam_update(w, m, va, gr, factor, rate)
        results += [m_new, v_new, w_new]
        if low:
            results.append(w_new.astype(BF))
    return (post_out, dual_out, post_grad, total_norm.reshape(1), *results, factor * norm_grads)


def solution(mesh):
    rows = P(("dp", "head"), None)
    tall, flat, rep = P("dp", "head"), P("head", "dp"), P()
    weights = (tall, flat, tall, flat, flat, rep)
    in_specs = (rows, rows, P("dp", None), rows, rows) + weights * 3 + (rep,)
    out_specs = (rows, rows, rows, rep)
    for spec in (tall, flat, tall, flat, flat):
        out_specs += (spec,) * 4
    out_specs += (rep,) * 4
    return jax.shard_map(per_device, mesh=mesh, in_specs=in_specs, out_specs=out_specs, check_vma=False)
```

```python
import functools

import jax
import jax.numpy as jnp
from jax import lax
from jax.experimental import pallas as pl
from jax.experimental.pallas import tpu as pltpu
from jax.sharding import PartitionSpec as P

D = 512
HEADS = 8
HD = 64
TQ = 256
TK = 256
SEQ_MOST = 1024
KEY_BLOCKS = SEQ_MOST // TK + 1
CH = 64

EPS_NORM = 1e-05
NEG_LARGE = -1e30
LOG2E = 1.4426950408889634
SCORE_SCALE = HD ** (-0.5)
RATES = (0.04, 0.12, 0.04, 0.04, 0.16, 0.3)
DECAY = 0.01
ADAM_EPS = 1e-08
BETA = 0.5
BIAS_CORRECTION = 0.875
BF = jnp.bfloat16
FLOPS_PER_US = 10**9
F32 = jnp.float32
VMEM = pl.BlockSpec(memory_space=pltpu.VMEM)
SMEM = pl.BlockSpec(memory_space=pltpu.SMEM)


def dot(a, b, ca, cb):
    return lax.dot_general(a, b, (((ca,), (cb,)), ((), ())), preferred_element_type=F32)


def bits_of(count):
    bits = []
    while count > 1:
        count //= 2
        bits.append(count)
    return bits


def swap(v, step):
    axis, bit = step
    count = lax.axis_size(axis)
    return lax.ppermute(v, axis, [(i, i ^ bit) for i in range(count)])


def offsets(steps, axis):
    offs = [0]
    for name, bit in steps:
        offs = offs + [o ^ (bit if name == axis else 0) for o in offs]
    return offs


def after(v, *ready):
    return lax.optimization_barrier((v, *ready))[0]


def place(steps, axis, off):
    pos = 0
    for k, (name, bit) in enumerate(steps):
        if name == axis:
            pos = pos + ((off // bit) % 2) * (1 << k)
    return pos


class Scatter:
    def __init__(self, keep, send, steps):
        self.keep, self.steps = keep, list(steps)
        self.got = swap(send, self.steps[-1])
        self.send = send

    def advance(self, *ready):
        if len(self.steps) == 1:
            return ()
        self.steps.pop()
        half = self.keep.shape[0] // 2
        total = self.keep.astype(F32) + after(self.got, *ready).astype(F32)
        self.keep, self.send = total[:half].astype(BF), total[half:].astype(BF)
        self.got = swap(self.send, self.steps[-1])
        return (self.send,)


class Total:
    def __init__(self, value, steps):
        self.value, self.steps = value, list(steps)
        self.got = swap(value, self.steps[-1])

    def advance(self, *ready):
        if not self.steps:
            return ()
        self.steps.pop()
        self.value = self.value + after(self.got, *ready)
        if self.steps:
            self.got = swap(self.value, self.steps[-1])
        return (self.value,)

    def result(self):
        while self.steps:
            self.advance(self.value)
        return self.value


class RowSums:
    def __init__(self, pieces, bits):
        self.parts, self.bits = {off: [piece] for off, piece in enumerate(pieces)}, list(bits)
        self.flights = []
        self.start()

    def start(self, *ready):
        bit = self.bits.pop()
        sends = []
        for off in [off for off in self.parts if off & bit]:
            parts = self.parts.pop(off)
            total = parts[0]
            if len(parts) > 1:
                total = functools.reduce(
                    lambda a, b: a + b, [parts[0].astype(F32)] + [after(p, *ready).astype(F32) for p in parts[1:]]
                ).astype(BF)
            self.parts[off ^ bit].append(swap(total, ("head", bit)))
            sends.append(total)
        return tuple(sends)

    def advance(self, *ready):
        return self.start(*ready) if self.bits else ()

    def finish(self, value, *ready):
        return functools.reduce(lambda a, b: a + b, [after(p, *ready).astype(F32) for p in self.parts[0]], value)


def lane_mask_stack(v, lh):
    if lh == 1:
        return v
    lane = lax.broadcasted_iota(jnp.int32, v.shape, 1)
    zero = jnp.zeros_like(v)
    return jnp.concatenate(
        [jnp.where((lane >= l * HD) & (lane < (l + 1) * HD), v, zero) for l in range(lh)], axis=0
    )


def head_rows_merge(vt, lh):
    return jnp.concatenate(
        [vt[l * HD : (l + 1) * HD, l * TQ : (l + 1) * TQ] for l in range(lh)], axis=0
    )


def qkv_kernel(lh, n_dp, n_h, dp_offs, idx_ref, w_own, w_got, *refs):
    rows = refs[:n_h]
    q_ref, k_ref, v_ref, vt_ref, wg_ref, inner_ref, w_s, b_s = refs[n_h:]
    g, h = idx_ref[0], idx_ref[1]
    width = lh * HD
    ds_rows = D // n_dp
    rw = rows[0].shape[0]
    shares = b_s.shape[1] // lh
    for p in range(n_dp):
        block = g ^ dp_offs[p]
        w_ref, p = (w_own, p) if p < n_dp // 2 else (w_got, p - n_dp // 2)
        w_s[pl.ds(pl.multiple_of(block * ds_rows, ds_rows), ds_rows), :] = w_ref[p, :ds_rows, :]
        b_s[pl.ds(block, 1), :] = w_ref[p, ds_rows : ds_rows + 16, : lh * shares][:1].astype(F32)
    wide = w_s[...].astype(F32)
    wg = jnp.concatenate(
        [
            wide[:, l * 3 * HD + kind * HD : l * 3 * HD + (kind + 1) * HD]
            for kind in range(3)
            for l in range(lh)
        ],
        axis=1,
    ).astype(BF)
    wg_ref[...] = wg
    per_head = [
        jnp.concatenate([b_s[b : b + 1, l * shares : (l + 1) * shares] for b in range(n_dp)], axis=1)
        for l in range(lh)
    ]
    q_bias = jnp.concatenate([r[:, :HD] for r in per_head], axis=1)
    v_bias = jnp.concatenate([r[:, HD : 2 * HD] for r in per_head], axis=1)
    inner = jnp.concatenate([r[:, 2 * HD :] for r in per_head], axis=1)
    inner_ref[...] = jnp.concatenate(
        [inner[:, i * width : (i + 1) * width] for i in range(inner.shape[1] // width)]
        + [jnp.zeros((16 - inner.shape[1] // width, width), F32)],
        axis=0,
    ).astype(BF)
    for off in range(n_h):
        base = pl.multiple_of((h ^ off) * rw, rw)
        qkv = dot(rows[off][...], wg_ref[...], 1, 0)
        q_ref[pl.ds(base, rw), :] = (qkv[:, :width] + q_bias).astype(BF)
        k_ref[pl.ds(base, rw), :] = qkv[:, width : 2 * width].astype(BF)
        v_ref[pl.ds(base, rw), :] = (qkv[:, 2 * width :] + v_bias).astype(BF)
    vt_ref[:width, :] = v_ref[...].T
    vt_ref[width:, :] = jnp.ones((16, v_ref.shape[0]), BF)


def attend_kernel(lh, offs, idx_ref, seg_ref, q_ref, k_ref, vt_ref, inner_ref, *refs):
    pieces = refs[: len(offs)]
    lse_ref, s_s, acc_s, start_s = refs[len(offs) :]
    h = idx_ref[1]
    width = lh * HD
    rw = pieces[0].shape[0] - 16
    start_s[...] = document_starts(seg_ref[...])
    factor = SCORE_SCALE * LOG2E
    cols = lh * TQ

    def query_block(piece_ref, place_at, base, i, carry):
        inside = pl.multiple_of(i * TQ, TQ)
        r0 = pl.multiple_of(base + inside, TQ)
        qb = r0 // TQ
        q2 = lane_mask_stack(q_ref[pl.ds(r0, TQ), :], lh)
        start = start_s[:, pl.ds(r0, TQ)]
        lo = (jnp.min(start) * (1.0 / TK)).astype(jnp.int32)
        start = jnp.concatenate([start.astype(jnp.int32)] * lh, axis=1)
        column = lax.broadcasted_iota(jnp.int32, (1, cols), 1) % TQ

        def scores(kb, top):
            c0 = pl.multiple_of(kb * TK, TK)
            s = dot(k_ref[pl.ds(c0, TK), :], q2, 1, 1)
            key = lax.broadcasted_iota(jnp.int32, (TK, cols), 0)
            ok = (key >= start - c0) & (key <= column + (r0 - c0))
            s = jnp.where(ok, s, NEG_LARGE)
            s_s[kb - lo] = s
            return jnp.maximum(top, jnp.max(s.reshape(TK // 8, 8, cols), axis=0))

        top = lax.fori_loop(lo, qb + 1, scores, jnp.full((8, cols), NEG_LARGE, F32))
        top = jnp.max(top, axis=0, keepdims=True)
        acc_s[...] = jnp.zeros_like(acc_s)

        def mix(kb, carry):
            c0 = pl.multiple_of(kb * TK, TK)
            p = jnp.exp2((s_s[kb - lo] - top) * factor).astype(BF)
            acc_s[...] += dot(vt_ref[:, pl.ds(c0, TK)], p, 1, 0)
            return carry

        lax.fori_loop(lo, qb + 1, mix, 0)
        total = acc_s[width : width + 1, :]
        out_t = head_rows_merge(acc_s[:width, :] / total, lh)
        piece_ref[pl.ds(inside, TQ), :] = out_t.T.astype(BF)
        lse_ref[place_at + i] = jnp.broadcast_to(top * factor + jnp.log2(total), (8, cols))
        return carry

    for n, off in enumerate(offs):
        body = functools.partial(query_block, pieces[n], n * (rw // TQ), (h ^ off) * rw)
        lax.fori_loop(0, rw // TQ, body, 0)
        pieces[n][rw:, :] = inner_ref[...]


def document_starts(segment):
    seg = segment.astype(F32)
    start = jnp.zeros(seg.shape, F32)
    for s in range(HEADS):
        count = jnp.sum(jnp.where(seg == float(s), 1.0, 0.0), axis=1, keepdims=True)
        start = start + jnp.where(seg > float(s), count, 0.0)
    return start


def norm_back(grad, xhat, rstd, gain):
    g = grad * gain
    return rstd * (
        g - jnp.mean(g, axis=-1, keepdims=True) - xhat * jnp.mean(g * xhat, axis=-1, keepdims=True)
    )


def fold(v):
    return jnp.sum(v.reshape(v.shape[0] // 8, 8, v.shape[1]), axis=0)


def middle_kernel(lh, n_dp, n_h, e_steps, c_steps, idx_ref, norm_ref, *refs):
    width = lh * HD
    mixed = refs[:n_h]
    e_parts, c_parts = refs[n_h : n_h + 4], refs[n_h + 4 : n_h + 8]
    post_in, dual_in, post_cot, dual_cot = refs[n_h + 8 : n_h + 12]
    outs = refs[n_h + 12 :]
    post_out, dual_out, gmid1_ref = outs[:3]
    gm = outs[3 : 3 + n_h]
    ge_keep, ge_send, gc_keep, gc_send, small_ref = outs[3 + n_h : 8 + n_h]
    (e_s, c_s, o_s, mix_s, bias_s, hid_s, acc_s, xh_s, rs_s, pn_s, xb_s, xt_s, gb_s, gmid2_s, ffb_s) = outs[
        8 + n_h :
    ]
    g, h = idx_ref[0], idx_ref[1]
    rw = post_in.shape[0]
    ds_rows = D // n_dp
    units = hid_s.shape[2]
    row = lambda i: norm_ref[i : i + 1, :]

    e_dp, e_h = offsets(e_steps, "dp"), offsets(e_steps, "head")
    c_dp, c_h = offsets(c_steps, "dp"), offsets(c_steps, "head")
    quarter = n_dp * n_h // 4
    for p in range(n_dp * n_h):
        at = pl.ds(pl.multiple_of((g ^ e_dp[p]) * ds_rows, ds_rows), ds_rows)
        e_ref, c_ref, i = e_parts[p // quarter], c_parts[p // quarter], p % quarter
        e_s[e_h[p], at, :] = e_ref[i]
        at = pl.ds(pl.multiple_of((g ^ c_dp[p]) * ds_rows, ds_rows), ds_rows)
        c_s[c_h[p], at, :] = c_ref[i, :, :units]
        o_s[at, c_h[p] * width : (c_h[p] + 1) * width] = c_ref[i, :, units:]
    for off in range(n_h):
        mix_s[:, off * width : (off + 1) * width] = mixed[off][:rw, :]
        tail = mixed[off][rw : rw + 16, :].astype(F32)
        bias_s[off] = jnp.concatenate([tail[i : i + 1, :] for i in range(units // width)], axis=1)

    acc_s[...] = dot(mix_s[...], o_s[...], 1, 1)

    def chunk_one(i, carry):
        at = pl.ds(pl.multiple_of(i * CH, CH), CH)
        attn_out = acc_s[at, :] + row(2)
        v = post_in[at, :] + attn_out
        centered = v - jnp.mean(v, axis=-1, keepdims=True)
        rstd = lax.rsqrt(jnp.mean(centered * centered, axis=-1, keepdims=True) + EPS_NORM)
        xhat = centered * rstd
        pn = xhat * row(0) + row(1)
        xh_s[at, :] = xhat
        rs_s[at, :] = jnp.broadcast_to(rstd, (CH, 128))
        pn_s[at, :] = pn
        xb_s[at, :] = pn.astype(BF)
        dual_out[at, :] = dual_in[at, :] + attn_out
        return carry

    lax.fori_loop(0, rw // CH, chunk_one, 0)
    xt_s[...] = xb_s[...].T
    acc_s[...] = jnp.zeros_like(acc_s)

    def inner(oh, carry):
        pre = dot(xb_s[...], e_s[oh], 1, 0) + bias_s[oh]
        hid = jnp.maximum(pre, 0.0).astype(BF)
        hid_s[oh] = hid
        acc_s[...] += dot(hid, c_s[oh], 1, 1)
        return carry

    lax.fori_loop(0, n_h, inner, 0)

    def chunk_two(i, carry):
        gain_sum, shift_sum, ffn_sum = carry
        at = pl.ds(pl.multiple_of(i * CH, CH), CH)
        ffn_out = acc_s[at, :] + row(5)
        v = pn_s[at, :] + ffn_out
        centered = v - jnp.mean(v, axis=-1, keepdims=True)
        rstd = lax.rsqrt(jnp.mean(centered * centered, axis=-1, keepdims=True) + EPS_NORM)
        xhat = centered * rstd
        post_out[at, :] = xhat * row(3) + row(4)
        dual_out[at, :] = dual_out[at, :] + ffn_out
        cot = post_cot[at, :]
        gmid2 = norm_back(cot, xhat, rstd, row(3))
        gffn = gmid2 + dual_cot[at, :]
        gmid2_s[at, :] = gmid2
        gb_s[at, :] = gffn.astype(BF)
        return gain_sum + fold(cot * xhat), shift_sum + fold(cot), ffn_sum + fold(gffn)

    zero = jnp.zeros((8, D), F32)
    gain2, shift2, ffn_sum = lax.fori_loop(0, rw // CH, chunk_two, (zero, zero, zero))
    acc_s[...] = jnp.zeros_like(acc_s)
    gt = gb_s[...].T
    hid_t = gt

    def inner_back(pair, carry):
        for low in range(2):
            oh = pair * 2 + low
            ge, gc = (ge_keep, gc_keep) if low == 0 else (ge_send, gc_send)
            hid = hid_s[oh]
            gh = dot(gb_s[...], c_s[oh], 1, 0)
            gp = jnp.where(hid > 0, gh, 0.0).astype(BF)
            ffb_s[oh] = jnp.sum(gp.astype(F32), axis=0, keepdims=True)
            acc_s[...] += dot(gp, e_s[oh], 1, 1)
            grad_c = dot(hid_t, hid, 1, 0).astype(BF)
            grad_e = dot(xt_s[...], gp, 1, 0).astype(BF)
            for b in range(n_dp):
                ge[place(e_steps, "dp", b ^ g) + place(e_steps, "head", oh - low)] = grad_e[
                    b * ds_rows : (b + 1) * ds_rows
                ]
                gc[place(c_steps, "dp", b ^ g) + place(c_steps, "head", oh - low), :, :units] = grad_c[
                    b * ds_rows : (b + 1) * ds_rows
                ]
        return carry

    lax.fori_loop(0, n_h // 2, inner_back, 0)

    def chunk_three(i, carry):
        gain_sum, shift_sum, attn_sum = carry
        at = pl.ds(pl.multiple_of(i * CH, CH), CH)
        grad = gmid2_s[at, :] + acc_s[at, :]
        xhat = xh_s[at, :]
        gmid1 = norm_back(grad, xhat, rs_s[at, :1], row(0))
        gmid1_ref[at, :] = gmid1
        gattn = gmid1 + dual_cot[at, :]
        gb_s[at, :] = gattn.astype(BF)
        return gain_sum + fold(grad * xhat), shift_sum + fold(grad), attn_sum + fold(gattn)

    gain1, shift1, attn_sum = lax.fori_loop(0, rw // CH, chunk_three, (zero, zero, zero))
    grad_mixed = dot(gb_s[...], o_s[...], 1, 0).astype(BF)
    for off in range(n_h):
        gm[off][...] = grad_mixed[:, off * width : (off + 1) * width]
    grad_o = dot(gb_s[...].T, mix_s[...], 1, 0).astype(BF)
    for oh in range(n_h):
        gc = gc_keep if oh % 2 == 0 else gc_send
        for b in range(n_dp):
            gc[place(c_steps, "dp", b ^ g) + place(c_steps, "head", oh - oh % 2), :, units:] = grad_o[
                b * ds_rows : (b + 1) * ds_rows, oh * width : (oh + 1) * width
            ]
    for i, part in enumerate((gain1, shift1, attn_sum, gain2, shift2, ffn_sum)):
        line = jnp.sum(part, axis=0, keepdims=True)
        for j in range(D // 128):
            small_ref[4 * i + j : 4 * i + j + 1, :] = line[:, j * 128 : (j + 1) * 128]
    for oh in range(n_h):
        first = 24 + (h ^ oh) * (units // 128)
        for j in range(units // 128):
            small_ref[pl.ds(first + j, 1), :] = ffb_s[oh, :, j * 128 : (j + 1) * 128]


def attend_back_kernel(lh, n_h, idx_ref, seg_ref, q_ref, k_ref, v_ref, lse_near, lse_far, small_in, *refs):
    gm, pieces = refs[:n_h], refs[n_h : 2 * n_h]
    gqkv_ref, small_ref, do_s, o_ref, lse_ref, kt_s, dk_s, dv_s, dq_s, start_s = refs[2 * n_h :]
    h = idx_ref[1]
    width = lh * HD
    rw = gm[0].shape[0]
    n_rows = q_ref.shape[0]
    cols = lh * TQ
    factor = SCORE_SCALE * LOG2E
    for off in range(n_h):
        at = pl.ds(pl.multiple_of((h ^ off) * rw, rw), rw)
        do_s[at, :] = gm[off][...]
        o_ref[at, :] = pieces[off][:rw, :]
        lse_part, n = (lse_near, off) if off < n_h // 2 else (lse_far, off - n_h // 2)
        for i in range(rw // TQ):
            lse_ref[(h ^ off) * (rw // TQ) + i] = lse_part[n * (rw // TQ) + i]
    start_s[...] = document_starts(seg_ref[...])
    kt_s[...] = k_ref[...].T
    dk_s[...] = jnp.zeros_like(dk_s)
    dv_s[...] = jnp.zeros_like(dv_s)

    def query_block(qb, q_sum):
        r0 = pl.multiple_of(qb * TQ, TQ)
        at = pl.ds(r0, TQ)
        q2 = lane_mask_stack(q_ref[at, :], lh)
        do = do_s[at, :]
        do2 = lane_mask_stack(do, lh)
        prod = (do.astype(F32) * o_ref[at, :].astype(F32)).T
        delta = jnp.concatenate(
            [jnp.sum(prod[l * HD : (l + 1) * HD, :], axis=0, keepdims=True) for l in range(lh)], axis=1
        )
        lse = lse_ref[qb][:1]
        start = start_s[:, at]
        lo = (jnp.min(start) * (1.0 / TK)).astype(jnp.int32)
        start = jnp.concatenate([start.astype(jnp.int32)] * lh, axis=1)
        column = lax.broadcasted_iota(jnp.int32, (1, cols), 1) % TQ
        dq_s[...] = jnp.zeros_like(dq_s)

        def pair(kb, carry):
            c0 = pl.multiple_of(kb * TK, TK)
            keys = pl.ds(c0, TK)
            s = dot(k_ref[keys, :], q2, 1, 1)
            key = lax.broadcasted_iota(jnp.int32, (TK, cols), 0)
            ok = (key >= start - c0) & (key <= column + (r0 - c0))
            p = jnp.exp2(jnp.where(ok, s, NEG_LARGE) * factor - lse)
            dp = dot(v_ref[keys, :], do2, 1, 1)
            grad = (p * (dp - delta)).astype(BF)
            dv_s[keys, :] += dot(p.astype(BF), do2, 1, 0)
            dk_s[keys, :] += dot(grad, q2, 1, 0)
            dq_s[...] += dot(kt_s[:, keys], grad, 1, 0)
            return carry

        lax.fori_loop(lo, qb + 1, pair, 0)
        dq = (head_rows_merge(dq_s[...], lh) * SCORE_SCALE).T.astype(BF)
        gqkv_ref[at, :width] = dq
        return q_sum + jnp.sum(dq.astype(F32), axis=0, keepdims=True)

    q_sum = lax.fori_loop(0, n_rows // TQ, query_block, jnp.zeros((1, width), F32))
    gqkv_ref[:, width : 2 * width] = (dk_s[...] * SCORE_SCALE).astype(BF)
    dv = dv_s[...].astype(BF)
    gqkv_ref[:, 2 * width :] = dv
    v_sum = jnp.sum(dv.astype(F32), axis=0, keepdims=True)
    small_ref[:40, :] = small_in[...]
    small_ref[40:, :] = jnp.zeros((8, 128), F32)
    for l in range(lh):
        small_ref[pl.ds(40 + h * lh + l, 1), :] = jnp.concatenate(
            [q_sum[:, l * HD : (l + 1) * HD], v_sum[:, l * HD : (l + 1) * HD]], axis=1
        )


def rows_back_kernel(n_h, idx_ref, gqkv_ref, wg_ref, *outs):
    h = idx_ref[1]
    rw = outs[0].shape[0]
    for off in range(n_h):
        at = pl.ds(pl.multiple_of((h ^ off) * rw, rw), rw)
        outs[off][...] = dot(gqkv_ref[at, :], wg_ref[...], 1, 1).astype(BF)


def attend_grad_kernel(lh, n_dp, n_h, steps, idx_ref, gqkv_ref, *refs):
    rows = refs[:n_h]
    out_ref, acc_s = refs[n_h:]
    g, h = idx_ref[0], idx_ref[1]
    rw = rows[0].shape[0]
    ds_rows = D // n_dp
    width = lh * HD
    for off in range(n_h):
        at = pl.ds(pl.multiple_of((h ^ off) * rw, rw), rw)
        part = dot(rows[off][...], gqkv_ref[at, :], 0, 0)
        acc_s[...] = part if off == 0 else acc_s[...] + part
    full = acc_s[...]
    full = jnp.concatenate(
        [full[:, kind * width + l * HD : kind * width + (l + 1) * HD] for l in range(lh) for kind in range(3)],
        axis=1,
    ).astype(BF)
    for b in range(n_dp):
        out_ref[place(steps, "dp", b ^ g)] = full[b * ds_rows : (b + 1) * ds_rows]


def total_of_pair(keep_ref, got_ref):
    return keep_ref[0].astype(F32) + got_ref[0].astype(F32)


def squares_kernel(*refs):
    out_ref = refs[-1]
    acc = jnp.zeros((8, 128), F32)
    for i in range(0, len(refs) - 1, 2):
        v = total_of_pair(refs[i], refs[i + 1])
        v = fold(v * v)
        if v.shape[1] % 128:
            v = jnp.concatenate([v, jnp.zeros((8, 128 - v.shape[1] % 128), F32)], axis=1)
        for j in range(v.shape[1] // 128):
            acc = acc + v[:, j * 128 : (j + 1) * 128]
    out_ref[...] = acc


def adam_kernel(units, clip_ref, sq_ref, sq_got, small_ref, *refs):
    ga, ge, gc = refs[0:2], refs[2:4], refs[4:6]
    share_bias, norm_grads = refs[6:8]
    params, momenta, variances = refs[8:14], refs[14:20], refs[20:26]
    norm_ref, clipped_ref = refs[26:28]
    outs = list(refs[28:])
    small = small_ref[...]
    squares = jnp.sum(sq_ref[...] + sq_got[...]) + jnp.sum(small * small)
    norm = jnp.sqrt(jnp.full((8, 128), squares))
    norm_ref[...] = norm
    limit = clip_ref[0]
    factor = (limit / jnp.maximum(norm, limit))[:1, :1]
    share_co = total_of_pair(*gc)
    grads = (
        total_of_pair(*ga),
        share_co[:, units:],
        total_of_pair(*ge),
        share_co[:, :units],
        share_bias[...],
        norm_grads[...],
    )
    for w, m, va, grad, rate in zip(params, momenta, variances, grads, RATES):
        clipped = factor * grad
        momentum_new = BETA * m[...] + (1.0 - BETA) * clipped
        variance_new = BETA * va[...] + (1.0 - BETA) * clipped * clipped
        step = momentum_new / BIAS_CORRECTION / (jnp.sqrt(variance_new / BIAS_CORRECTION) + ADAM_EPS)
        master_new = w[...] - rate * (step + DECAY * w[...])
        outs.pop(0)[...] = momentum_new
        outs.pop(0)[...] = variance_new
        outs.pop(0)[...] = master_new
        if len(outs) > 2:
            outs.pop(0)[...] = master_new.astype(BF)
    clipped_ref[...] = factor * norm_grads[...]


def call(body, outs, scratch, n_smem, args, limit, us):
    return pl.pallas_call(
        body,
        out_shape=outs,
        in_specs=[SMEM] * n_smem + [VMEM] * (len(args) - n_smem),
        out_specs=jax.tree.map(lambda _: VMEM, outs),
        scratch_shapes=scratch,
        compiler_params=pltpu.CompilerParams(vmem_limit_bytes=limit << 20),
        cost_estimate=pl.CostEstimate(flops=us * FLOPS_PER_US, bytes_accessed=1 << 20, transcendentals=0),
    )(*args)


def sds(shape, dtype):
    return jax.ShapeDtypeStruct(shape, dtype)


def per_device(
    post_in,
    dual_in,
    segment_ids,
    post_cot,
    dual_cot,
    attend_weight,
    output_weight,
    expand_weight,
    contract_weight,
    head_bias,
    norm_params,
    attend_momentum,
    output_momentum,
    expand_momentum,
    contract_momentum,
    bias_momentum,
    norm_momentum,
    attend_variance,
    output_variance,
    expand_variance,
    contract_variance,
    bias_variance,
    norm_variance,
    clip_limit,
):
    n_dp, n_h = lax.axis_size("dp"), lax.axis_size("head")
    g, h = lax.axis_index("dp"), lax.axis_index("head")
    idx = jnp.stack([g, h]).astype(jnp.int32)
    rw = post_in.shape[0]
    n_rows = rw * n_h
    lh = HEADS // n_h
    width = lh * HD
    ds_rows = attend_weight.shape[0]
    a_cols = attend_weight.shape[1]
    units = expand_weight.shape[1]
    shares = head_bias.shape[1]
    dp_bits, h_bits = bits_of(n_dp), bits_of(n_h)
    a_steps = [("dp", b) for b in dp_bits]
    e_steps = [("dp", b) for b in dp_bits] + [("head", b) for b in h_bits]
    c_steps = (
        [("dp", b) for b in dp_bits[:-1]]
        + [("head", b) for b in h_bits[:-1]]
        + [("dp", dp_bits[-1])]
        + [("head", h_bits[-1])]
    )

    rows_own = post_in.astype(BF)
    bias_block = jnp.pad(
        head_bias.astype(BF).reshape(1, lh * shares), ((0, 15), (0, a_cols - lh * shares))
    )
    a_msg = jnp.concatenate([attend_weight.astype(BF), bias_block], axis=0)
    e_msg = expand_weight.astype(BF)
    c_msg = jnp.concatenate([contract_weight.T.astype(BF), output_weight.T.astype(BF)], axis=1)

    rows = {0: rows_own}
    for bit in h_bits:
        for off in list(rows):
            rows[off ^ bit] = swap(rows[off], ("head", bit))
    rows = [rows[off] for off in range(n_h)]

    n_d, n_s = len(dp_bits), len(e_steps)
    a_in, a_got = [a_msg[None]], []
    for i, step in enumerate(a_steps):
        a_got.append(swap(a_in[i], step))
        if i < n_d - 1:
            a_in.append(jnp.concatenate([a_in[i], a_got[i]], axis=0))
    e_in, e_got, c_in, c_got = [e_msg[None]], [], [c_msg[None]], []

    def exchange(*ready):
        i = len(e_got)
        if i == 0:
            e_in[0], c_in[0] = after(e_in[0], *ready), after(c_in[0], *ready)
        else:
            e_in.append(jnp.concatenate([e_in[-1], after(e_got[-1], *ready)], axis=0))
            c_in.append(jnp.concatenate([c_in[-1], after(c_got[-1], *ready)], axis=0))
        e_got.append(swap(e_in[i], e_steps[i]))
        c_got.append(swap(c_in[i], c_steps[i]))

    for i in range(n_d - 1):
        exchange(a_got[i])
    n_q = n_rows // TQ
    cols = lh * TQ
    q, k, v, vt, wg, inner = call(
        functools.partial(qkv_kernel, lh, n_dp, n_h, offsets(a_steps, "dp")),
        [sds((n_rows, width), BF)] * 3
        + [sds((width + 16, n_rows), BF), sds((D, 3 * width), BF), sds((16, width), BF)],
        [pltpu.VMEM((D, a_cols), BF), pltpu.VMEM((n_dp, lh * shares), F32)],
        1,
        [idx, after(a_in[-1], e_in[n_d - 2], c_in[n_d - 2]), a_got[-1]] + rows,
        24,
        4,
    )

    def attend(offs, q):
        out = call(
            functools.partial(attend_kernel, lh, offs),
            [sds((rw + 16, width), BF)] * len(offs) + [sds((n_q // 2, 8, cols), F32)],
            [
                pltpu.VMEM((KEY_BLOCKS, TK, cols), F32),
                pltpu.VMEM((width + 16, cols), F32),
                pltpu.VMEM((1, n_rows), F32),
            ],
            1,
            [idx, segment_ids, q, k, vt, inner],
            24,
            5,
        )
        return out[:-1], out[-1]

    exchange(q)
    far, lse_far = attend(range(n_h // 2, n_h), after(q, e_in[n_d - 1], c_in[n_d - 1]))
    exchange(far[0])
    near, lse_near = attend(range(n_h // 2), after(q, e_in[n_d], c_in[n_d]))
    for i in range(n_d + 1, n_s - 1):
        exchange()
    pieces = list(near) + list(far)
    mixed = [pieces[0]] + [
        lax.ppermute(pieces[off], "head", [(i, i ^ off) for i in range(n_h)]) for off in range(1, n_h)
    ]
    arrived = [near[0]] + mixed[n_h // 2 :]
    e_in[-1], c_in[-1] = after(e_in[-1], *arrived), after(c_in[-1], *arrived)
    e_got[-1], c_got[-1] = after(e_got[-1], *arrived), after(c_got[-1], *arrived)
    e_parts = [e_in[-1], e_got[-1]]
    e_parts += [swap(part, e_steps[-1]) for part in e_parts]
    c_parts = [c_in[-1], c_got[-1]]
    c_parts += [swap(part, c_steps[-1]) for part in c_parts]
    half = n_dp * n_h // 2
    middle_out = call(
        functools.partial(middle_kernel, lh, n_dp, n_h, e_steps, c_steps),
        [sds((rw, D), F32)] * 3
        + [sds((rw, width), BF)] * n_h
        + [sds((half, ds_rows, units), BF)] * 2
        + [sds((half, ds_rows, units + width), BF)] * 2
        + [sds((40, 128), F32)],
        [
            pltpu.VMEM((n_h, D, units), BF),
            pltpu.VMEM((n_h, D, units), BF),
            pltpu.VMEM((D, n_h * width), BF),
            pltpu.VMEM((rw, n_h * width), BF),
            pltpu.VMEM((n_h, 1, units), F32),
            pltpu.VMEM((n_h, rw, units), BF),
            pltpu.VMEM((rw, D), F32),
            pltpu.VMEM((rw, D), F32),
            pltpu.VMEM((rw, 128), F32),
            pltpu.VMEM((rw, D), F32),
            pltpu.VMEM((rw, D), BF),
            pltpu.VMEM((D, rw), BF),
            pltpu.VMEM((rw, D), BF),
            pltpu.VMEM((rw, D), F32),
            pltpu.VMEM((n_h, 1, units), F32),
        ],
        1,
        [idx, norm_params] + mixed + e_parts + c_parts + [post_in, dual_in, post_cot, dual_cot],
        52,
        20,
    )
    post_out, dual_out, grad_mid1 = middle_out[:3]
    gm = middle_out[3 : 3 + n_h]
    ge_keep, ge_send, gc_keep, gc_send, small_mid = middle_out[3 + n_h :]
    gm = [gm[0]] + [
        lax.ppermute(gm[off], "head", [(i, i ^ off) for i in range(n_h)]) for off in range(1, n_h)
    ]
    ge, gc = Scatter(ge_keep, ge_send, e_steps), Scatter(gc_keep, gc_send, c_steps)
    gm[0] = after(gm[0], *ge.advance(), *gc.advance())
    gqkv, small = call(
        functools.partial(attend_back_kernel, lh, n_h),
        [sds((n_rows, 3 * width), BF), sds((48, 128), F32)],
        [
            pltpu.VMEM((n_rows, width), BF),
            pltpu.VMEM((n_rows, width), BF),
            pltpu.VMEM((n_q, 8, cols), F32),
            pltpu.VMEM((width, n_rows), BF),
            pltpu.VMEM((n_rows, width), F32),
            pltpu.VMEM((n_rows, width), F32),
            pltpu.VMEM((width, cols), F32),
            pltpu.VMEM((1, n_rows), F32),
        ],
        1,
        [idx, segment_ids, q, k, v, lse_near, lse_far, small_mid] + gm + pieces,
        32,
        15,
    )
    total = Total(small, e_steps)
    sent = ge.advance(gqkv) + gc.advance(gqkv)
    ga = call(
        functools.partial(attend_grad_kernel, lh, n_dp, n_h, a_steps),
        sds((n_dp, ds_rows, a_cols), BF),
        [pltpu.VMEM((D, 3 * width), F32)],
        1,
        [idx, after(gqkv, *sent)] + rows,
        24,
        2,
    )
    ga = Scatter(ga[: n_dp // 2], ga[n_dp // 2 :], a_steps)
    back = call(
        functools.partial(rows_back_kernel, n_h),
        [sds((rw, D), BF)] * n_h,
        [],
        1,
        [idx, after(gqkv, ga.send), wg],
        24,
        2,
    )
    back = RowSums(back, sorted(h_bits, reverse=True))
    sent = ()
    for _ in range(len(h_bits) - 1):
        sent = back.advance(*sent)
    for i in range(n_s):
        for chain in (ge, gc, total, ga):
            sent = chain.advance(*sent) or sent
            if i == 1 and chain is gc:
                post_grad = back.finish(grad_mid1, *sent)
                sent = (post_grad,)
    small = total.result()
    norm_grads = small[:24].reshape(6, D)
    bias_full = jnp.concatenate(
        [
            lax.dynamic_slice_in_dim(small, 40 + h * lh, lh, 0),
            lax.dynamic_slice_in_dim(small, 24 + h * 2 * lh, 2 * lh, 0).reshape(lh, 256),
        ],
        axis=1,
    )
    share_bias = lax.dynamic_slice_in_dim(bias_full, g * shares, shares, 1)
    pairs = [ga.keep, ga.got, ge.keep, ge.got, gc.keep, gc.got]
    pairs[0] = after(pairs[0], *sent)
    squares = call(squares_kernel, sds((8, 128), F32), [], 0, pairs, 16, 1)
    squares = Total(squares, e_steps)
    for _ in e_steps[:-1]:
        squares.advance()
    flip = lambda arrays: [a.T if i in (1, 3) else a for i, a in enumerate(arrays)]
    params = flip([attend_weight, output_weight, expand_weight, contract_weight, head_bias, norm_params])
    momenta = flip(
        [attend_momentum, output_momentum, expand_momentum, contract_momentum, bias_momentum, norm_momentum]
    )
    variances = flip(
        [attend_variance, output_variance, expand_variance, contract_variance, bias_variance, norm_variance]
    )
    shapes = [sds((8, 128), F32), sds((6, D), F32)]
    for i, w in enumerate(params):
        shapes += [sds(w.shape, F32)] * 3 + ([sds(w.shape, BF)] if i < 5 else [])
    norm, norm_clipped, *results = call(
        functools.partial(adam_kernel, units),
        shapes,
        [],
        1,
        [clip_limit, squares.value, squares.got, small] + pairs + [share_bias, norm_grads] + params + momenta + variances,
        24,
        2,
    )
    results = [a.T if i // 4 in (1, 3) else a for i, a in enumerate(results)]
    return (post_out, dual_out, post_grad, norm[0, :1], *results, norm_clipped)


def solution(mesh):
    rows = P(("dp", "head"), None)
    tall, flat, rep = P("dp", "head"), P("head", "dp"), P()
    weights = (tall, flat, tall, flat, flat, rep)
    in_specs = (rows, rows, P("dp", None), rows, rows) + weights * 3 + (rep,)
    out_specs = (rows, rows, rows, rep)
    for spec in (tall, flat, tall, flat, flat):
        out_specs += (spec,) * 4
    out_specs += (rep,) * 4
    return jax.shard_map(per_device, mesh=mesh, in_specs=in_specs, out_specs=out_specs, check_vma=False)
```

```python
import functools

import jax
import jax.numpy as jnp
from jax import lax
from jax.experimental import pallas as pl
from jax.experimental.pallas import tpu as pltpu
from jax.sharding import PartitionSpec as P

D = 512
HEADS = 8
HD = 64
TQ = 256
TK = 256
SEQ_MOST = 1024
KEY_BLOCKS = SEQ_MOST // TK + 1
CH = 64

EPS_NORM = 1e-05
NEG_LARGE = -1e30
LOG2E = 1.4426950408889634
SCORE_SCALE = HD ** (-0.5)
RATES = (0.04, 0.12, 0.04, 0.04, 0.16, 0.3)
DECAY = 0.01
ADAM_EPS = 1e-08
BETA = 0.5
BIAS_CORRECTION = 0.875
BF = jnp.bfloat16
FLOPS_PER_US = 10**9
F32 = jnp.float32
VMEM = pl.BlockSpec(memory_space=pltpu.VMEM)
SMEM = pl.BlockSpec(memory_space=pltpu.SMEM)


def dot(a, b, ca, cb):
    return lax.dot_general(a, b, (((ca,), (cb,)), ((), ())), preferred_element_type=F32)


def bits_of(count):
    bits = []
    while count > 1:
        count //= 2
        bits.append(count)
    return bits


def swap(v, step):
    axis, bit = step
    count = lax.axis_size(axis)
    return lax.ppermute(v, axis, [(i, i ^ bit) for i in range(count)])


def offsets(steps, axis):
    offs = [0]
    for name, bit in steps:
        offs = offs + [o ^ (bit if name == axis else 0) for o in offs]
    return offs


def after(v, *ready):
    return lax.optimization_barrier((v, *ready))[0]


def place(steps, axis, off):
    pos = 0
    for k, (name, bit) in enumerate(steps):
        if name == axis:
            pos = pos + ((off // bit) % 2) * (1 << k)
    return pos


class Scatter:
    def __init__(self, keep, send, steps):
        self.keep, self.steps = keep, list(steps)
        self.got = swap(send, self.steps[-1])
        self.send = send

    def advance(self, *ready):
        self.keep, self.send = self.take(*ready)
        self.steps.pop()
        self.got = swap(self.send, self.steps[-1])
        return (self.send,)

    def take(self, *ready):
        half = self.keep.shape[0] // 2
        total = self.keep.astype(F32) + after(self.got, *ready).astype(F32)
        return total[:half].astype(BF), total[half:].astype(BF)


class Total:
    def __init__(self, value, steps):
        self.value, self.steps = value, list(steps)
        self.got = swap(value, self.steps[-1])

    def advance(self, *ready):
        if not self.steps:
            return ()
        self.steps.pop()
        self.value = self.value + after(self.got, *ready)
        if self.steps:
            self.got = swap(self.value, self.steps[-1])
        return (self.value,)

    def result(self):
        while self.steps:
            self.advance(self.value)
        return self.value


class RowSums:
    def __init__(self, pieces, bits):
        self.parts, self.bits = {off: [piece] for off, piece in enumerate(pieces)}, list(bits)
        self.flights = []
        self.start()

    def start(self, *ready):
        bit = self.bits.pop()
        sends = []
        for off in [off for off in self.parts if off & bit]:
            parts = self.parts.pop(off)
            total = parts[0]
            if len(parts) > 1:
                total = functools.reduce(
                    lambda a, b: a + b, [parts[0].astype(F32)] + [after(p, *ready).astype(F32) for p in parts[1:]]
                ).astype(BF)
            self.parts[off ^ bit].append(swap(total, ("head", bit)))
            sends.append(total)
        return tuple(sends)

    def advance(self, *ready):
        return self.start(*ready) if self.bits else ()

    def finish(self, value, *ready):
        return functools.reduce(lambda a, b: a + b, [after(p, *ready).astype(F32) for p in self.parts[0]], value)


def lane_mask_stack(v, lh):
    if lh == 1:
        return v
    lane = lax.broadcasted_iota(jnp.int32, v.shape, 1)
    zero = jnp.zeros_like(v)
    return jnp.concatenate(
        [jnp.where((lane >= l * HD) & (lane < (l + 1) * HD), v, zero) for l in range(lh)], axis=0
    )


def head_rows_merge(vt, lh):
    return jnp.concatenate(
        [vt[l * HD : (l + 1) * HD, l * TQ : (l + 1) * TQ] for l in range(lh)], axis=0
    )


def qkv_kernel(lh, n_dp, n_h, dp_offs, idx_ref, w_own, w_got, *refs):
    rows = refs[:n_h]
    q_ref, k_ref, v_ref, vt_ref, wg_ref, inner_ref, w_s, b_s = refs[n_h:]
    g, h = idx_ref[0], idx_ref[1]
    width = lh * HD
    ds_rows = D // n_dp
    rw = rows[0].shape[0]
    shares = b_s.shape[1] // lh
    for p in range(n_dp):
        block = g ^ dp_offs[p]
        w_ref, p = (w_own, p) if p < n_dp // 2 else (w_got, p - n_dp // 2)
        w_s[pl.ds(pl.multiple_of(block * ds_rows, ds_rows), ds_rows), :] = w_ref[p, :ds_rows, :]
        b_s[pl.ds(block, 1), :] = w_ref[p, ds_rows : ds_rows + 16, : lh * shares][:1].astype(F32)
    wide = w_s[...].astype(F32)
    wg = jnp.concatenate(
        [
            wide[:, l * 3 * HD + kind * HD : l * 3 * HD + (kind + 1) * HD]
            for kind in range(3)
            for l in range(lh)
        ],
        axis=1,
    ).astype(BF)
    wg_ref[...] = wg
    per_head = [
        jnp.concatenate([b_s[b : b + 1, l * shares : (l + 1) * shares] for b in range(n_dp)], axis=1)
        for l in range(lh)
    ]
    q_bias = jnp.concatenate([r[:, :HD] for r in per_head], axis=1)
    v_bias = jnp.concatenate([r[:, HD : 2 * HD] for r in per_head], axis=1)
    inner = jnp.concatenate([r[:, 2 * HD :] for r in per_head], axis=1)
    inner_ref[...] = jnp.concatenate(
        [inner[:, i * width : (i + 1) * width] for i in range(inner.shape[1] // width)]
        + [jnp.zeros((16 - inner.shape[1] // width, width), F32)],
        axis=0,
    ).astype(BF)
    for off in range(n_h):
        base = pl.multiple_of((h ^ off) * rw, rw)
        qkv = dot(rows[off][...], wg_ref[...], 1, 0)
        q_ref[pl.ds(base, rw), :] = (qkv[:, :width] + q_bias).astype(BF)
        k_ref[pl.ds(base, rw), :] = qkv[:, width : 2 * width].astype(BF)
        v_ref[pl.ds(base, rw), :] = (qkv[:, 2 * width :] + v_bias).astype(BF)
    vt_ref[:width, :] = v_ref[...].T
    vt_ref[width:, :] = jnp.ones((16, v_ref.shape[0]), BF)


def attend_kernel(lh, offs, idx_ref, seg_ref, q_ref, k_ref, vt_ref, inner_ref, *refs):
    pieces = refs[: len(offs)]
    lse_ref, s_s, acc_s, start_s = refs[len(offs) :]
    h = idx_ref[1]
    width = lh * HD
    rw = pieces[0].shape[0] - 16
    start_s[...] = document_starts(seg_ref[...])
    factor = SCORE_SCALE * LOG2E
    cols = lh * TQ

    def query_block(piece_ref, place_at, base, i, carry):
        inside = pl.multiple_of(i * TQ, TQ)
        r0 = pl.multiple_of(base + inside, TQ)
        qb = r0 // TQ
        q2 = lane_mask_stack(q_ref[pl.ds(r0, TQ), :], lh)
        start = start_s[:, pl.ds(r0, TQ)]
        lo = (jnp.min(start) * (1.0 / TK)).astype(jnp.int32)
        start = jnp.concatenate([start.astype(jnp.int32)] * lh, axis=1)
        column = lax.broadcasted_iota(jnp.int32, (1, cols), 1) % TQ

        def scores(kb, top):
            c0 = pl.multiple_of(kb * TK, TK)
            s = dot(k_ref[pl.ds(c0, TK), :], q2, 1, 1)
            key = lax.broadcasted_iota(jnp.int32, (TK, cols), 0)
            ok = (key >= start - c0) & (key <= column + (r0 - c0))
            s = jnp.where(ok, s, NEG_LARGE)
            s_s[kb - lo] = s
            return jnp.maximum(top, jnp.max(s.reshape(TK // 8, 8, cols), axis=0))

        top = lax.fori_loop(lo, qb + 1, scores, jnp.full((8, cols), NEG_LARGE, F32))
        top = jnp.max(top, axis=0, keepdims=True)
        acc_s[...] = jnp.zeros_like(acc_s)

        def mix(kb, carry):
            c0 = pl.multiple_of(kb * TK, TK)
            p = jnp.exp2((s_s[kb - lo] - top) * factor).astype(BF)
            acc_s[...] += dot(vt_ref[:, pl.ds(c0, TK)], p, 1, 0)
            return carry

        lax.fori_loop(lo, qb + 1, mix, 0)
        total = acc_s[width : width + 1, :]
        out_t = head_rows_merge(acc_s[:width, :] / total, lh)
        piece_ref[pl.ds(inside, TQ), :] = out_t.T.astype(BF)
        lse_ref[place_at + i] = jnp.broadcast_to(top * factor + jnp.log2(total), (8, cols))
        return carry

    for n, off in enumerate(offs):
        body = functools.partial(query_block, pieces[n], n * (rw // TQ), (h ^ off) * rw)
        lax.fori_loop(0, rw // TQ, body, 0)
        pieces[n][rw:, :] = inner_ref[...]


def document_starts(segment):
    seg = segment.astype(F32)
    start = jnp.zeros(seg.shape, F32)
    for s in range(HEADS):
        count = jnp.sum(jnp.where(seg == float(s), 1.0, 0.0), axis=1, keepdims=True)
        start = start + jnp.where(seg > float(s), count, 0.0)
    return start


def norm_back(grad, xhat, rstd, gain):
    g = grad * gain
    return rstd * (
        g - jnp.mean(g, axis=-1, keepdims=True) - xhat * jnp.mean(g * xhat, axis=-1, keepdims=True)
    )


def fold(v):
    return jnp.sum(v.reshape(v.shape[0] // 8, 8, v.shape[1]), axis=0)


def middle_kernel(lh, n_dp, n_h, e_steps, c_steps, es_steps, cs_steps, idx_ref, norm_ref, *refs):
    width = lh * HD
    mixed = refs[:n_h]
    e_parts, c_parts = refs[n_h : n_h + 4], refs[n_h + 4 : n_h + 8]
    post_in, dual_in, post_cot, dual_cot = refs[n_h + 8 : n_h + 12]
    outs = refs[n_h + 12 :]
    post_out, dual_out, gmid1_ref = outs[:3]
    gm = outs[3 : 3 + n_h]
    ge_keep, ge_send, gc_keep, gc_send, small_ref = outs[3 + n_h : 8 + n_h]
    (e_s, c_s, o_s, mix_s, bias_s, hid_s, acc_s, xh_s, rs_s, pn_s, xb_s, xt_s, gb_s, gmid2_s, ffb_s, gp_s, gt_s) = outs[
        8 + n_h :
    ]
    g, h = idx_ref[0], idx_ref[1]
    rw = post_in.shape[0]
    ds_rows = D // n_dp
    units = hid_s.shape[1] // n_h
    row = lambda i: norm_ref[i : i + 1, :]

    e_dp, e_h = offsets(e_steps, "dp"), offsets(e_steps, "head")
    c_dp, c_h = offsets(c_steps, "dp"), offsets(c_steps, "head")
    quarter = n_dp * n_h // 4
    for p in range(n_dp * n_h):
        at = pl.ds(pl.multiple_of((g ^ e_dp[p]) * ds_rows, ds_rows), ds_rows)
        e_ref, c_ref, i = e_parts[p // quarter], c_parts[p // quarter], p % quarter
        e_s[at, e_h[p] * units : (e_h[p] + 1) * units] = e_ref[i]
        at = pl.ds(pl.multiple_of((g ^ c_dp[p]) * ds_rows, ds_rows), ds_rows)
        c_s[at, c_h[p] * units : (c_h[p] + 1) * units] = c_ref[i, :, :units]
        o_s[at, c_h[p] * width : (c_h[p] + 1) * width] = c_ref[i, :, units:]
    for off in range(n_h):
        mix_s[:, off * width : (off + 1) * width] = mixed[off][:rw, :]
        tail = mixed[off][rw : rw + 16, :].astype(F32)
        bias_s[off] = jnp.concatenate([tail[i : i + 1, :] for i in range(units // width)], axis=1)

    acc_s[...] = dot(mix_s[...], o_s[...], 1, 1)

    def chunk_one(i, carry):
        at = pl.ds(pl.multiple_of(i * CH, CH), CH)
        attn_out = acc_s[at, :] + row(2)
        v = post_in[at, :] + attn_out
        centered = v - jnp.mean(v, axis=-1, keepdims=True)
        rstd = lax.rsqrt(jnp.mean(centered * centered, axis=-1, keepdims=True) + EPS_NORM)
        xhat = centered * rstd
        pn = xhat * row(0) + row(1)
        xh_s[at, :] = xhat
        rs_s[at, :] = jnp.broadcast_to(rstd, (CH, 128))
        pn_s[at, :] = pn
        xb_s[at, :] = pn.astype(BF)
        dual_out[at, :] = dual_in[at, :] + attn_out
        return carry

    lax.fori_loop(0, rw // CH, chunk_one, 0)
    xt_s[...] = xb_s[...].T
    for oh in range(n_h):
        part = slice(oh * units, (oh + 1) * units)
        pre = dot(xb_s[...], e_s[:, part], 1, 0) + bias_s[oh]
        hid_s[:, part] = jnp.maximum(pre, 0.0).astype(BF)
    acc_s[...] = dot(hid_s[...], c_s[...], 1, 1)

    def chunk_two(i, carry):
        gain_sum, shift_sum, ffn_sum = carry
        at = pl.ds(pl.multiple_of(i * CH, CH), CH)
        ffn_out = acc_s[at, :] + row(5)
        v = pn_s[at, :] + ffn_out
        centered = v - jnp.mean(v, axis=-1, keepdims=True)
        rstd = lax.rsqrt(jnp.mean(centered * centered, axis=-1, keepdims=True) + EPS_NORM)
        xhat = centered * rstd
        post_out[at, :] = xhat * row(3) + row(4)
        dual_out[at, :] = dual_out[at, :] + ffn_out
        cot = post_cot[at, :]
        gmid2 = norm_back(cot, xhat, rstd, row(3))
        gffn = gmid2 + dual_cot[at, :]
        gmid2_s[at, :] = gmid2
        gb_s[at, :] = gffn.astype(BF)
        return gain_sum + fold(cot * xhat), shift_sum + fold(cot), ffn_sum + fold(gffn)

    zero = jnp.zeros((8, D), F32)
    gain2, shift2, ffn_sum = lax.fori_loop(0, rw // CH, chunk_two, (zero, zero, zero))
    gt_s[...] = gb_s[...].T
    for oh in range(n_h):
        part = slice(oh * units, (oh + 1) * units)
        ge, gc = (ge_keep, gc_keep) if oh % 2 == 0 else (ge_send, gc_send)
        gh = dot(gb_s[...], c_s[:, part], 1, 0)
        gp = jnp.where(hid_s[:, part] > 0, gh, 0.0).astype(BF)
        gp_s[:, part] = gp
        ffb_s[oh] = jnp.sum(gp.astype(F32), axis=0, keepdims=True)
        grad_c = dot(gt_s[...], hid_s[:, part], 1, 0).astype(BF)
        grad_e = dot(xt_s[...], gp, 1, 0).astype(BF)
        e_at, c_at = place(es_steps, "head", oh - oh % 2), place(cs_steps, "head", oh - oh % 2)
        for b in range(n_dp):
            ge[place(es_steps, "dp", b ^ g) + e_at] = grad_e[b * ds_rows : (b + 1) * ds_rows]
            gc[place(cs_steps, "dp", b ^ g) + c_at, :, :units] = grad_c[b * ds_rows : (b + 1) * ds_rows]
    acc_s[...] = dot(gp_s[...], e_s[...], 1, 1)

    def chunk_three(i, carry):
        gain_sum, shift_sum, attn_sum = carry
        at = pl.ds(pl.multiple_of(i * CH, CH), CH)
        grad = gmid2_s[at, :] + acc_s[at, :]
        xhat = xh_s[at, :]
        gmid1 = norm_back(grad, xhat, rs_s[at, :1], row(0))
        gmid1_ref[at, :] = gmid1
        gattn = gmid1 + dual_cot[at, :]
        gb_s[at, :] = gattn.astype(BF)
        return gain_sum + fold(grad * xhat), shift_sum + fold(grad), attn_sum + fold(gattn)

    gain1, shift1, attn_sum = lax.fori_loop(0, rw // CH, chunk_three, (zero, zero, zero))
    grad_mixed = dot(gb_s[...], o_s[...], 1, 0).astype(BF)
    for off in range(n_h):
        gm[off][...] = grad_mixed[:, off * width : (off + 1) * width]
    grad_o = dot(gb_s[...].T, mix_s[...], 1, 0).astype(BF)
    for oh in range(n_h):
        gc = gc_keep if oh % 2 == 0 else gc_send
        for b in range(n_dp):
            gc[place(cs_steps, "dp", b ^ g) + place(cs_steps, "head", oh - oh % 2), :, units:] = grad_o[
                b * ds_rows : (b + 1) * ds_rows, oh * width : (oh + 1) * width
            ]
    for i, part in enumerate((gain1, shift1, attn_sum, gain2, shift2, ffn_sum)):
        line = jnp.sum(part, axis=0, keepdims=True)
        for j in range(D // 128):
            small_ref[4 * i + j : 4 * i + j + 1, :] = line[:, j * 128 : (j + 1) * 128]
    for oh in range(n_h):
        first = 24 + (h ^ oh) * (units // 128)
        for j in range(units // 128):
            small_ref[pl.ds(first + j, 1), :] = ffb_s[oh, :, j * 128 : (j + 1) * 128]


def first_key_blocks(start, lo_ref):
    total = 0
    for qb in range(start.shape[1] // TQ):
        lo = (jnp.min(start[:, qb * TQ : (qb + 1) * TQ]) * (1.0 / TK)).astype(jnp.int32)
        lo_ref[qb] = lo
        total = total + (qb + 1 - lo)
    return total


def next_pair(qb, kb, lo_ref, last):
    done = kb >= qb
    following = jnp.minimum(qb + 1, last)
    return jnp.where(done, following, qb), jnp.where(done, lo_ref[following], kb + 1)


def attend_back_kernel(lh, n_h, idx_ref, seg_ref, q_ref, k_ref, v_ref, lse_near, lse_far, small_in, *refs):
    gm, pieces = refs[:n_h], refs[n_h : 2 * n_h]
    gqkv_ref, small_ref, lo_s, q2_s, do2_s, delta_s, lse_s, start_s, kt_s, dk_s, dv_s, dq_s = refs[
        2 * n_h : 2 * n_h + 12
    ]
    slots = (refs[2 * n_h + 12 : 2 * n_h + 14], refs[2 * n_h + 14 :])
    h = idx_ref[1]
    width = lh * HD
    rw = gm[0].shape[0]
    n_rows = q_ref.shape[0]
    n_q = n_rows // TQ
    cols = lh * TQ
    factor = SCORE_SCALE * LOG2E
    starts = document_starts(seg_ref[...])
    n_pairs = first_key_blocks(starts, lo_s)
    starts = starts.astype(jnp.int32)
    for qb in range(n_q):
        start_s[qb] = jnp.concatenate([starts[:, qb * TQ : (qb + 1) * TQ]] * lh, axis=1)
        q2_s[qb] = lane_mask_stack(q_ref[qb * TQ : (qb + 1) * TQ, :], lh)
    for off in range(n_h):
        lse_part, n = (lse_near, off) if off < n_h // 2 else (lse_far, off - n_h // 2)
        for i in range(rw // TQ):
            qb = (h ^ off) * (rw // TQ) + i
            do = gm[off][i * TQ : (i + 1) * TQ, :]
            do2_s[qb] = lane_mask_stack(do, lh)
            prod = (do.astype(F32) * pieces[off][i * TQ : (i + 1) * TQ, :].astype(F32)).T
            delta_s[qb] = jnp.concatenate(
                [jnp.sum(prod[l * HD : (l + 1) * HD, :], axis=0, keepdims=True) for l in range(lh)], axis=1
            )
            lse_s[qb] = lse_part[n * (rw // TQ) + i][:1]
    kt_s[...] = k_ref[...].T
    dk_s[...] = jnp.zeros_like(dk_s)
    dv_s[...] = jnp.zeros_like(dv_s)
    dq_s[...] = jnp.zeros_like(dq_s)
    column = lax.broadcasted_iota(jnp.int32, (1, cols), 1) % TQ

    def products(qb, kb, slot):
        keys = pl.ds(pl.multiple_of(kb * TK, TK), TK)
        slot[0][...] = dot(k_ref[keys, :], q2_s[qb], 1, 1)
        slot[1][...] = dot(v_ref[keys, :], do2_s[qb], 1, 1)

    def gradients(qb, kb, slot, least):
        c0 = pl.multiple_of(kb * TK, TK)
        keys = pl.ds(c0, TK)
        key = lax.broadcasted_iota(jnp.int32, (TK, cols), 0)
        ok = (key >= start_s[qb] - c0 + least) & (key <= column + (qb * TQ - c0))
        p = jnp.exp2(jnp.where(ok, slot[0][...], NEG_LARGE) * factor - lse_s[qb])
        grad = (p * (slot[1][...] - delta_s[qb])).astype(BF)
        dv_s[keys, :] += dot(p.astype(BF), do2_s[qb], 1, 0)
        dk_s[keys, :] += dot(grad, q2_s[qb], 1, 0)
        dq_s[qb] += dot(kt_s[:, keys], grad, 1, 0)

    products(0, 0, slots[0])

    def two_pairs(i, carry):
        qb, kb = carry
        one = next_pair(qb, kb, lo_s, n_q - 1)
        products(*one, slots[1])
        gradients(qb, kb, slots[0], 0)
        two = next_pair(*one, lo_s, n_q - 1)
        products(*two, slots[0])
        gradients(*one, slots[1], jnp.where(2 * i + 1 < n_pairs, 0, 2 * n_rows))
        return two

    lax.fori_loop(0, (n_pairs + 1) // 2, two_pairs, (jnp.int32(0), jnp.int32(0)))
    q_sum = jnp.zeros((1, width), F32)
    for qb in range(n_q):
        dq = (head_rows_merge(dq_s[qb], lh) * SCORE_SCALE).T.astype(BF)
        gqkv_ref[qb * TQ : (qb + 1) * TQ, :width] = dq
        q_sum = q_sum + jnp.sum(dq.astype(F32), axis=0, keepdims=True)
    gqkv_ref[:, width : 2 * width] = (dk_s[...] * SCORE_SCALE).astype(BF)
    dv = dv_s[...].astype(BF)
    gqkv_ref[:, 2 * width :] = dv
    v_sum = jnp.sum(dv.astype(F32), axis=0, keepdims=True)
    small_ref[:40, :] = small_in[...]
    small_ref[40:, :] = jnp.zeros((8, 128), F32)
    for l in range(lh):
        small_ref[pl.ds(40 + h * lh + l, 1), :] = jnp.concatenate(
            [q_sum[:, l * HD : (l + 1) * HD], v_sum[:, l * HD : (l + 1) * HD]], axis=1
        )


def rows_back_kernel(n_h, idx_ref, gqkv_ref, wg_ref, *outs):
    h = idx_ref[1]
    rw = outs[0].shape[0]
    for off in range(n_h):
        at = pl.ds(pl.multiple_of((h ^ off) * rw, rw), rw)
        outs[off][...] = dot(gqkv_ref[at, :], wg_ref[...], 1, 1).astype(BF)


def attend_grad_kernel(lh, n_dp, n_h, steps, idx_ref, gqkv_ref, *refs):
    rows = refs[:n_h]
    out_ref, acc_s = refs[n_h:]
    g, h = idx_ref[0], idx_ref[1]
    rw = rows[0].shape[0]
    ds_rows = D // n_dp
    width = lh * HD
    for off in range(n_h):
        at = pl.ds(pl.multiple_of((h ^ off) * rw, rw), rw)
        part = dot(rows[off][...], gqkv_ref[at, :], 0, 0)
        acc_s[...] = part if off == 0 else acc_s[...] + part
    full = acc_s[...]
    full = jnp.concatenate(
        [full[:, kind * width + l * HD : kind * width + (l + 1) * HD] for l in range(lh) for kind in range(3)],
        axis=1,
    ).astype(BF)
    for b in range(n_dp):
        out_ref[place(steps, "dp", b ^ g)] = full[b * ds_rows : (b + 1) * ds_rows]


def total_of_pair(keep_ref, got_ref):
    return keep_ref[0].astype(F32) + got_ref[0].astype(F32)


def squares_kernel(*refs):
    out_ref = refs[-1]
    acc = jnp.zeros((8, 128), F32)
    for i in range(0, len(refs) - 1, 2):
        v = total_of_pair(refs[i], refs[i + 1])
        v = fold(v * v)
        if v.shape[1] % 128:
            v = jnp.concatenate([v, jnp.zeros((8, 128 - v.shape[1] % 128), F32)], axis=1)
        for j in range(v.shape[1] // 128):
            acc = acc + v[:, j * 128 : (j + 1) * 128]
    out_ref[...] = acc


def adam_kernel(units, clip_ref, sq_ref, sq_got, small_ref, *refs):
    share_bias, norm_grads = refs[6:8]
    params, momenta, variances = refs[8:14], refs[14:20], refs[20:26]
    norm_ref, clipped_ref = refs[26:28]
    outs = list(refs[28:])
    small = small_ref[...]
    squares = jnp.sum(sq_ref[...] + sq_got[...]) + jnp.sum(small * small)
    norm = jnp.sqrt(jnp.full((8, 128), squares))
    norm_ref[...] = norm
    limit = clip_ref[0]
    factor = (limit / jnp.maximum(norm, limit))[:1, :1]
    shares = total_of_pair(refs[4], refs[5])
    grads = (
        total_of_pair(refs[0], refs[1]),
        shares[:, units:],
        total_of_pair(refs[2], refs[3]),
        shares[:, :units],
        share_bias[...],
        norm_grads[...],
    )
    for w, m, va, grad, rate in zip(params, momenta, variances, grads, RATES):
        clipped = factor * grad
        momentum_new = BETA * m[...] + (1.0 - BETA) * clipped
        variance_new = BETA * va[...] + (1.0 - BETA) * clipped * clipped
        step = momentum_new / BIAS_CORRECTION / (jnp.sqrt(variance_new / BIAS_CORRECTION) + ADAM_EPS)
        master_new = w[...] - rate * (step + DECAY * w[...])
        outs.pop(0)[...] = momentum_new
        outs.pop(0)[...] = variance_new
        outs.pop(0)[...] = master_new
        if len(outs) > 2:
            outs.pop(0)[...] = master_new.astype(BF)
    clipped_ref[...] = factor * norm_grads[...]


def call(body, outs, scratch, n_smem, args, limit, us):
    return pl.pallas_call(
        body,
        out_shape=outs,
        in_specs=[SMEM] * n_smem + [VMEM] * (len(args) - n_smem),
        out_specs=jax.tree.map(lambda _: VMEM, outs),
        scratch_shapes=scratch,
        compiler_params=pltpu.CompilerParams(vmem_limit_bytes=limit << 20),
        cost_estimate=pl.CostEstimate(flops=us * FLOPS_PER_US, bytes_accessed=1 << 20, transcendentals=0),
    )(*args)


def sds(shape, dtype):
    return jax.ShapeDtypeStruct(shape, dtype)


def per_device(
    post_in,
    dual_in,
    segment_ids,
    post_cot,
    dual_cot,
    attend_weight,
    output_weight,
    expand_weight,
    contract_weight,
    head_bias,
    norm_params,
    attend_momentum,
    output_momentum,
    expand_momentum,
    contract_momentum,
    bias_momentum,
    norm_momentum,
    attend_variance,
    output_variance,
    expand_variance,
    contract_variance,
    bias_variance,
    norm_variance,
    clip_limit,
):
    n_dp, n_h = lax.axis_size("dp"), lax.axis_size("head")
    g, h = lax.axis_index("dp"), lax.axis_index("head")
    idx = jnp.stack([g, h]).astype(jnp.int32)
    rw = post_in.shape[0]
    n_rows = rw * n_h
    lh = HEADS // n_h
    width = lh * HD
    ds_rows = attend_weight.shape[0]
    a_cols = attend_weight.shape[1]
    units = expand_weight.shape[1]
    shares = head_bias.shape[1]
    dp_bits, h_bits = bits_of(n_dp), bits_of(n_h)
    a_steps = [("dp", b) for b in dp_bits]
    dp_steps, h_steps = [("dp", b) for b in dp_bits], [("head", b) for b in h_bits]
    e_steps = dp_steps + h_steps
    c_steps = dp_steps[:-1] + h_steps[:-1] + dp_steps[-1:] + h_steps[-1:]
    es_steps = dp_steps[:-1] + h_steps[:-1] + dp_steps[-1:] + h_steps[-1:]
    cs_steps = dp_steps[:1] + h_steps[:-1] + dp_steps[-1:] + dp_steps[1:-1] + h_steps[-1:]
    g_steps = dp_steps[:1] + dp_steps[-1:] + dp_steps[1:-1]

    bias_block = jnp.pad(
        head_bias.astype(BF).reshape(1, lh * shares), ((0, 15), (0, a_cols - lh * shares))
    )
    a_msg = jnp.concatenate([attend_weight.astype(BF), bias_block], axis=0)
    m_msg = jnp.concatenate(
        [expand_weight.astype(BF), contract_weight.T.astype(BF), output_weight.T.astype(BF)], axis=1
    )
    rows_own = after(post_in, a_msg).astype(BF)

    n_d, n_s = len(dp_bits), len(e_steps)
    a_in, a_got = [a_msg[None]], []
    for i, step in enumerate(a_steps):
        a_got.append(swap(a_in[i], step))
        if i < n_d - 1:
            a_in.append(jnp.concatenate([a_in[i], a_got[i]], axis=0))
    m_in, m_got = m_msg[None], None
    for i in range(n_d - 1):
        if i > 0:
            m_in = jnp.concatenate([m_in, after(m_got, a_got[i - 1])], axis=0)
        m_got = swap(m_in, e_steps[i])
    e_in, c_in = m_in[..., :units], m_in[..., units:]
    e_got, c_got = m_got[..., :units], m_got[..., units:]

    def exchange(i, *ready):
        nonlocal e_in, c_in, e_got, c_got
        e_in = jnp.concatenate([e_in, after(e_got, *ready)], axis=0)
        c_in = jnp.concatenate([c_in, after(c_got, *ready)], axis=0)
        e_got, c_got = swap(e_in, e_steps[i]), swap(c_in, c_steps[i])

    rows = {0: rows_own}
    for bit in h_bits:
        for off in list(rows):
            rows[off ^ bit] = swap(rows[off], ("head", bit))
    rows = [rows[off] for off in range(n_h)]
    exchange(n_d - 1)
    n_q = n_rows // TQ
    cols = lh * TQ
    q, k, v, vt, wg, inner = call(
        functools.partial(qkv_kernel, lh, n_dp, n_h, offsets(a_steps, "dp")),
        [sds((n_rows, width), BF)] * 3
        + [sds((width + 16, n_rows), BF), sds((D, 3 * width), BF), sds((16, width), BF)],
        [pltpu.VMEM((D, a_cols), BF), pltpu.VMEM((n_dp, lh * shares), F32)],
        1,
        [idx, after(a_in[-1], e_in, c_in), a_got[-1]] + rows,
        24,
        4,
    )

    def attend(offs, q):
        out = call(
            functools.partial(attend_kernel, lh, offs),
            [sds((rw + 16, width), BF)] * len(offs) + [sds((n_q // 2, 8, cols), F32)],
            [
                pltpu.VMEM((KEY_BLOCKS, TK, cols), F32),
                pltpu.VMEM((width + 16, cols), F32),
                pltpu.VMEM((1, n_rows), F32),
            ],
            1,
            [idx, segment_ids, q, k, vt, inner],
            24,
            1,
        )
        return out[:-1], out[-1]

    exchange(n_d, q)
    far, lse_far = attend(range(n_h // 2, n_h), after(q, e_in, c_in))
    early = n_d + 1 == n_s - 1
    crossed = [swap(e_in, e_steps[-1]), swap(c_in, c_steps[-1])] if early else []
    near, lse_near = attend(range(n_h // 2), after(q, far[0], *crossed))
    for i in range(n_d + 1, n_s - 1):
        exchange(i, near[0])
    pieces = list(near) + list(far)
    mixed = [pieces[0]] + [
        lax.ppermute(pieces[off], "head", [(i, i ^ off) for i in range(n_h)]) for off in range(1, n_h)
    ]
    arrived = [near[0]] + mixed[n_h // 2 :]
    if not early:
        crossed = [swap(e_in, e_steps[-1]), swap(c_in, c_steps[-1])]
    e_got, c_got = after(e_got, *arrived), after(c_got, *arrived)
    e_parts = [e_in, e_got, crossed[0], swap(e_got, e_steps[-1])]
    c_parts = [c_in, c_got, crossed[1], swap(c_got, c_steps[-1])]

    half = n_dp * n_h // 2
    middle_out = call(
        functools.partial(middle_kernel, lh, n_dp, n_h, e_steps, c_steps, es_steps, cs_steps),
        [sds((rw, D), F32)] * 3
        + [sds((rw, width), BF)] * n_h
        + [sds((half, ds_rows, units), BF)] * 2
        + [sds((half, ds_rows, units + width), BF)] * 2
        + [sds((40, 128), F32)],
        [
            pltpu.VMEM((D, n_h * units), BF),
            pltpu.VMEM((D, n_h * units), BF),
            pltpu.VMEM((D, n_h * width), BF),
            pltpu.VMEM((rw, n_h * width), BF),
            pltpu.VMEM((n_h, 1, units), F32),
            pltpu.VMEM((rw, n_h * units), BF),
            pltpu.VMEM((rw, D), F32),
            pltpu.VMEM((rw, D), F32),
            pltpu.VMEM((rw, 128), F32),
            pltpu.VMEM((rw, D), F32),
            pltpu.VMEM((rw, D), BF),
            pltpu.VMEM((D, rw), BF),
            pltpu.VMEM((rw, D), BF),
            pltpu.VMEM((rw, D), F32),
            pltpu.VMEM((n_h, 1, units), F32),
            pltpu.VMEM((rw, n_h * units), BF),
            pltpu.VMEM((D, rw), BF),
        ],
        1,
        [idx, norm_params] + mixed + e_parts + c_parts + [post_in, dual_in, post_cot, dual_cot],
        34,
        20,
    )
    post_out, dual_out, grad_mid1 = middle_out[:3]
    gm = middle_out[3 : 3 + n_h]
    ge_keep, ge_send, gc_keep, gc_send, small_mid = middle_out[3 + n_h :]
    gm = [gm[0]] + [
        lax.ppermute(gm[off], "head", [(i, i ^ off) for i in range(n_h)]) for off in range(1, n_h)
    ]
    ge, gc = Scatter(ge_keep, ge_send, es_steps), Scatter(gc_keep, gc_send, cs_steps)
    gm[0] = after(gm[0], *ge.advance(), *gc.advance())
    gqkv, small = call(
        functools.partial(attend_back_kernel, lh, n_h),
        [sds((n_rows, 3 * width), BF), sds((48, 128), F32)],
        [
            pltpu.SMEM((n_q,), jnp.int32),
            pltpu.VMEM((n_q, cols, width), BF),
            pltpu.VMEM((n_q, cols, width), BF),
            pltpu.VMEM((n_q, 1, cols), F32),
            pltpu.VMEM((n_q, 1, cols), F32),
            pltpu.VMEM((n_q, 1, cols), jnp.int32),
            pltpu.VMEM((width, n_rows), BF),
            pltpu.VMEM((n_rows, width), F32),
            pltpu.VMEM((n_rows, width), F32),
            pltpu.VMEM((n_q, width, cols), F32),
        ]
        + [pltpu.VMEM((TK, cols), F32)] * 4,
        1,
        [idx, segment_ids, q, k, v, lse_near, lse_far, small_mid] + gm + pieces,
        32,
        15,
    )
    sent = ge.advance(gqkv) + gc.advance(gqkv)
    total = Total(small, dp_steps + h_steps)
    sent = total.advance(*sent)
    ga = call(
        functools.partial(attend_grad_kernel, lh, n_dp, n_h, g_steps),
        sds((n_dp, ds_rows, a_cols), BF),
        [pltpu.VMEM((D, 3 * width), F32)],
        1,
        [idx, after(gqkv, *sent)] + rows,
        24,
        2,
    )
    ga = Scatter(ga[: n_dp // 2], ga[n_dp // 2 :], g_steps)
    back = call(
        functools.partial(rows_back_kernel, n_h),
        [sds((rw, D), BF)] * n_h,
        [],
        1,
        [idx, after(gqkv, ga.send), wg],
        24,
        2,
    )
    sent = (back[0],)
    back = RowSums(back, sorted(h_bits, reverse=True))
    for i in range(n_s - 3):
        sent = ge.advance(*sent)
        sent = gc.advance(*sent)
        if i == 0:
            sent = total.advance(*sent)
            for _ in range(len(h_bits) - 1):
                sent = back.advance(*sent)
        if i < n_d - 1:
            sent = ga.advance(*sent)
    sent = total.advance(*sent)
    post_grad = back.finish(grad_mid1, *sent)
    sent = (post_grad,)
    pairs = [ga.keep, ga.got, ge.keep, ge.got, gc.keep, gc.got]
    squares = call(squares_kernel, sds((8, 128), F32), [], 0, pairs, 16, 1)
    squares = Total(squares, h_steps[:-1] + dp_steps[::-1] + h_steps[-1:])
    for _ in e_steps[:-1]:
        total.advance(*squares.advance(*sent))
    small = total.result()
    norm_grads = small[:24].reshape(6, D)
    bias_full = jnp.concatenate(
        [
            lax.dynamic_slice_in_dim(small, 40 + h * lh, lh, 0),
            lax.dynamic_slice_in_dim(small, 24 + h * 2 * lh, 2 * lh, 0).reshape(lh, 256),
        ],
        axis=1,
    )
    share_bias = lax.dynamic_slice_in_dim(bias_full, g * shares, shares, 1)
    flip = lambda arrays: [a.T if i in (1, 3) else a for i, a in enumerate(arrays)]
    params = flip([attend_weight, output_weight, expand_weight, contract_weight, head_bias, norm_params])
    momenta = flip(
        [attend_momentum, output_momentum, expand_momentum, contract_momentum, bias_momentum, norm_momentum]
    )
    variances = flip(
        [attend_variance, output_variance, expand_variance, contract_variance, bias_variance, norm_variance]
    )
    shapes = [sds((8, 128), F32), sds((6, D), F32)]
    for i, w in enumerate(params):
        shapes += [sds(w.shape, F32)] * 3 + ([sds(w.shape, BF)] if i < 5 else [])
    norm, norm_clipped, *results = call(
        functools.partial(adam_kernel, units),
        shapes,
        [],
        1,
        [clip_limit, squares.value, squares.got, small] + pairs + [share_bias, norm_grads] + params + momenta + variances,
        24,
        2,
    )
    results = [a.T if i // 4 in (1, 3) else a for i, a in enumerate(results)]
    return (post_out, dual_out, post_grad, norm[0, :1], *results, norm_clipped)


def solution(mesh):
    rows = P(("dp", "head"), None)
    tall, flat, rep = P("dp", "head"), P("head", "dp"), P()
    weights = (tall, flat, tall, flat, flat, rep)
    in_specs = (rows, rows, P("dp", None), rows, rows) + weights * 3 + (rep,)
    out_specs = (rows, rows, rows, rep)
    for spec in (tall, flat, tall, flat, flat):
        out_specs += (spec,) * 4
    out_specs += (rep,) * 4
    return jax.shard_map(per_device, mesh=mesh, in_specs=in_specs, out_specs=out_specs, check_vma=False)
```

```python
import functools

import jax
import jax.numpy as jnp
from jax import lax
from jax.experimental import pallas as pl
from jax.experimental.pallas import tpu as pltpu
from jax.sharding import PartitionSpec as P

D = 512
HEADS = 8
HD = 64
TQ = 256
TK = 256
CH = 64

EPS_NORM = 1e-05
NEG_LARGE = -1e30
LOG2E = 1.4426950408889634
SCORE_SCALE = HD ** (-0.5)
RATES = (0.04, 0.12, 0.04, 0.04, 0.16, 0.3)
DECAY = 0.01
ADAM_EPS = 1e-08
BETA = 0.5
BIAS_CORRECTION = 0.875
BF = jnp.bfloat16
FLOPS_PER_US = 10**9
F32 = jnp.float32
VMEM = pl.BlockSpec(memory_space=pltpu.VMEM)
SMEM = pl.BlockSpec(memory_space=pltpu.SMEM)


def dot(a, b, ca, cb):
    return lax.dot_general(a, b, (((ca,), (cb,)), ((), ())), preferred_element_type=F32)


def bits_of(count):
    bits = []
    while count > 1:
        count //= 2
        bits.append(count)
    return bits


def swap(v, step):
    axis, bit = step
    count = lax.axis_size(axis)
    return lax.ppermute(v, axis, [(i, i ^ bit) for i in range(count)])


def offsets(steps, axis):
    offs = [0]
    for name, bit in steps:
        offs = offs + [o ^ (bit if name == axis else 0) for o in offs]
    return offs


def after(v, *ready):
    return lax.optimization_barrier((v, *ready))[0]


def place(steps, axis, off):
    pos = 0
    for k, (name, bit) in enumerate(steps):
        if name == axis:
            pos = pos + ((off // bit) % 2) * (1 << k)
    return pos


class Scatter:
    def __init__(self, keep, send, steps):
        self.keep, self.steps = keep, list(steps)
        self.got = swap(send, self.steps[-1])
        self.send = send

    def advance(self, *ready):
        self.keep, self.send = self.take(*ready)
        self.steps.pop()
        self.got = swap(self.send, self.steps[-1])
        return (self.send,)

    def take(self, *ready):
        half = self.keep.shape[0] // 2
        total = self.keep.astype(F32) + after(self.got, *ready).astype(F32)
        return total[:half].astype(BF), total[half:].astype(BF)


def swap_both(v, one, two):
    n_h = lax.axis_size("head")
    flip = sum(bit * (n_h if axis == "dp" else 1) for axis, bit in (one, two))
    return lax.ppermute(v, ("dp", "head"), [(i, i ^ flip) for i in range(n_h * lax.axis_size("dp"))])


def sum_groups(value, groups, ready):
    for i, group in enumerate(groups):
        got = [value] + [swap(value, step) for step in group]
        if len(group) == 2:
            got.append(swap_both(value, *group))
        if i == len(groups) - 1:
            return got
        if i == 1:
            got[1] = after(got[1], *ready)
        pairs = [a + b for a, b in zip(got[::2], got[1::2])]
        value = functools.reduce(lambda a, b: a + b, pairs)


class RowSums:
    def __init__(self, pieces, bits):
        self.parts, self.bits = {off: [piece] for off, piece in enumerate(pieces)}, list(bits)
        self.flights = []
        self.start()

    def start(self, *ready):
        bit = self.bits.pop()
        sends = []
        for off in [off for off in self.parts if off & bit]:
            parts = self.parts.pop(off)
            total = parts[0]
            if len(parts) > 1:
                total = functools.reduce(
                    lambda a, b: a + b, [parts[0].astype(F32)] + [after(p, *ready).astype(F32) for p in parts[1:]]
                ).astype(BF)
            self.parts[off ^ bit].append(swap(total, ("head", bit)))
            sends.append(total)
        return tuple(sends)

    def advance(self, *ready):
        return self.start(*ready) if self.bits else ()

    def finish(self, value, *ready):
        return functools.reduce(lambda a, b: a + b, [after(p, *ready).astype(F32) for p in self.parts[0]], value)


def lane_mask_stack(v, lh):
    if lh == 1:
        return v
    lane = lax.broadcasted_iota(jnp.int32, v.shape, 1)
    zero = jnp.zeros_like(v)
    return jnp.concatenate(
        [jnp.where((lane >= l * HD) & (lane < (l + 1) * HD), v, zero) for l in range(lh)], axis=0
    )


def head_rows_merge(vt, lh):
    return jnp.concatenate(
        [vt[l * HD : (l + 1) * HD, l * TQ : (l + 1) * TQ] for l in range(lh)], axis=0
    )


def qkv_kernel(lh, n_dp, n_h, dp_offs, idx_ref, w_own, w_got, *refs):
    rows = refs[:n_h]
    q_ref, k_ref, v_ref, vt_ref, wg_ref, inner_ref, w_s, b_s = refs[n_h:]
    g, h = idx_ref[0], idx_ref[1]
    width = lh * HD
    ds_rows = D // n_dp
    rw = rows[0].shape[0]
    shares = b_s.shape[1] // lh
    for p in range(n_dp):
        block = g ^ dp_offs[p]
        w_ref, p = (w_own, p) if p < n_dp // 2 else (w_got, p - n_dp // 2)
        w_s[pl.ds(pl.multiple_of(block * ds_rows, ds_rows), ds_rows), :] = w_ref[p, :ds_rows, :]
        b_s[pl.ds(block, 1), :] = w_ref[p, ds_rows : ds_rows + 16, : lh * shares][:1].astype(F32)
    wide = w_s[...].astype(F32)
    wg = jnp.concatenate(
        [
            wide[:, l * 3 * HD + kind * HD : l * 3 * HD + (kind + 1) * HD]
            for kind in range(3)
            for l in range(lh)
        ],
        axis=1,
    ).astype(BF)
    wg_ref[...] = wg
    per_head = [
        jnp.concatenate([b_s[b : b + 1, l * shares : (l + 1) * shares] for b in range(n_dp)], axis=1)
        for l in range(lh)
    ]
    q_bias = jnp.concatenate([r[:, :HD] for r in per_head], axis=1)
    v_bias = jnp.concatenate([r[:, HD : 2 * HD] for r in per_head], axis=1)
    inner = jnp.concatenate([r[:, 2 * HD :] for r in per_head], axis=1)
    inner_ref[...] = jnp.concatenate(
        [inner[:, i * width : (i + 1) * width] for i in range(inner.shape[1] // width)]
        + [jnp.zeros((16 - inner.shape[1] // width, width), F32)],
        axis=0,
    ).astype(BF)
    for off in range(n_h):
        base = pl.multiple_of((h ^ off) * rw, rw)
        qkv = dot(rows[off][...], wg_ref[...], 1, 0)
        q_ref[pl.ds(base, rw), :] = (qkv[:, :width] + q_bias).astype(BF)
        k_ref[pl.ds(base, rw), :] = qkv[:, width : 2 * width].astype(BF)
        v_ref[pl.ds(base, rw), :] = (qkv[:, 2 * width :] + v_bias).astype(BF)
    vt_ref[:width, :] = v_ref[...].T
    vt_ref[width:, :] = jnp.ones((16, v_ref.shape[0]), BF)


def attend_kernel(lh, offs, idx_ref, seg_ref, q_ref, k_ref, vt_ref, inner_ref, *refs):
    pieces = refs[: len(offs)]
    lse_ref, qb_s, lo_s, all_s, start_s, q2_s, acc_s, top_s, slot_a, slot_b = refs[len(offs) :]
    h = idx_ref[1]
    width = lh * HD
    rw = pieces[0].shape[0] - 16
    per_piece = rw // TQ
    n_t = len(offs) * per_piece
    factor = SCORE_SCALE * LOG2E
    cols = lh * TQ
    column = lax.broadcasted_iota(jnp.int32, (1, cols), 1) % TQ
    all_s[...] = document_starts(seg_ref[...])
    n_pairs = 0
    for t in range(n_t):
        qb = (h ^ offs[t // per_piece]) * per_piece + t % per_piece
        at = pl.ds(pl.multiple_of(qb * TQ, TQ), TQ)
        start = all_s[:, at]
        lo = (jnp.min(start) * (1.0 / TK)).astype(jnp.int32)
        qb_s[t] = qb * (TQ // TK) + (TQ // TK - 1)
        lo_s[t] = lo
        n_pairs = n_pairs + qb_s[t] + 1 - lo
        start_s[t] = jnp.concatenate([start.astype(jnp.int32)] * lh, axis=1)
        q2_s[t] = lane_mask_stack(q_ref[at, :], lh)
    acc_s[...] = jnp.zeros_like(acc_s)
    top_s[...] = jnp.full(top_s.shape, NEG_LARGE, F32)

    def scores(t, kb, slot):
        keys = pl.ds(pl.multiple_of(kb * TK, TK), TK)
        slot[...] = dot(k_ref[keys, :], q2_s[t], 1, 1)

    def mix(t, kb, slot, least):
        c0 = pl.multiple_of(kb * TK, TK)
        key = lax.broadcasted_iota(jnp.int32, (TK, cols), 0)
        first = (qb_s[t] + 1) * TK - TQ
        ok = (key >= start_s[t] - c0 + least) & (key <= column + (first - c0))
        s = jnp.where(ok, slot[...], NEG_LARGE)
        old = top_s[t]
        top = jnp.maximum(old, jnp.max(s, axis=0, keepdims=True))
        p = jnp.exp2((s - top) * factor).astype(BF)
        acc_s[t] = acc_s[t] * jnp.exp2((old - top) * factor) + dot(vt_ref[:, pl.ds(c0, TK)], p, 1, 0)
        top_s[t] = top

    def following(t, kb):
        done = kb >= qb_s[t]
        nt = jnp.minimum(t + 1, n_t - 1)
        return jnp.where(done, nt, t), jnp.where(done, lo_s[nt], kb + 1)

    def two_pairs(i, carry):
        one = following(*carry)
        scores(*one, slot_b)
        mix(*carry, slot_a, 0)
        two = following(*one)
        scores(*two, slot_a)
        mix(*one, slot_b, jnp.where(2 * i + 1 < n_pairs, 0, 4 * q_ref.shape[0]))
        return two

    scores(0, lo_s[0], slot_a)
    lax.fori_loop(0, (n_pairs + 1) // 2, two_pairs, (jnp.int32(0), lo_s[0]))
    for t in range(n_t):
        total = acc_s[t, width : width + 1, :]
        out_t = head_rows_merge(acc_s[t, :width, :] / total, lh)
        inside = (t % per_piece) * TQ
        pieces[t // per_piece][inside : inside + TQ, :] = out_t.T.astype(BF)
        lse_ref[t] = jnp.broadcast_to(top_s[t] * factor + jnp.log2(total), (8, cols))
    for piece in pieces:
        piece[rw:, :] = inner_ref[...]


def document_starts(segment):
    seg = segment.astype(F32)
    start = jnp.zeros(seg.shape, F32)
    for s in range(HEADS):
        count = jnp.sum(jnp.where(seg == float(s), 1.0, 0.0), axis=1, keepdims=True)
        start = start + jnp.where(seg > float(s), count, 0.0)
    return start


def norm_back(grad, xhat, rstd, gain):
    g = grad * gain
    return rstd * (
        g - jnp.mean(g, axis=-1, keepdims=True) - xhat * jnp.mean(g * xhat, axis=-1, keepdims=True)
    )


def fold(v):
    return jnp.sum(v.reshape(v.shape[0] // 8, 8, v.shape[1]), axis=0)


def middle_kernel(lh, n_dp, n_h, e_steps, c_steps, es_steps, cs_steps, idx_ref, norm_ref, *refs):
    width = lh * HD
    mixed = refs[:n_h]
    e_parts, c_parts = refs[n_h : n_h + 4], refs[n_h + 4 : n_h + 8]
    post_in, dual_in, post_cot, dual_cot = refs[n_h + 8 : n_h + 12]
    outs = refs[n_h + 12 :]
    post_out, dual_out, gmid1_ref = outs[:3]
    gm = outs[3 : 3 + n_h]
    ge_keep, ge_send, gc_keep, gc_send, small_ref = outs[3 + n_h : 8 + n_h]
    (e_s, c_s, o_s, mix_s, bias_s, hid_s, acc_s, xh_s, rs_s, pn_s, xb_s, xt_s, gb_s, gmid2_s, ffb_s, gp_s, gt_s) = outs[
        8 + n_h :
    ]
    g, h = idx_ref[0], idx_ref[1]
    rw = post_in.shape[0]
    ds_rows = D // n_dp
    units = hid_s.shape[1] // n_h
    row = lambda i: norm_ref[i : i + 1, :]

    e_dp, e_h = offsets(e_steps, "dp"), offsets(e_steps, "head")
    c_dp, c_h = offsets(c_steps, "dp"), offsets(c_steps, "head")
    quarter = n_dp * n_h // 4
    for p in range(n_dp * n_h):
        at = pl.ds(pl.multiple_of((g ^ e_dp[p]) * ds_rows, ds_rows), ds_rows)
        e_ref, c_ref, i = e_parts[p // quarter], c_parts[p // quarter], p % quarter
        e_s[at, e_h[p] * units : (e_h[p] + 1) * units] = e_ref[i]
        at = pl.ds(pl.multiple_of((g ^ c_dp[p]) * ds_rows, ds_rows), ds_rows)
        c_s[at, c_h[p] * units : (c_h[p] + 1) * units] = c_ref[i, :, :units]
        o_s[at, c_h[p] * width : (c_h[p] + 1) * width] = c_ref[i, :, units:]
    for off in range(n_h):
        mix_s[:, off * width : (off + 1) * width] = mixed[off][:rw, :]
        tail = mixed[off][rw : rw + 16, :].astype(F32)
        bias_s[off] = jnp.concatenate([tail[i : i + 1, :] for i in range(units // width)], axis=1)

    acc_s[...] = dot(mix_s[...], o_s[...], 1, 1)

    def chunk_one(i, carry):
        at = pl.ds(pl.multiple_of(i * CH, CH), CH)
        attn_out = acc_s[at, :] + row(2)
        v = post_in[at, :] + attn_out
        centered = v - jnp.mean(v, axis=-1, keepdims=True)
        rstd = lax.rsqrt(jnp.mean(centered * centered, axis=-1, keepdims=True) + EPS_NORM)
        xhat = centered * rstd
        pn = xhat * row(0) + row(1)
        xh_s[at, :] = xhat
        rs_s[at, :] = jnp.broadcast_to(rstd, (CH, 128))
        pn_s[at, :] = pn
        xb_s[at, :] = pn.astype(BF)
        dual_out[at, :] = dual_in[at, :] + attn_out
        return carry

    lax.fori_loop(0, rw // CH, chunk_one, 0)
    xt_s[...] = xb_s[...].T
    for oh in range(n_h):
        part = slice(oh * units, (oh + 1) * units)
        pre = dot(xb_s[...], e_s[:, part], 1, 0) + bias_s[oh]
        hid_s[:, part] = jnp.maximum(pre, 0.0).astype(BF)
    acc_s[...] = dot(hid_s[...], c_s[...], 1, 1)

    def chunk_two(i, carry):
        gain_sum, shift_sum, ffn_sum = carry
        at = pl.ds(pl.multiple_of(i * CH, CH), CH)
        ffn_out = acc_s[at, :] + row(5)
        v = pn_s[at, :] + ffn_out
        centered = v - jnp.mean(v, axis=-1, keepdims=True)
        rstd = lax.rsqrt(jnp.mean(centered * centered, axis=-1, keepdims=True) + EPS_NORM)
        xhat = centered * rstd
        post_out[at, :] = xhat * row(3) + row(4)
        dual_out[at, :] = dual_out[at, :] + ffn_out
        cot = post_cot[at, :]
        gmid2 = norm_back(cot, xhat, rstd, row(3))
        gffn = gmid2 + dual_cot[at, :]
        gmid2_s[at, :] = gmid2
        gb_s[at, :] = gffn.astype(BF)
        return gain_sum + fold(cot * xhat), shift_sum + fold(cot), ffn_sum + fold(gffn)

    zero = jnp.zeros((8, D), F32)
    gain2, shift2, ffn_sum = lax.fori_loop(0, rw // CH, chunk_two, (zero, zero, zero))
    gt_s[...] = gb_s[...].T
    for oh in range(n_h):
        part = slice(oh * units, (oh + 1) * units)
        ge, gc = (ge_keep, gc_keep) if oh % 2 == 0 else (ge_send, gc_send)
        gh = dot(gb_s[...], c_s[:, part], 1, 0)
        gp = jnp.where(hid_s[:, part] > 0, gh, 0.0).astype(BF)
        gp_s[:, part] = gp
        ffb_s[oh] = jnp.sum(gp.astype(F32), axis=0, keepdims=True)
        grad_c = dot(gt_s[...], hid_s[:, part], 1, 0).astype(BF)
        grad_e = dot(xt_s[...], gp, 1, 0).astype(BF)
        e_at, c_at = place(es_steps, "head", oh - oh % 2), place(cs_steps, "head", oh - oh % 2)
        for b in range(n_dp):
            ge[place(es_steps, "dp", b ^ g) + e_at] = grad_e[b * ds_rows : (b + 1) * ds_rows]
            gc[place(cs_steps, "dp", b ^ g) + c_at, :, :units] = grad_c[b * ds_rows : (b + 1) * ds_rows]
    acc_s[...] = dot(gp_s[...], e_s[...], 1, 1)

    def chunk_three(i, carry):
        gain_sum, shift_sum, attn_sum = carry
        at = pl.ds(pl.multiple_of(i * CH, CH), CH)
        grad = gmid2_s[at, :] + acc_s[at, :]
        xhat = xh_s[at, :]
        gmid1 = norm_back(grad, xhat, rs_s[at, :1], row(0))
        gmid1_ref[at, :] = gmid1
        gattn = gmid1 + dual_cot[at, :]
        gb_s[at, :] = gattn.astype(BF)
        return gain_sum + fold(grad * xhat), shift_sum + fold(grad), attn_sum + fold(gattn)

    gain1, shift1, attn_sum = lax.fori_loop(0, rw // CH, chunk_three, (zero, zero, zero))
    grad_mixed = dot(gb_s[...], o_s[...], 1, 0).astype(BF)
    for off in range(n_h):
        gm[off][...] = grad_mixed[:, off * width : (off + 1) * width]
    grad_o = dot(gb_s[...].T, mix_s[...], 1, 0).astype(BF)
    for oh in range(n_h):
        gc = gc_keep if oh % 2 == 0 else gc_send
        for b in range(n_dp):
            gc[place(cs_steps, "dp", b ^ g) + place(cs_steps, "head", oh - oh % 2), :, units:] = grad_o[
                b * ds_rows : (b + 1) * ds_rows, oh * width : (oh + 1) * width
            ]
    for i, part in enumerate((gain1, shift1, attn_sum, gain2, shift2, ffn_sum)):
        line = jnp.sum(part, axis=0, keepdims=True)
        for j in range(D // 128):
            small_ref[4 * i + j : 4 * i + j + 1, :] = line[:, j * 128 : (j + 1) * 128]
    for oh in range(n_h):
        first = 24 + (h ^ oh) * (units // 128)
        for j in range(units // 128):
            small_ref[pl.ds(first + j, 1), :] = ffb_s[oh, :, j * 128 : (j + 1) * 128]


def first_key_blocks(start, lo_ref):
    total = 0
    for qb in range(start.shape[1] // TQ):
        lo = (jnp.min(start[:, qb * TQ : (qb + 1) * TQ]) * (1.0 / TK)).astype(jnp.int32)
        lo_ref[qb] = lo
        total = total + ((qb + 1) * (TQ // TK) - lo)
    return total


def next_pair(qb, kb, lo_ref, last):
    done = kb >= (qb + 1) * (TQ // TK) - 1
    following = jnp.minimum(qb + 1, last)
    return jnp.where(done, following, qb), jnp.where(done, lo_ref[following], kb + 1)


def attend_back_kernel(lh, n_h, idx_ref, seg_ref, q_ref, k_ref, v_ref, lse_near, lse_far, small_in, *refs):
    gm, pieces = refs[:n_h], refs[n_h : 2 * n_h]
    gqkv_ref, small_ref, lo_s, q2_s, do2_s, delta_s, lse_s, start_s, kt_s, dk_s, dv_s, dq_s = refs[
        2 * n_h : 2 * n_h + 12
    ]
    slots = (refs[2 * n_h + 12 : 2 * n_h + 14], refs[2 * n_h + 14 :])
    h = idx_ref[1]
    width = lh * HD
    rw = gm[0].shape[0]
    n_rows = q_ref.shape[0]
    n_q = n_rows // TQ
    cols = lh * TQ
    factor = SCORE_SCALE * LOG2E
    starts = document_starts(seg_ref[...])
    n_pairs = first_key_blocks(starts, lo_s)
    starts = starts.astype(jnp.int32)
    for qb in range(n_q):
        start_s[qb] = jnp.concatenate([starts[:, qb * TQ : (qb + 1) * TQ]] * lh, axis=1)
        q2_s[qb] = lane_mask_stack(q_ref[qb * TQ : (qb + 1) * TQ, :], lh)
    for off in range(n_h):
        lse_part, n = (lse_near, off) if off < n_h // 2 else (lse_far, off - n_h // 2)
        for i in range(rw // TQ):
            qb = (h ^ off) * (rw // TQ) + i
            do = gm[off][i * TQ : (i + 1) * TQ, :]
            do2_s[qb] = lane_mask_stack(do, lh)
            prod = (do.astype(F32) * pieces[off][i * TQ : (i + 1) * TQ, :].astype(F32)).T
            delta_s[qb] = jnp.concatenate(
                [jnp.sum(prod[l * HD : (l + 1) * HD, :], axis=0, keepdims=True) for l in range(lh)], axis=1
            )
            lse_s[qb] = lse_part[n * (rw // TQ) + i][:1]
    kt_s[...] = k_ref[...].T
    dk_s[...] = jnp.zeros_like(dk_s)
    dv_s[...] = jnp.zeros_like(dv_s)
    dq_s[...] = jnp.zeros_like(dq_s)
    column = lax.broadcasted_iota(jnp.int32, (1, cols), 1) % TQ

    def products(qb, kb, slot):
        keys = pl.ds(pl.multiple_of(kb * TK, TK), TK)
        slot[0][...] = dot(k_ref[keys, :], q2_s[qb], 1, 1)
        slot[1][...] = dot(v_ref[keys, :], do2_s[qb], 1, 1)

    def gradients(qb, kb, slot, least):
        c0 = pl.multiple_of(kb * TK, TK)
        keys = pl.ds(c0, TK)
        key = lax.broadcasted_iota(jnp.int32, (TK, cols), 0)
        ok = (key >= start_s[qb] - c0 + least) & (key <= column + (qb * TQ - c0))
        p = jnp.exp2(jnp.where(ok, slot[0][...], NEG_LARGE) * factor - lse_s[qb])
        grad = (p * (slot[1][...] - delta_s[qb])).astype(BF)
        dv_s[keys, :] += dot(p.astype(BF), do2_s[qb], 1, 0)
        dk_s[keys, :] += dot(grad, q2_s[qb], 1, 0)
        dq_s[qb] += dot(kt_s[:, keys], grad, 1, 0)

    products(0, 0, slots[0])

    def two_pairs(i, carry):
        qb, kb = carry
        one = next_pair(qb, kb, lo_s, n_q - 1)
        products(*one, slots[1])
        gradients(qb, kb, slots[0], 0)
        two = next_pair(*one, lo_s, n_q - 1)
        products(*two, slots[0])
        gradients(*one, slots[1], jnp.where(2 * i + 1 < n_pairs, 0, 2 * n_rows))
        return two

    lax.fori_loop(0, (n_pairs + 1) // 2, two_pairs, (jnp.int32(0), jnp.int32(0)))
    q_sum = jnp.zeros((1, width), F32)
    for qb in range(n_q):
        dq = (head_rows_merge(dq_s[qb], lh) * SCORE_SCALE).T.astype(BF)
        gqkv_ref[qb * TQ : (qb + 1) * TQ, :width] = dq
        q_sum = q_sum + jnp.sum(dq.astype(F32), axis=0, keepdims=True)
    gqkv_ref[:, width : 2 * width] = (dk_s[...] * SCORE_SCALE).astype(BF)
    dv = dv_s[...].astype(BF)
    gqkv_ref[:, 2 * width :] = dv
    v_sum = jnp.sum(dv.astype(F32), axis=0, keepdims=True)
    small_ref[:40, :] = small_in[...]
    small_ref[40:, :] = jnp.zeros((8, 128), F32)
    for l in range(lh):
        small_ref[pl.ds(40 + h * lh + l, 1), :] = jnp.concatenate(
            [q_sum[:, l * HD : (l + 1) * HD], v_sum[:, l * HD : (l + 1) * HD]], axis=1
        )


def rows_back_kernel(n_h, idx_ref, gqkv_ref, wg_ref, *outs):
    h = idx_ref[1]
    rw = outs[0].shape[0]
    for off in range(n_h):
        at = pl.ds(pl.multiple_of((h ^ off) * rw, rw), rw)
        outs[off][...] = dot(gqkv_ref[at, :], wg_ref[...], 1, 1).astype(BF)


def attend_grad_kernel(lh, n_dp, n_h, steps, idx_ref, gqkv_ref, *refs):
    rows = refs[:n_h]
    out_ref, acc_s = refs[n_h:]
    g, h = idx_ref[0], idx_ref[1]
    rw = rows[0].shape[0]
    ds_rows = D // n_dp
    width = lh * HD
    for off in range(n_h):
        at = pl.ds(pl.multiple_of((h ^ off) * rw, rw), rw)
        part = dot(rows[off][...], gqkv_ref[at, :], 0, 0)
        acc_s[...] = part if off == 0 else acc_s[...] + part
    full = acc_s[...]
    full = jnp.concatenate(
        [full[:, kind * width + l * HD : kind * width + (l + 1) * HD] for l in range(lh) for kind in range(3)],
        axis=1,
    ).astype(BF)
    for b in range(n_dp):
        out_ref[place(steps, "dp", b ^ g)] = full[b * ds_rows : (b + 1) * ds_rows]


def total_of_pair(keep_ref, got_ref):
    return keep_ref[0].astype(F32) + got_ref[0].astype(F32)


def squares_kernel(small_ref, *refs):
    out_ref = refs[-1]
    acc = jnp.zeros((8, 128), F32)
    for i in range(0, len(refs) - 1, 2):
        v = total_of_pair(refs[i], refs[i + 1])
        v = fold(v * v)
        if v.shape[1] % 128:
            v = jnp.concatenate([v, jnp.zeros((8, 128 - v.shape[1] % 128), F32)], axis=1)
        for j in range(v.shape[1] // 128):
            acc = acc + v[:, j * 128 : (j + 1) * 128]
    out_ref[:8, :] = acc
    out_ref[8:, :] = small_ref[...]


def adam_kernel(units, n_dp, lh, n_sums, idx_ref, clip_ref, *refs):
    sums, refs = [r[...] for r in refs[:n_sums]], refs[n_sums:]
    sums = [a + b for a, b in zip(sums[::2], sums[1::2])]
    sums = functools.reduce(lambda a, b: a + b, sums)
    params, momenta, variances = refs[6:12], refs[12:18], refs[18:24]
    norm_ref, clipped_ref = refs[24:26]
    outs, small_s = list(refs[26:-1]), refs[-1]
    g, h = idx_ref[0], idx_ref[1]
    small = sums[8:, :]
    small_s[...] = small
    squares = jnp.sum(sums[:8, :]) + jnp.sum(small * small)
    norm_grads = jnp.concatenate(
        [
            jnp.concatenate([small[4 * i + j : 4 * i + j + 1, :] for j in range(D // 128)], axis=1)
            for i in range(6)
        ],
        axis=0,
    )
    width = params[4].shape[1]
    bias_rows = []
    for l in range(lh):
        head = h * lh + l
        full = jnp.concatenate(
            [small_s[pl.ds(at, 1), :] for at in (40 + head, 24 + 2 * head, 25 + 2 * head)], axis=1
        )
        share = jnp.zeros((1, width), F32)
        for b in range(n_dp):
            share = share + jnp.where(g == b, full[:, b * width : (b + 1) * width], 0.0)
        bias_rows.append(share)
    share_bias = jnp.concatenate(bias_rows, axis=0)
    norm = jnp.sqrt(jnp.full((8, 128), squares))
    norm_ref[0] = jnp.max(norm)
    limit = clip_ref[0]
    factor = (limit / jnp.maximum(norm, limit))[:1, :1]
    shares = total_of_pair(refs[4], refs[5])
    grads = (
        total_of_pair(refs[0], refs[1]),
        shares[:, units:],
        total_of_pair(refs[2], refs[3]),
        shares[:, :units],
        share_bias,
        norm_grads,
    )
    for w, m, va, grad, rate in zip(params, momenta, variances, grads, RATES):
        clipped = factor * grad
        momentum_new = BETA * m[...] + (1.0 - BETA) * clipped
        variance_new = BETA * va[...] + (1.0 - BETA) * clipped * clipped
        step = momentum_new / BIAS_CORRECTION / (jnp.sqrt(variance_new / BIAS_CORRECTION) + ADAM_EPS)
        master_new = w[...] - rate * (step + DECAY * w[...])
        outs.pop(0)[...] = momentum_new
        outs.pop(0)[...] = variance_new
        outs.pop(0)[...] = master_new
        if len(outs) > 2:
            outs.pop(0)[...] = master_new.astype(BF)
    clipped_ref[...] = factor * norm_grads


def call(body, outs, scratch, n_smem, args, limit, us):
    return pl.pallas_call(
        body,
        out_shape=outs,
        in_specs=[SMEM] * n_smem + [VMEM] * (len(args) - n_smem),
        out_specs=jax.tree.map(lambda o: SMEM if o.shape == (1,) else VMEM, outs),
        scratch_shapes=scratch,
        compiler_params=pltpu.CompilerParams(vmem_limit_bytes=limit << 20),
        cost_estimate=pl.CostEstimate(flops=us * FLOPS_PER_US, bytes_accessed=1 << 20, transcendentals=0),
    )(*args)


def sds(shape, dtype):
    return jax.ShapeDtypeStruct(shape, dtype)


def per_device(
    post_in,
    dual_in,
    segment_ids,
    post_cot,
    dual_cot,
    attend_weight,
    output_weight,
    expand_weight,
    contract_weight,
    head_bias,
    norm_params,
    attend_momentum,
    output_momentum,
    expand_momentum,
    contract_momentum,
    bias_momentum,
    norm_momentum,
    attend_variance,
    output_variance,
    expand_variance,
    contract_variance,
    bias_variance,
    norm_variance,
    clip_limit,
):
    n_dp, n_h = lax.axis_size("dp"), lax.axis_size("head")
    g, h = lax.axis_index("dp"), lax.axis_index("head")
    idx = jnp.stack([g, h]).astype(jnp.int32)
    rw = post_in.shape[0]
    n_rows = rw * n_h
    lh = HEADS // n_h
    width = lh * HD
    ds_rows = attend_weight.shape[0]
    a_cols = attend_weight.shape[1]
    units = expand_weight.shape[1]
    shares = head_bias.shape[1]
    dp_bits, h_bits = bits_of(n_dp), bits_of(n_h)
    a_steps = [("dp", b) for b in dp_bits]
    dp_steps, h_steps = [("dp", b) for b in dp_bits], [("head", b) for b in h_bits]
    e_steps = dp_steps + h_steps
    c_steps = dp_steps[:-1] + h_steps[:-1] + dp_steps[-1:] + h_steps[-1:]
    es_steps = dp_steps[:-1] + h_steps[:-1] + dp_steps[-1:] + h_steps[-1:]
    cs_steps = dp_steps[:1] + h_steps[:-1] + dp_steps[-1:] + dp_steps[1:-1] + h_steps[-1:]
    g_steps = dp_steps[:1] + dp_steps[-1:] + dp_steps[1:-1]

    bias_block = jnp.pad(
        head_bias.astype(BF).reshape(1, lh * shares), ((0, 15), (0, a_cols - lh * shares))
    )
    a_msg = jnp.concatenate([attend_weight.astype(BF), bias_block], axis=0)
    m_msg = jnp.concatenate(
        [expand_weight.astype(BF), contract_weight.T.astype(BF), output_weight.T.astype(BF)], axis=1
    )
    rows_own = after(post_in, a_msg).astype(BF)

    n_d, n_s = len(dp_bits), len(e_steps)
    a_in, a_got = [a_msg[None]], []
    for i, step in enumerate(a_steps):
        a_got.append(swap(a_in[i], step))
        if i < n_d - 1:
            a_in.append(jnp.concatenate([a_in[i], a_got[i]], axis=0))
    m_in, m_got = m_msg[None], None
    for i in range(n_d - 1):
        if i > 0:
            m_in = jnp.concatenate([m_in, after(m_got, a_got[i - 1])], axis=0)
        m_got = swap(m_in, e_steps[i])
    e_in, c_in = m_in[..., :units], m_in[..., units:]
    e_got, c_got = m_got[..., :units], m_got[..., units:]

    def exchange(i, *ready):
        nonlocal e_in, c_in, e_got, c_got
        e_in = jnp.concatenate([e_in, after(e_got, *ready)], axis=0)
        c_in = jnp.concatenate([c_in, after(c_got, *ready)], axis=0)
        e_got, c_got = swap(e_in, e_steps[i]), swap(c_in, c_steps[i])

    rows = {0: rows_own}
    for bit in h_bits:
        for off in list(rows):
            rows[off ^ bit] = swap(rows[off], ("head", bit))
    rows = [rows[off] for off in range(n_h)]
    exchange(n_d - 1)
    n_q = n_rows // TQ
    cols = lh * TQ
    q, k, v, vt, wg, inner = call(
        functools.partial(qkv_kernel, lh, n_dp, n_h, offsets(a_steps, "dp")),
        [sds((n_rows, width), BF)] * 3
        + [sds((width + 16, n_rows), BF), sds((D, 3 * width), BF), sds((16, width), BF)],
        [pltpu.VMEM((D, a_cols), BF), pltpu.VMEM((n_dp, lh * shares), F32)],
        1,
        [idx, after(a_in[-1], e_in, c_in), a_got[-1]] + rows,
        24,
        4,
    )

    def attend(offs, q):
        out = call(
            functools.partial(attend_kernel, lh, offs),
            [sds((rw + 16, width), BF)] * len(offs) + [sds((n_q // 2, 8, cols), F32)],
            [
                pltpu.SMEM((n_q // 2,), jnp.int32),
                pltpu.SMEM((n_q // 2,), jnp.int32),
                pltpu.VMEM((1, n_rows), F32),
                pltpu.VMEM((n_q // 2, 1, cols), jnp.int32),
                pltpu.VMEM((n_q // 2, cols, width), BF),
                pltpu.VMEM((n_q // 2, width + 16, cols), F32),
                pltpu.VMEM((n_q // 2, 1, cols), F32),
                pltpu.VMEM((TK, cols), F32),
                pltpu.VMEM((TK, cols), F32),
            ],
            1,
            [idx, segment_ids, q, k, vt, inner],
            24,
            1,
        )
        return out[:-1], out[-1]

    exchange(n_d, q)
    far, lse_far = attend(range(n_h // 2, n_h), after(q, e_in, c_in))
    early = n_d + 1 == n_s - 1
    crossed = [swap(e_in, e_steps[-1]), swap(c_in, c_steps[-1])] if early else []
    near, lse_near = attend(range(n_h // 2), after(q, far[0], *crossed))
    for i in range(n_d + 1, n_s - 1):
        exchange(i, near[0])
    pieces = list(near) + list(far)
    mixed = [pieces[0]] + [
        lax.ppermute(pieces[off], "head", [(i, i ^ off) for i in range(n_h)]) for off in range(1, n_h)
    ]
    arrived = [near[0]] + mixed[n_h // 2 :]
    if not early:
        crossed = [swap(e_in, e_steps[-1]), swap(c_in, c_steps[-1])]
    e_got, c_got = after(e_got, *arrived), after(c_got, *arrived)
    e_parts = [e_in, e_got, crossed[0], swap(e_got, e_steps[-1])]
    c_parts = [c_in, c_got, crossed[1], swap(c_got, c_steps[-1])]

    half = n_dp * n_h // 2
    middle_out = call(
        functools.partial(middle_kernel, lh, n_dp, n_h, e_steps, c_steps, es_steps, cs_steps),
        [sds((rw, D), F32)] * 3
        + [sds((rw, width), BF)] * n_h
        + [sds((half, ds_rows, units), BF)] * 2
        + [sds((half, ds_rows, units + width), BF)] * 2
        + [sds((40, 128), F32)],
        [
            pltpu.VMEM((D, n_h * units), BF),
            pltpu.VMEM((D, n_h * units), BF),
            pltpu.VMEM((D, n_h * width), BF),
            pltpu.VMEM((rw, n_h * width), BF),
            pltpu.VMEM((n_h, 1, units), F32),
            pltpu.VMEM((rw, n_h * units), BF),
            pltpu.VMEM((rw, D), F32),
            pltpu.VMEM((rw, D), F32),
            pltpu.VMEM((rw, 128), F32),
            pltpu.VMEM((rw, D), F32),
            pltpu.VMEM((rw, D), BF),
            pltpu.VMEM((D, rw), BF),
            pltpu.VMEM((rw, D), BF),
            pltpu.VMEM((rw, D), F32),
            pltpu.VMEM((n_h, 1, units), F32),
            pltpu.VMEM((rw, n_h * units), BF),
            pltpu.VMEM((D, rw), BF),
        ],
        1,
        [idx, norm_params] + mixed + e_parts + c_parts + [post_in, dual_in, post_cot, dual_cot],
        34,
        20,
    )
    post_out, dual_out, grad_mid1 = middle_out[:3]
    gm = middle_out[3 : 3 + n_h]
    ge_keep, ge_send, gc_keep, gc_send, small_mid = middle_out[3 + n_h :]
    gm = [gm[0]] + [
        lax.ppermute(gm[off], "head", [(i, i ^ off) for i in range(n_h)]) for off in range(1, n_h)
    ]
    ge, gc = Scatter(ge_keep, ge_send, es_steps), Scatter(gc_keep, gc_send, cs_steps)
    gm[0] = after(gm[0], *ge.advance(), *gc.advance())
    gqkv, small = call(
        functools.partial(attend_back_kernel, lh, n_h),
        [sds((n_rows, 3 * width), BF), sds((48, 128), F32)],
        [
            pltpu.SMEM((n_q,), jnp.int32),
            pltpu.VMEM((n_q, cols, width), BF),
            pltpu.VMEM((n_q, cols, width), BF),
            pltpu.VMEM((n_q, 1, cols), F32),
            pltpu.VMEM((n_q, 1, cols), F32),
            pltpu.VMEM((n_q, 1, cols), jnp.int32),
            pltpu.VMEM((width, n_rows), BF),
            pltpu.VMEM((n_rows, width), F32),
            pltpu.VMEM((n_rows, width), F32),
            pltpu.VMEM((n_q, width, cols), F32),
        ]
        + [pltpu.VMEM((TK, cols), F32)] * 4,
        1,
        [idx, segment_ids, q, k, v, lse_near, lse_far, small_mid] + gm + pieces,
        32,
        15,
    )
    sent = ge.advance(gqkv) + gc.advance(gqkv)
    ga = call(
        functools.partial(attend_grad_kernel, lh, n_dp, n_h, g_steps),
        sds((n_dp, ds_rows, a_cols), BF),
        [pltpu.VMEM((D, 3 * width), F32)],
        1,
        [idx, after(gqkv, *sent)] + rows,
        24,
        2,
    )
    ga = Scatter(ga[: n_dp // 2], ga[n_dp // 2 :], g_steps)
    back = call(
        functools.partial(rows_back_kernel, n_h),
        [sds((rw, D), BF)] * n_h,
        [],
        1,
        [idx, after(gqkv, ga.send), wg],
        24,
        2,
    )
    sent = (back[0],)
    back = RowSums(back, sorted(h_bits, reverse=True))
    for i in range(n_s - 3):
        sent = ge.advance(*sent)
        sent = gc.advance(*sent)
        if i == 0:
            for _ in range(len(h_bits) - 1):
                sent = back.advance(*sent)
        if i < n_d - 1:
            sent = ga.advance(*sent)
    post_grad = back.finish(grad_mid1, *sent)
    pairs = [ga.keep, ga.got, ge.keep, ge.got, gc.keep, gc.got]
    squares = call(squares_kernel, sds((56, 128), F32), [], 0, [small] + pairs, 16, 1)
    order = h_steps[-1:] + [step for step in h_steps[:-1] + dp_steps[::-1]]
    groups = [order[:1]] + [order[i : i + 2] for i in range(1, len(order), 2)]
    sums = sum_groups(squares, groups, (post_grad,))
    flip = lambda arrays: [a.T if i in (1, 3) else a for i, a in enumerate(arrays)]
    params = flip([attend_weight, output_weight, expand_weight, contract_weight, head_bias, norm_params])
    momenta = flip(
        [attend_momentum, output_momentum, expand_momentum, contract_momentum, bias_momentum, norm_momentum]
    )
    variances = flip(
        [attend_variance, output_variance, expand_variance, contract_variance, bias_variance, norm_variance]
    )
    shapes = [sds((1,), F32), sds((6, D), F32)]
    for i, w in enumerate(params):
        shapes += [sds(w.shape, F32)] * 3 + ([sds(w.shape, BF)] if i < 5 else [])
    norm, norm_clipped, *results = call(
        functools.partial(adam_kernel, units, n_dp, lh, len(sums)),
        shapes,
        [pltpu.VMEM((48, 128), F32)],
        2,
        [idx, clip_limit] + sums + pairs + params + momenta + variances,
        24,
        2,
    )
    results = [a.T if i // 4 in (1, 3) else a for i, a in enumerate(results)]
    return (post_out, dual_out, post_grad, norm, *results, norm_clipped)


def solution(mesh):
    rows = P(("dp", "head"), None)
    tall, flat, rep = P("dp", "head"), P("head", "dp"), P()
    weights = (tall, flat, tall, flat, flat, rep)
    in_specs = (rows, rows, P("dp", None), rows, rows) + weights * 3 + (rep,)
    out_specs = (rows, rows, rows, rep)
    for spec in (tall, flat, tall, flat, flat):
        out_specs += (spec,) * 4
    out_specs += (rep,) * 4
    return jax.shard_map(per_device, mesh=mesh, in_specs=in_specs, out_specs=out_specs, check_vma=False)
```

```python
import functools

import jax
import jax.numpy as jnp
from jax import lax
from jax.experimental import pallas as pl
from jax.experimental.pallas import tpu as pltpu
from jax.sharding import PartitionSpec as P

D = 512
HEADS = 8
HD = 64
TQ = 256
TK = 256
CHUNK = 512

EPS_NORM = 1e-05
NEG_LARGE = -1e30
LOG2E = 1.4426950408889634
SCORE_SCALE = HD ** (-0.5)
RATES = (0.04, 0.12, 0.04, 0.04, 0.16, 0.3)
DECAY = 0.01
ADAM_EPS = 1e-08
BETA = 0.5
BIAS_CORRECTION = 0.875
BF = jnp.bfloat16
FLOPS_PER_US = 10**9
F32 = jnp.float32
VMEM = pl.BlockSpec(memory_space=pltpu.VMEM)
SMEM = pl.BlockSpec(memory_space=pltpu.SMEM)


def dot(a, b, ca, cb):
    return lax.dot_general(a, b, (((ca,), (cb,)), ((), ())), preferred_element_type=F32)


def bits_of(count):
    bits = []
    while count > 1:
        count //= 2
        bits.append(count)
    return bits


def swap(v, step):
    axis, bit = step
    count = lax.axis_size(axis)
    return lax.ppermute(v, axis, [(i, i ^ bit) for i in range(count)])


def offsets(steps, axis):
    offs = [0]
    for name, bit in steps:
        offs = offs + [o ^ (bit if name == axis else 0) for o in offs]
    return offs


def after(v, *ready):
    return lax.optimization_barrier((v, *ready))[0]


def place(steps, axis, off):
    pos = 0
    for k, (name, bit) in enumerate(steps):
        if name == axis:
            pos = pos + ((off // bit) % 2) * (1 << k)
    return pos


class Scatter:
    def __init__(self, keep, send, steps):
        self.keep, self.steps = keep, list(steps)
        self.got = swap(send, self.steps[-1])
        self.send = send

    def advance(self, *ready):
        self.keep, self.send = self.take(*ready)
        self.steps.pop()
        self.got = swap(self.send, self.steps[-1])
        return (self.send,)

    def take(self, *ready):
        half = self.keep.shape[0] // 2
        total = self.keep.astype(F32) + after(self.got, *ready).astype(F32)
        return total[:half].astype(BF), total[half:].astype(BF)


def swap_both(v, one, two):
    n_h = lax.axis_size("head")
    flip = sum(bit * (n_h if axis == "dp" else 1) for axis, bit in (one, two))
    return lax.ppermute(v, ("dp", "head"), [(i, i ^ flip) for i in range(n_h * lax.axis_size("dp"))])


def sum_groups(value, groups, ready):
    for i, group in enumerate(groups):
        got = [value] + [swap(value, step) for step in group]
        if len(group) == 2:
            got.append(swap_both(value, *group))
        if i == len(groups) - 1:
            return got
        if i == 1:
            got[1] = after(got[1], *ready)
        pairs = [a + b for a, b in zip(got[::2], got[1::2])]
        value = functools.reduce(lambda a, b: a + b, pairs)


class RowSums:
    def __init__(self, pieces, bits):
        self.parts, self.bits = {off: [piece] for off, piece in enumerate(pieces)}, list(bits)
        self.flights = []
        self.start()

    def start(self, *ready):
        bit = self.bits.pop()
        sends = []
        for off in [off for off in self.parts if off & bit]:
            parts = self.parts.pop(off)
            total = parts[0]
            if len(parts) > 1:
                total = functools.reduce(
                    lambda a, b: a + b, [parts[0].astype(F32)] + [after(p, *ready).astype(F32) for p in parts[1:]]
                ).astype(BF)
            self.parts[off ^ bit].append(swap(total, ("head", bit)))
            sends.append(total)
        return tuple(sends)

    def advance(self, *ready):
        return self.start(*ready) if self.bits else ()

    def finish(self, value, *ready):
        return functools.reduce(lambda a, b: a + b, [after(p, *ready).astype(F32) for p in self.parts[0]], value)


def lane_mask_stack(v, lh):
    if lh == 1:
        return v
    lane = lax.broadcasted_iota(jnp.int32, v.shape, 1)
    zero = jnp.zeros_like(v)
    return jnp.concatenate(
        [jnp.where((lane >= l * HD) & (lane < (l + 1) * HD), v, zero) for l in range(lh)], axis=0
    )


def head_rows_merge(vt, lh):
    return jnp.concatenate(
        [vt[l * HD : (l + 1) * HD, l * TQ : (l + 1) * TQ] for l in range(lh)], axis=0
    )


def qkv_kernel(lh, n_dp, n_h, dp_offs, idx_ref, w_own, w_got, *refs):
    rows = refs[:n_h]
    q_ref, k_ref, v_ref, vt_ref, wg_ref, inner_ref, w_s, b_s = refs[n_h:]
    g, h = idx_ref[0], idx_ref[1]
    width = lh * HD
    ds_rows = D // n_dp
    rw = rows[0].shape[0]
    shares = b_s.shape[1] // lh
    for p in range(n_dp):
        block = g ^ dp_offs[p]
        w_ref, p = (w_own, p) if p < n_dp // 2 else (w_got, p - n_dp // 2)
        w_s[pl.ds(pl.multiple_of(block * ds_rows, ds_rows), ds_rows), :] = w_ref[p, :ds_rows, :]
        b_s[pl.ds(block, 1), :] = w_ref[p, ds_rows : ds_rows + 16, : lh * shares][:1].astype(F32)
    wide = w_s[...].astype(F32)
    wg = jnp.concatenate(
        [
            wide[:, l * 3 * HD + kind * HD : l * 3 * HD + (kind + 1) * HD]
            for kind in range(3)
            for l in range(lh)
        ],
        axis=1,
    ).astype(BF)
    wg_ref[...] = wg
    per_head = [
        jnp.concatenate([b_s[b : b + 1, l * shares : (l + 1) * shares] for b in range(n_dp)], axis=1)
        for l in range(lh)
    ]
    q_bias = jnp.concatenate([r[:, :HD] for r in per_head], axis=1)
    v_bias = jnp.concatenate([r[:, HD : 2 * HD] for r in per_head], axis=1)
    inner = jnp.concatenate([r[:, 2 * HD :] for r in per_head], axis=1)
    inner_ref[...] = jnp.concatenate(
        [inner[:, i * width : (i + 1) * width] for i in range(inner.shape[1] // width)]
        + [jnp.zeros((16 - inner.shape[1] // width, width), F32)],
        axis=0,
    ).astype(BF)
    for off in range(n_h):
        base = pl.multiple_of((h ^ off) * rw, rw)
        qkv = dot(rows[off][...], wg_ref[...], 1, 0)
        q_ref[pl.ds(base, rw), :] = (qkv[:, :width] + q_bias).astype(BF)
        k_ref[pl.ds(base, rw), :] = qkv[:, width : 2 * width].astype(BF)
        v_ref[pl.ds(base, rw), :] = (qkv[:, 2 * width :] + v_bias).astype(BF)
    vt_ref[:width, :] = v_ref[...].T
    vt_ref[width:, :] = jnp.ones((16, v_ref.shape[0]), BF)


def attend_kernel(lh, offs, idx_ref, seg_ref, q_ref, k_ref, vt_ref, inner_ref, *refs):
    pieces = refs[: len(offs)]
    lse_ref, qb_s, lo_s, all_s, start_s, q2_s, acc_s, top_s, slot_a, slot_b = refs[len(offs) :]
    h = idx_ref[1]
    width = lh * HD
    rw = pieces[0].shape[0] - 16
    per_piece = rw // TQ
    n_t = len(offs) * per_piece
    factor = SCORE_SCALE * LOG2E
    cols = lh * TQ
    column = lax.broadcasted_iota(jnp.int32, (1, cols), 1) % TQ
    all_s[...] = document_starts(seg_ref[...])
    n_pairs = 0
    for t in range(n_t):
        qb = (h ^ offs[t // per_piece]) * per_piece + t % per_piece
        at = pl.ds(pl.multiple_of(qb * TQ, TQ), TQ)
        start = all_s[:, at]
        lo = (jnp.min(start) * (1.0 / TK)).astype(jnp.int32)
        qb_s[t] = qb * (TQ // TK) + (TQ // TK - 1)
        lo_s[t] = lo
        n_pairs = n_pairs + qb_s[t] + 1 - lo
        start_s[t] = jnp.concatenate([start.astype(jnp.int32)] * lh, axis=1)
        q2_s[t] = lane_mask_stack(q_ref[at, :], lh)
    acc_s[...] = jnp.zeros_like(acc_s)
    top_s[...] = jnp.full(top_s.shape, NEG_LARGE, F32)

    def scores(t, kb, slot):
        keys = pl.ds(pl.multiple_of(kb * TK, TK), TK)
        slot[...] = dot(k_ref[keys, :], q2_s[t], 1, 1)

    def mix(t, kb, slot, least):
        c0 = pl.multiple_of(kb * TK, TK)
        key = lax.broadcasted_iota(jnp.int32, (TK, cols), 0)
        first = (qb_s[t] + 1) * TK - TQ
        ok = (key >= start_s[t] - c0 + least) & (key <= column + (first - c0))
        s = jnp.where(ok, slot[...], NEG_LARGE)
        old = top_s[t]
        top = jnp.maximum(old, jnp.max(s, axis=0, keepdims=True))
        p = jnp.exp2((s - top) * factor).astype(BF)
        acc_s[t] = acc_s[t] * jnp.exp2((old - top) * factor) + dot(vt_ref[:, pl.ds(c0, TK)], p, 1, 0)
        top_s[t] = top

    def following(t, kb):
        done = kb >= qb_s[t]
        nt = jnp.minimum(t + 1, n_t - 1)
        return jnp.where(done, nt, t), jnp.where(done, lo_s[nt], kb + 1)

    def two_pairs(i, carry):
        one = following(*carry)
        scores(*one, slot_b)
        mix(*carry, slot_a, 0)
        two = following(*one)
        scores(*two, slot_a)
        mix(*one, slot_b, jnp.where(2 * i + 1 < n_pairs, 0, 4 * q_ref.shape[0]))
        return two

    scores(0, lo_s[0], slot_a)
    lax.fori_loop(0, (n_pairs + 1) // 2, two_pairs, (jnp.int32(0), lo_s[0]))
    for t in range(n_t):
        total = acc_s[t, width : width + 1, :]
        out_t = head_rows_merge(acc_s[t, :width, :] / total, lh)
        inside = (t % per_piece) * TQ
        pieces[t // per_piece][inside : inside + TQ, :] = out_t.T.astype(BF)
        lse_ref[t] = jnp.broadcast_to(top_s[t] * factor + jnp.log2(total), (8, cols))
    for piece in pieces:
        piece[rw:, :] = inner_ref[...]


def document_starts(segment):
    seg = segment.astype(F32)
    start = jnp.zeros(seg.shape, F32)
    for s in range(HEADS):
        count = jnp.sum(jnp.where(seg == float(s), 1.0, 0.0), axis=1, keepdims=True)
        start = start + jnp.where(seg > float(s), count, 0.0)
    return start


def norm_back(grad, xhat, rstd, gain):
    g = grad * gain
    return rstd * (
        g - jnp.mean(g, axis=-1, keepdims=True) - xhat * jnp.mean(g * xhat, axis=-1, keepdims=True)
    )


def fold(v):
    return jnp.sum(v.reshape(v.shape[0] // 8, 8, v.shape[1]), axis=0)


def middle_kernel(lh, n_dp, n_h, e_steps, c_steps, es_steps, cs_steps, idx_ref, norm_ref, *refs):
    width = lh * HD
    mixed = refs[:n_h]
    e_parts, c_parts = refs[n_h : n_h + 4], refs[n_h + 4 : n_h + 8]
    post_in, dual_in, post_cot, dual_cot = refs[n_h + 8 : n_h + 12]
    outs = refs[n_h + 12 :]
    post_out, dual_out, gmid1_ref = outs[:3]
    gm = outs[3 : 3 + n_h]
    ge_keep, ge_send, gc_keep, gc_send, small_ref = outs[3 + n_h : 8 + n_h]
    (e_s, c_s, o_s, mix_s, bias_s, hid_s, acc_s, xh_s, rs_s, pn_s, xb_s, xt_s, gb_s, gmid2_s, ffb_s, gp_s, gt_s) = outs[
        8 + n_h :
    ]
    g, h = idx_ref[0], idx_ref[1]
    rw = post_in.shape[0]
    chunk = min(CHUNK, rw)
    ds_rows = D // n_dp
    units = hid_s.shape[1] // n_h
    row = lambda i: norm_ref[i : i + 1, :]

    e_dp, e_h = offsets(e_steps, "dp"), offsets(e_steps, "head")
    c_dp, c_h = offsets(c_steps, "dp"), offsets(c_steps, "head")
    quarter = n_dp * n_h // 4
    for p in range(n_dp * n_h):
        at = pl.ds(pl.multiple_of((g ^ e_dp[p]) * ds_rows, ds_rows), ds_rows)
        e_ref, c_ref, i = e_parts[p // quarter], c_parts[p // quarter], p % quarter
        e_s[at, e_h[p] * units : (e_h[p] + 1) * units] = e_ref[i]
        at = pl.ds(pl.multiple_of((g ^ c_dp[p]) * ds_rows, ds_rows), ds_rows)
        c_s[at, c_h[p] * units : (c_h[p] + 1) * units] = c_ref[i, :, :units]
        o_s[at, c_h[p] * width : (c_h[p] + 1) * width] = c_ref[i, :, units:]
    for off in range(n_h):
        mix_s[:, off * width : (off + 1) * width] = mixed[off][:rw, :]
        tail = mixed[off][rw : rw + 16, :].astype(F32)
        bias_s[off] = jnp.concatenate([tail[i : i + 1, :] for i in range(units // width)], axis=1)

    acc_s[...] = dot(mix_s[...], o_s[...], 1, 1)

    def chunk_one(i, carry):
        at = pl.ds(pl.multiple_of(i * chunk, chunk), chunk)
        attn_out = acc_s[at, :] + row(2)
        v = post_in[at, :] + attn_out
        centered = v - jnp.mean(v, axis=-1, keepdims=True)
        rstd = lax.rsqrt(jnp.mean(centered * centered, axis=-1, keepdims=True) + EPS_NORM)
        xhat = centered * rstd
        pn = xhat * row(0) + row(1)
        xh_s[at, :] = xhat
        rs_s[at, :] = jnp.broadcast_to(rstd, (chunk, 128))
        pn_s[at, :] = pn
        xb_s[at, :] = pn.astype(BF)
        dual_out[at, :] = dual_in[at, :] + attn_out
        return carry

    lax.fori_loop(0, rw // chunk, chunk_one, 0)
    xt_s[...] = xb_s[...].T
    for oh in range(n_h):
        part = slice(oh * units, (oh + 1) * units)
        pre = dot(xb_s[...], e_s[:, part], 1, 0) + bias_s[oh]
        hid_s[:, part] = jnp.maximum(pre, 0.0).astype(BF)
    acc_s[...] = dot(hid_s[...], c_s[...], 1, 1)

    def chunk_two(i, carry):
        gain_sum, shift_sum, ffn_sum = carry
        at = pl.ds(pl.multiple_of(i * chunk, chunk), chunk)
        ffn_out = acc_s[at, :] + row(5)
        v = pn_s[at, :] + ffn_out
        centered = v - jnp.mean(v, axis=-1, keepdims=True)
        rstd = lax.rsqrt(jnp.mean(centered * centered, axis=-1, keepdims=True) + EPS_NORM)
        xhat = centered * rstd
        post_out[at, :] = xhat * row(3) + row(4)
        dual_out[at, :] = dual_out[at, :] + ffn_out
        cot = post_cot[at, :]
        gmid2 = norm_back(cot, xhat, rstd, row(3))
        gffn = gmid2 + dual_cot[at, :]
        gmid2_s[at, :] = gmid2
        gb_s[at, :] = gffn.astype(BF)
        return gain_sum + fold(cot * xhat), shift_sum + fold(cot), ffn_sum + fold(gffn)

    zero = jnp.zeros((8, D), F32)
    gain2, shift2, ffn_sum = lax.fori_loop(0, rw // chunk, chunk_two, (zero, zero, zero))
    gt_s[...] = gb_s[...].T
    for oh in range(n_h):
        part = slice(oh * units, (oh + 1) * units)
        ge, gc = (ge_keep, gc_keep) if oh % 2 == 0 else (ge_send, gc_send)
        gh = dot(gb_s[...], c_s[:, part], 1, 0)
        gp = jnp.where(hid_s[:, part] > 0, gh, 0.0).astype(BF)
        gp_s[:, part] = gp
        ffb_s[oh] = jnp.sum(gp.astype(F32), axis=0, keepdims=True)
        grad_c = dot(gt_s[...], hid_s[:, part], 1, 0).astype(BF)
        grad_e = dot(xt_s[...], gp, 1, 0).astype(BF)
        e_at, c_at = place(es_steps, "head", oh - oh % 2), place(cs_steps, "head", oh - oh % 2)
        for b in range(n_dp):
            ge[place(es_steps, "dp", b ^ g) + e_at] = grad_e[b * ds_rows : (b + 1) * ds_rows]
            gc[place(cs_steps, "dp", b ^ g) + c_at, :, :units] = grad_c[b * ds_rows : (b + 1) * ds_rows]
    acc_s[...] = dot(gp_s[...], e_s[...], 1, 1)

    def chunk_three(i, carry):
        gain_sum, shift_sum, attn_sum = carry
        at = pl.ds(pl.multiple_of(i * chunk, chunk), chunk)
        grad = gmid2_s[at, :] + acc_s[at, :]
        xhat = xh_s[at, :]
        gmid1 = norm_back(grad, xhat, rs_s[at, :1], row(0))
        gmid1_ref[at, :] = gmid1
        gattn = gmid1 + dual_cot[at, :]
        gb_s[at, :] = gattn.astype(BF)
        return gain_sum + fold(grad * xhat), shift_sum + fold(grad), attn_sum + fold(gattn)

    gain1, shift1, attn_sum = lax.fori_loop(0, rw // chunk, chunk_three, (zero, zero, zero))
    grad_mixed = dot(gb_s[...], o_s[...], 1, 0).astype(BF)
    for off in range(n_h):
        gm[off][...] = grad_mixed[:, off * width : (off + 1) * width]
    grad_o = dot(gb_s[...].T, mix_s[...], 1, 0).astype(BF)
    for oh in range(n_h):
        gc = gc_keep if oh % 2 == 0 else gc_send
        for b in range(n_dp):
            gc[place(cs_steps, "dp", b ^ g) + place(cs_steps, "head", oh - oh % 2), :, units:] = grad_o[
                b * ds_rows : (b + 1) * ds_rows, oh * width : (oh + 1) * width
            ]
    for i, part in enumerate((gain1, shift1, attn_sum, gain2, shift2, ffn_sum)):
        line = jnp.sum(part, axis=0, keepdims=True)
        for j in range(D // 128):
            small_ref[4 * i + j : 4 * i + j + 1, :] = line[:, j * 128 : (j + 1) * 128]
    for oh in range(n_h):
        first = 24 + (h ^ oh) * (units // 128)
        for j in range(units // 128):
            small_ref[pl.ds(first + j, 1), :] = ffb_s[oh, :, j * 128 : (j + 1) * 128]


def first_key_blocks(start, lo_ref):
    total = 0
    for qb in range(start.shape[1] // TQ):
        lo = (jnp.min(start[:, qb * TQ : (qb + 1) * TQ]) * (1.0 / TK)).astype(jnp.int32)
        lo_ref[qb] = lo
        total = total + ((qb + 1) * (TQ // TK) - lo)
    return total


def next_pair(qb, kb, lo_ref, last):
    done = kb >= (qb + 1) * (TQ // TK) - 1
    following = jnp.minimum(qb + 1, last)
    return jnp.where(done, following, qb), jnp.where(done, lo_ref[following], kb + 1)


def attend_back_kernel(lh, n_h, idx_ref, seg_ref, q_ref, k_ref, v_ref, lse_near, lse_far, small_in, *refs):
    gm, pieces = refs[:n_h], refs[n_h : 2 * n_h]
    gqkv_ref, small_ref, lo_s, q2_s, do2_s, delta_s, lse_s, start_s, kt_s, dk_s, dv_s, dq_s = refs[
        2 * n_h : 2 * n_h + 12
    ]
    slots = (refs[2 * n_h + 12 : 2 * n_h + 14], refs[2 * n_h + 14 :])
    h = idx_ref[1]
    width = lh * HD
    rw = gm[0].shape[0]
    n_rows = q_ref.shape[0]
    n_q = n_rows // TQ
    cols = lh * TQ
    factor = SCORE_SCALE * LOG2E
    starts = document_starts(seg_ref[...])
    n_pairs = first_key_blocks(starts, lo_s)
    starts = starts.astype(jnp.int32)
    for qb in range(n_q):
        start_s[qb] = jnp.concatenate([starts[:, qb * TQ : (qb + 1) * TQ]] * lh, axis=1)
        q2_s[qb] = lane_mask_stack(q_ref[qb * TQ : (qb + 1) * TQ, :], lh)
    for off in range(n_h):
        lse_part, n = (lse_near, off) if off < n_h // 2 else (lse_far, off - n_h // 2)
        for i in range(rw // TQ):
            qb = (h ^ off) * (rw // TQ) + i
            do = gm[off][i * TQ : (i + 1) * TQ, :]
            do2_s[qb] = lane_mask_stack(do, lh)
            prod = (do.astype(F32) * pieces[off][i * TQ : (i + 1) * TQ, :].astype(F32)).T
            delta_s[qb] = jnp.concatenate(
                [jnp.sum(prod[l * HD : (l + 1) * HD, :], axis=0, keepdims=True) for l in range(lh)], axis=1
            )
            lse_s[qb] = lse_part[n * (rw // TQ) + i][:1]
    kt_s[...] = k_ref[...].T
    dk_s[...] = jnp.zeros_like(dk_s)
    dv_s[...] = jnp.zeros_like(dv_s)
    dq_s[...] = jnp.zeros_like(dq_s)
    column = lax.broadcasted_iota(jnp.int32, (1, cols), 1) % TQ

    def products(qb, kb, slot):
        keys = pl.ds(pl.multiple_of(kb * TK, TK), TK)
        slot[0][...] = dot(k_ref[keys, :], q2_s[qb], 1, 1)
        slot[1][...] = dot(v_ref[keys, :], do2_s[qb], 1, 1)

    def gradients(qb, kb, slot, least):
        c0 = pl.multiple_of(kb * TK, TK)
        keys = pl.ds(c0, TK)
        key = lax.broadcasted_iota(jnp.int32, (TK, cols), 0)
        ok = (key >= start_s[qb] - c0 + least) & (key <= column + (qb * TQ - c0))
        p = jnp.exp2(jnp.where(ok, slot[0][...], NEG_LARGE) * factor - lse_s[qb])
        grad = (p * (slot[1][...] - delta_s[qb])).astype(BF)
        dv_s[keys, :] += dot(p.astype(BF), do2_s[qb], 1, 0)
        dk_s[keys, :] += dot(grad, q2_s[qb], 1, 0)
        dq_s[qb] += dot(kt_s[:, keys], grad, 1, 0)

    products(0, 0, slots[0])

    def two_pairs(i, carry):
        qb, kb = carry
        one = next_pair(qb, kb, lo_s, n_q - 1)
        products(*one, slots[1])
        gradients(qb, kb, slots[0], 0)
        two = next_pair(*one, lo_s, n_q - 1)
        products(*two, slots[0])
        gradients(*one, slots[1], jnp.where(2 * i + 1 < n_pairs, 0, 2 * n_rows))
        return two

    lax.fori_loop(0, (n_pairs + 1) // 2, two_pairs, (jnp.int32(0), jnp.int32(0)))
    q_sum = jnp.zeros((1, width), F32)
    for qb in range(n_q):
        dq = (head_rows_merge(dq_s[qb], lh) * SCORE_SCALE).T.astype(BF)
        gqkv_ref[qb * TQ : (qb + 1) * TQ, :width] = dq
        q_sum = q_sum + jnp.sum(dq.astype(F32), axis=0, keepdims=True)
    gqkv_ref[:, width : 2 * width] = (dk_s[...] * SCORE_SCALE).astype(BF)
    dv = dv_s[...].astype(BF)
    gqkv_ref[:, 2 * width :] = dv
    v_sum = jnp.sum(dv.astype(F32), axis=0, keepdims=True)
    small_ref[:40, :] = small_in[...]
    small_ref[40:, :] = jnp.zeros((8, 128), F32)
    for l in range(lh):
        small_ref[pl.ds(40 + h * lh + l, 1), :] = jnp.concatenate(
            [q_sum[:, l * HD : (l + 1) * HD], v_sum[:, l * HD : (l + 1) * HD]], axis=1
        )


def rows_back_kernel(n_h, idx_ref, gqkv_ref, wg_ref, *outs):
    h = idx_ref[1]
    rw = outs[0].shape[0]
    for off in range(n_h):
        at = pl.ds(pl.multiple_of((h ^ off) * rw, rw), rw)
        outs[off][...] = dot(gqkv_ref[at, :], wg_ref[...], 1, 1).astype(BF)


def attend_grad_kernel(lh, n_dp, n_h, steps, idx_ref, gqkv_ref, *refs):
    rows = refs[:n_h]
    out_ref, acc_s = refs[n_h:]
    g, h = idx_ref[0], idx_ref[1]
    rw = rows[0].shape[0]
    ds_rows = D // n_dp
    width = lh * HD
    for off in range(n_h):
        at = pl.ds(pl.multiple_of((h ^ off) * rw, rw), rw)
        part = dot(rows[off][...], gqkv_ref[at, :], 0, 0)
        acc_s[...] = part if off == 0 else acc_s[...] + part
    full = acc_s[...]
    full = jnp.concatenate(
        [full[:, kind * width + l * HD : kind * width + (l + 1) * HD] for l in range(lh) for kind in range(3)],
        axis=1,
    ).astype(BF)
    for b in range(n_dp):
        out_ref[place(steps, "dp", b ^ g)] = full[b * ds_rows : (b + 1) * ds_rows]


def total_of_pair(keep_ref, got_ref):
    return keep_ref[0].astype(F32) + got_ref[0].astype(F32)


def squares_kernel(small_ref, *refs):
    out_ref = refs[-1]
    acc = jnp.zeros((8, 128), F32)
    for i in range(0, len(refs) - 1, 2):
        v = total_of_pair(refs[i], refs[i + 1])
        v = fold(v * v)
        if v.shape[1] % 128:
            v = jnp.concatenate([v, jnp.zeros((8, 128 - v.shape[1] % 128), F32)], axis=1)
        for j in range(v.shape[1] // 128):
            acc = acc + v[:, j * 128 : (j + 1) * 128]
    out_ref[:8, :] = acc
    out_ref[8:, :] = small_ref[...]


def adam_kernel(units, n_dp, lh, n_sums, idx_ref, clip_ref, *refs):
    sums, refs = [r[...] for r in refs[:n_sums]], refs[n_sums:]
    sums = [a + b for a, b in zip(sums[::2], sums[1::2])]
    sums = functools.reduce(lambda a, b: a + b, sums)
    params, momenta, variances = refs[6:12], refs[12:18], refs[18:24]
    norm_ref, clipped_ref = refs[24:26]
    outs, small_s = list(refs[26:-1]), refs[-1]
    g, h = idx_ref[0], idx_ref[1]
    small = sums[8:, :]
    small_s[...] = small
    squares = jnp.sum(sums[:8, :]) + jnp.sum(small * small)
    norm_grads = jnp.concatenate(
        [
            jnp.concatenate([small[4 * i + j : 4 * i + j + 1, :] for j in range(D // 128)], axis=1)
            for i in range(6)
        ],
        axis=0,
    )
    width = params[4].shape[1]
    bias_rows = []
    for l in range(lh):
        head = h * lh + l
        full = jnp.concatenate(
            [small_s[pl.ds(at, 1), :] for at in (40 + head, 24 + 2 * head, 25 + 2 * head)], axis=1
        )
        share = jnp.zeros((1, width), F32)
        for b in range(n_dp):
            share = share + jnp.where(g == b, full[:, b * width : (b + 1) * width], 0.0)
        bias_rows.append(share)
    share_bias = jnp.concatenate(bias_rows, axis=0)
    norm = jnp.sqrt(jnp.full((8, 128), squares))
    norm_ref[0] = jnp.max(norm)
    limit = clip_ref[0]
    factor = (limit / jnp.maximum(norm, limit))[:1, :1]
    shares = total_of_pair(refs[4], refs[5])
    grads = (
        total_of_pair(refs[0], refs[1]),
        shares[:, units:],
        total_of_pair(refs[2], refs[3]),
        shares[:, :units],
        share_bias,
        norm_grads,
    )
    for w, m, va, grad, rate in zip(params, momenta, variances, grads, RATES):
        clipped = factor * grad
        momentum_new = BETA * m[...] + (1.0 - BETA) * clipped
        variance_new = BETA * va[...] + (1.0 - BETA) * clipped * clipped
        step = momentum_new / BIAS_CORRECTION / (jnp.sqrt(variance_new / BIAS_CORRECTION) + ADAM_EPS)
        master_new = w[...] - rate * (step + DECAY * w[...])
        outs.pop(0)[...] = momentum_new
        outs.pop(0)[...] = variance_new
        outs.pop(0)[...] = master_new
        if len(outs) > 2:
            outs.pop(0)[...] = master_new.astype(BF)
    clipped_ref[...] = factor * norm_grads


def call(body, outs, scratch, n_smem, args, limit, us):
    return pl.pallas_call(
        body,
        out_shape=outs,
        in_specs=[SMEM] * n_smem + [VMEM] * (len(args) - n_smem),
        out_specs=jax.tree.map(lambda o: SMEM if o.shape == (1,) else VMEM, outs),
        scratch_shapes=scratch,
        compiler_params=pltpu.CompilerParams(vmem_limit_bytes=limit << 20),
        cost_estimate=pl.CostEstimate(flops=us * FLOPS_PER_US, bytes_accessed=1 << 20, transcendentals=0),
    )(*args)


def sds(shape, dtype):
    return jax.ShapeDtypeStruct(shape, dtype)


def per_device(
    post_in,
    dual_in,
    segment_ids,
    post_cot,
    dual_cot,
    attend_weight,
    output_weight,
    expand_weight,
    contract_weight,
    head_bias,
    norm_params,
    attend_momentum,
    output_momentum,
    expand_momentum,
    contract_momentum,
    bias_momentum,
    norm_momentum,
    attend_variance,
    output_variance,
    expand_variance,
    contract_variance,
    bias_variance,
    norm_variance,
    clip_limit,
):
    n_dp, n_h = lax.axis_size("dp"), lax.axis_size("head")
    g, h = lax.axis_index("dp"), lax.axis_index("head")
    idx = jnp.stack([g, h]).astype(jnp.int32)
    rw = post_in.shape[0]
    n_rows = rw * n_h
    lh = HEADS // n_h
    width = lh * HD
    ds_rows = attend_weight.shape[0]
    a_cols = attend_weight.shape[1]
    units = expand_weight.shape[1]
    shares = head_bias.shape[1]
    dp_bits, h_bits = bits_of(n_dp), bits_of(n_h)
    a_steps = [("dp", b) for b in dp_bits]
    dp_steps, h_steps = [("dp", b) for b in dp_bits], [("head", b) for b in h_bits]
    e_steps = dp_steps + h_steps
    c_steps = dp_steps[:-1] + h_steps[:-1] + dp_steps[-1:] + h_steps[-1:]
    es_steps = dp_steps[:-1] + h_steps[:-1] + dp_steps[-1:] + h_steps[-1:]
    cs_steps = dp_steps[:1] + h_steps[:-1] + dp_steps[-1:] + dp_steps[1:-1] + h_steps[-1:]
    g_steps = dp_steps[:1] + dp_steps[-1:] + dp_steps[1:-1]

    bias_block = jnp.pad(
        head_bias.astype(BF).reshape(1, lh * shares), ((0, 15), (0, a_cols - lh * shares))
    )
    a_msg = jnp.concatenate([attend_weight.astype(BF), bias_block], axis=0)
    m_msg = jnp.concatenate(
        [expand_weight.astype(BF), contract_weight.T.astype(BF), output_weight.T.astype(BF)], axis=1
    )
    rows_own = after(post_in, a_msg).astype(BF)

    n_d, n_s = len(dp_bits), len(e_steps)
    a_in, a_got = [a_msg[None]], []
    for i, step in enumerate(a_steps):
        a_got.append(swap(a_in[i], step))
        if i < n_d - 1:
            a_in.append(jnp.concatenate([a_in[i], a_got[i]], axis=0))
    m_in, m_got = m_msg[None], None
    for i in range(n_d - 1):
        if i > 0:
            m_in = jnp.concatenate([m_in, after(m_got, a_got[i - 1])], axis=0)
        m_got = swap(m_in, e_steps[i])
    e_in, c_in = m_in[..., :units], m_in[..., units:]
    e_got, c_got = m_got[..., :units], m_got[..., units:]

    def exchange(i, *ready):
        nonlocal e_in, c_in, e_got, c_got
        e_in = jnp.concatenate([e_in, after(e_got, *ready)], axis=0)
        c_in = jnp.concatenate([c_in, after(c_got, *ready)], axis=0)
        e_got, c_got = swap(e_in, e_steps[i]), swap(c_in, c_steps[i])

    rows = {0: rows_own}
    for bit in h_bits:
        for off in list(rows):
            rows[off ^ bit] = swap(rows[off], ("head", bit))
    rows = [rows[off] for off in range(n_h)]
    exchange(n_d - 1)
    n_q = n_rows // TQ
    cols = lh * TQ
    q, k, v, vt, wg, inner = call(
        functools.partial(qkv_kernel, lh, n_dp, n_h, offsets(a_steps, "dp")),
        [sds((n_rows, width), BF)] * 3
        + [sds((width + 16, n_rows), BF), sds((D, 3 * width), BF), sds((16, width), BF)],
        [pltpu.VMEM((D, a_cols), BF), pltpu.VMEM((n_dp, lh * shares), F32)],
        1,
        [idx, after(a_in[-1], e_in, c_in), a_got[-1]] + rows,
        24,
        4,
    )

    def attend(offs, q):
        out = call(
            functools.partial(attend_kernel, lh, offs),
            [sds((rw + 16, width), BF)] * len(offs) + [sds((n_q // 2, 8, cols), F32)],
            [
                pltpu.SMEM((n_q // 2,), jnp.int32),
                pltpu.SMEM((n_q // 2,), jnp.int32),
                pltpu.VMEM((1, n_rows), F32),
                pltpu.VMEM((n_q // 2, 1, cols), jnp.int32),
                pltpu.VMEM((n_q // 2, cols, width), BF),
                pltpu.VMEM((n_q // 2, width + 16, cols), F32),
                pltpu.VMEM((n_q // 2, 1, cols), F32),
                pltpu.VMEM((TK, cols), F32),
                pltpu.VMEM((TK, cols), F32),
            ],
            1,
            [idx, segment_ids, q, k, vt, inner],
            24,
            1,
        )
        return out[:-1], out[-1]

    exchange(n_d, q)
    far, lse_far = attend(range(n_h // 2, n_h), after(q, e_in, c_in))
    early = n_d + 1 == n_s - 1
    crossed = [swap(e_in, e_steps[-1]), swap(c_in, c_steps[-1])] if early else []
    near, lse_near = attend(range(n_h // 2), after(q, far[0], *crossed))
    for i in range(n_d + 1, n_s - 1):
        exchange(i, near[0])
    pieces = list(near) + list(far)
    mixed = [pieces[0]] + [
        lax.ppermute(pieces[off], "head", [(i, i ^ off) for i in range(n_h)]) for off in range(1, n_h)
    ]
    arrived = [near[0]] + mixed[n_h // 2 :]
    if not early:
        crossed = [swap(e_in, e_steps[-1]), swap(c_in, c_steps[-1])]
    e_got, c_got = after(e_got, *arrived), after(c_got, *arrived)
    e_parts = [e_in, e_got, crossed[0], swap(e_got, e_steps[-1])]
    c_parts = [c_in, c_got, crossed[1], swap(c_got, c_steps[-1])]

    half = n_dp * n_h // 2
    middle_out = call(
        functools.partial(middle_kernel, lh, n_dp, n_h, e_steps, c_steps, es_steps, cs_steps),
        [sds((rw, D), F32)] * 3
        + [sds((rw, width), BF)] * n_h
        + [sds((half, ds_rows, units), BF)] * 2
        + [sds((half, ds_rows, units + width), BF)] * 2
        + [sds((40, 128), F32)],
        [
            pltpu.VMEM((D, n_h * units), BF),
            pltpu.VMEM((D, n_h * units), BF),
            pltpu.VMEM((D, n_h * width), BF),
            pltpu.VMEM((rw, n_h * width), BF),
            pltpu.VMEM((n_h, 1, units), F32),
            pltpu.VMEM((rw, n_h * units), BF),
            pltpu.VMEM((rw, D), F32),
            pltpu.VMEM((rw, D), F32),
            pltpu.VMEM((rw, 128), F32),
            pltpu.VMEM((rw, D), F32),
            pltpu.VMEM((rw, D), BF),
            pltpu.VMEM((D, rw), BF),
            pltpu.VMEM((rw, D), BF),
            pltpu.VMEM((rw, D), F32),
            pltpu.VMEM((n_h, 1, units), F32),
            pltpu.VMEM((rw, n_h * units), BF),
            pltpu.VMEM((D, rw), BF),
        ],
        1,
        [idx, norm_params] + mixed + e_parts + c_parts + [post_in, dual_in, post_cot, dual_cot],
        34,
        20,
    )
    post_out, dual_out, grad_mid1 = middle_out[:3]
    gm = middle_out[3 : 3 + n_h]
    ge_keep, ge_send, gc_keep, gc_send, small_mid = middle_out[3 + n_h :]
    gm = [gm[0]] + [
        lax.ppermute(gm[off], "head", [(i, i ^ off) for i in range(n_h)]) for off in range(1, n_h)
    ]
    ge, gc = Scatter(ge_keep, ge_send, es_steps), Scatter(gc_keep, gc_send, cs_steps)
    gm[0] = after(gm[0], *ge.advance(), *gc.advance())
    gqkv, small = call(
        functools.partial(attend_back_kernel, lh, n_h),
        [sds((n_rows, 3 * width), BF), sds((48, 128), F32)],
        [
            pltpu.SMEM((n_q,), jnp.int32),
            pltpu.VMEM((n_q, cols, width), BF),
            pltpu.VMEM((n_q, cols, width), BF),
            pltpu.VMEM((n_q, 1, cols), F32),
            pltpu.VMEM((n_q, 1, cols), F32),
            pltpu.VMEM((n_q, 1, cols), jnp.int32),
            pltpu.VMEM((width, n_rows), BF),
            pltpu.VMEM((n_rows, width), F32),
            pltpu.VMEM((n_rows, width), F32),
            pltpu.VMEM((n_q, width, cols), F32),
        ]
        + [pltpu.VMEM((TK, cols), F32)] * 4,
        1,
        [idx, segment_ids, q, k, v, lse_near, lse_far, small_mid] + gm + pieces,
        32,
        15,
    )
    sent = ge.advance(gqkv) + gc.advance(gqkv)
    ga = call(
        functools.partial(attend_grad_kernel, lh, n_dp, n_h, g_steps),
        sds((n_dp, ds_rows, a_cols), BF),
        [pltpu.VMEM((D, 3 * width), F32)],
        1,
        [idx, after(gqkv, *sent)] + rows,
        24,
        2,
    )
    ga = Scatter(ga[: n_dp // 2], ga[n_dp // 2 :], g_steps)
    back = call(
        functools.partial(rows_back_kernel, n_h),
        [sds((rw, D), BF)] * n_h,
        [],
        1,
        [idx, after(gqkv, ga.send), wg],
        24,
        2,
    )
    sent = (back[0],)
    back = RowSums(back, sorted(h_bits, reverse=True))
    for i in range(n_s - 3):
        sent = ge.advance(*sent)
        sent = gc.advance(*sent)
        if i == 0:
            for _ in range(len(h_bits) - 1):
                sent = back.advance(*sent)
        if i < n_d - 1:
            sent = ga.advance(*sent)
    post_grad = back.finish(grad_mid1, *sent)
    pairs = [ga.keep, ga.got, ge.keep, ge.got, gc.keep, gc.got]
    squares = call(squares_kernel, sds((56, 128), F32), [], 0, [small] + pairs, 16, 1)
    order = h_steps[-1:] + [step for step in h_steps[:-1] + dp_steps[::-1]]
    groups = [order[:1]] + [order[i : i + 2] for i in range(1, len(order), 2)]
    sums = sum_groups(squares, groups, (post_grad,))
    flip = lambda arrays: [a.T if i in (1, 3) else a for i, a in enumerate(arrays)]
    params = flip([attend_weight, output_weight, expand_weight, contract_weight, head_bias, norm_params])
    momenta = flip(
        [attend_momentum, output_momentum, expand_momentum, contract_momentum, bias_momentum, norm_momentum]
    )
    variances = flip(
        [attend_variance, output_variance, expand_variance, contract_variance, bias_variance, norm_variance]
    )
    shapes = [sds((1,), F32), sds((6, D), F32)]
    for i, w in enumerate(params):
        shapes += [sds(w.shape, F32)] * 3 + ([sds(w.shape, BF)] if i < 5 else [])
    norm, norm_clipped, *results = call(
        functools.partial(adam_kernel, units, n_dp, lh, len(sums)),
        shapes,
        [pltpu.VMEM((48, 128), F32)],
        2,
        [idx, clip_limit] + sums + pairs + params + momenta + variances,
        24,
        2,
    )
    results = [a.T if i // 4 in (1, 3) else a for i, a in enumerate(results)]
    return (post_out, dual_out, post_grad, norm, *results, norm_clipped)


def solution(mesh):
    rows = P(("dp", "head"), None)
    tall, flat, rep = P("dp", "head"), P("head", "dp"), P()
    weights = (tall, flat, tall, flat, flat, rep)
    in_specs = (rows, rows, P("dp", None), rows, rows) + weights * 3 + (rep,)
    out_specs = (rows, rows, rows, rep)
    for spec in (tall, flat, tall, flat, flat):
        out_specs += (spec,) * 4
    out_specs += (rep,) * 4
    return jax.shard_map(per_device, mesh=mesh, in_specs=in_specs, out_specs=out_specs, check_vma=False)
```

```python
import functools

import jax
import jax.numpy as jnp
from jax import lax
from jax.experimental import pallas as pl
from jax.experimental.pallas import tpu as pltpu
from jax.sharding import PartitionSpec as P

D = 512
HEADS = 8
HD = 64
TQ = 256
TK = 256
CHUNK = 512

EPS_NORM = 1e-05
NEG_LARGE = -1e30
LOG2E = 1.4426950408889634
SCORE_SCALE = HD ** (-0.5)
RATES = (0.04, 0.12, 0.04, 0.04, 0.16, 0.3)
DECAY = 0.01
ADAM_EPS = 1e-08
BETA = 0.5
BIAS_CORRECTION = 0.875
BF = jnp.bfloat16
FLOPS_PER_US = 10**9
F32 = jnp.float32
VMEM = pl.BlockSpec(memory_space=pltpu.VMEM)
SMEM = pl.BlockSpec(memory_space=pltpu.SMEM)


def dot(a, b, ca, cb):
    return lax.dot_general(a, b, (((ca,), (cb,)), ((), ())), preferred_element_type=F32)


def bits_of(count):
    bits = []
    while count > 1:
        count //= 2
        bits.append(count)
    return bits


def swap(v, step):
    axis, bit = step
    count = lax.axis_size(axis)
    return lax.ppermute(v, axis, [(i, i ^ bit) for i in range(count)])


def offsets(steps, axis):
    offs = [0]
    for name, bit in steps:
        offs = offs + [o ^ (bit if name == axis else 0) for o in offs]
    return offs


def after(v, *ready):
    return lax.optimization_barrier((v, *ready))[0]


def place(steps, axis, off):
    pos = 0
    for k, (name, bit) in enumerate(steps):
        if name == axis:
            pos = pos + ((off // bit) % 2) * (1 << k)
    return pos


class Scatter:
    def __init__(self, keep, send, steps):
        self.keep, self.steps = keep, list(steps)
        self.got = swap(send, self.steps[-1])
        self.send = send

    def advance(self, *ready):
        self.keep, self.send = self.take(*ready)
        self.steps.pop()
        self.got = swap(self.send, self.steps[-1])
        return (self.send,)

    def take(self, *ready):
        half = self.keep.shape[0] // 2
        total = self.keep.astype(F32) + after(self.got, *ready).astype(F32)
        return total[:half].astype(BF), total[half:].astype(BF)


def swap_both(v, one, two):
    n_h = lax.axis_size("head")
    flip = sum(bit * (n_h if axis == "dp" else 1) for axis, bit in (one, two))
    return lax.ppermute(v, ("dp", "head"), [(i, i ^ flip) for i in range(n_h * lax.axis_size("dp"))])


def sum_groups(value, groups, ready):
    for i, group in enumerate(groups):
        got = [value] + [swap(value, step) for step in group]
        if len(group) == 2:
            got.append(swap_both(value, *group))
        if i == len(groups) - 1:
            return got
        if i == 1:
            got[1] = after(got[1], *ready)
        pairs = [a + b for a, b in zip(got[::2], got[1::2])]
        value = functools.reduce(lambda a, b: a + b, pairs)


class RowSums:
    def __init__(self, pieces, bits):
        self.parts, self.bits = {off: [piece] for off, piece in enumerate(pieces)}, list(bits)
        self.flights = []
        self.start()

    def start(self, *ready):
        bit = self.bits.pop()
        sends = []
        for off in [off for off in self.parts if off & bit]:
            parts = self.parts.pop(off)
            total = parts[0]
            if len(parts) > 1:
                total = functools.reduce(
                    lambda a, b: a + b, [parts[0].astype(F32)] + [after(p, *ready).astype(F32) for p in parts[1:]]
                ).astype(BF)
            self.parts[off ^ bit].append(swap(total, ("head", bit)))
            sends.append(total)
        return tuple(sends)

    def advance(self, *ready):
        return self.start(*ready) if self.bits else ()

    def finish(self, value, *ready):
        return functools.reduce(lambda a, b: a + b, [after(p, *ready).astype(F32) for p in self.parts[0]], value)


def lane_mask_stack(v, lh):
    if lh == 1:
        return v
    lane = lax.broadcasted_iota(jnp.int32, v.shape, 1)
    zero = jnp.zeros_like(v)
    return jnp.concatenate(
        [jnp.where((lane >= l * HD) & (lane < (l + 1) * HD), v, zero) for l in range(lh)], axis=0
    )


def row_mask_stack(vt, lh):
    if lh == 1:
        return vt
    row = lax.broadcasted_iota(jnp.int32, vt.shape, 0)
    zero = jnp.zeros_like(vt)
    return jnp.concatenate(
        [jnp.where((row >= l * HD) & (row < (l + 1) * HD), vt, zero) for l in range(lh)], axis=1
    )


def head_rows_merge(vt, lh):
    return jnp.concatenate(
        [vt[l * HD : (l + 1) * HD, l * TQ : (l + 1) * TQ] for l in range(lh)], axis=0
    )


def qkv_kernel(lh, n_dp, n_h, dp_offs, idx_ref, w_own, w_got, *refs):
    rows = refs[:n_h]
    q_ref, k_ref, v_ref, vt_ref, wg_ref, inner_ref, w_s, b_s = refs[n_h:]
    g, h = idx_ref[0], idx_ref[1]
    width = lh * HD
    ds_rows = D // n_dp
    rw = rows[0].shape[0]
    shares = b_s.shape[1] // lh
    for p in range(n_dp):
        block = g ^ dp_offs[p]
        w_ref, p = (w_own, p) if p < n_dp // 2 else (w_got, p - n_dp // 2)
        w_s[pl.ds(pl.multiple_of(block * ds_rows, ds_rows), ds_rows), :] = w_ref[p, :ds_rows, :]
        b_s[pl.ds(block, 1), :] = w_ref[p, ds_rows : ds_rows + 16, : lh * shares][:1].astype(F32)
    wide = w_s[...].astype(F32)
    wg = jnp.concatenate(
        [
            wide[:, l * 3 * HD + kind * HD : l * 3 * HD + (kind + 1) * HD]
            for kind in range(3)
            for l in range(lh)
        ],
        axis=1,
    ).astype(BF)
    wg_ref[...] = wg
    per_head = [
        jnp.concatenate([b_s[b : b + 1, l * shares : (l + 1) * shares] for b in range(n_dp)], axis=1)
        for l in range(lh)
    ]
    q_bias = jnp.concatenate([r[:, :HD] for r in per_head], axis=1)
    v_bias = jnp.concatenate([r[:, HD : 2 * HD] for r in per_head], axis=1)
    inner = jnp.concatenate([r[:, 2 * HD :] for r in per_head], axis=1)
    inner_ref[...] = jnp.concatenate(
        [inner[:, i * width : (i + 1) * width] for i in range(inner.shape[1] // width)]
        + [jnp.zeros((16 - inner.shape[1] // width, width), F32)],
        axis=0,
    ).astype(BF)
    for off in range(n_h):
        base = pl.multiple_of((h ^ off) * rw, rw)
        qkv = dot(rows[off][...], wg_ref[...], 1, 0)
        q_ref[pl.ds(base, rw), :] = (qkv[:, :width] + q_bias).astype(BF)
        k_ref[pl.ds(base, rw), :] = qkv[:, width : 2 * width].astype(BF)
        v_ref[pl.ds(base, rw), :] = (qkv[:, 2 * width :] + v_bias).astype(BF)
    vt_ref[:width, :] = v_ref[...].T
    vt_ref[width:, :] = jnp.ones((16, v_ref.shape[0]), BF)


def attend_kernel(lh, offs, idx_ref, seg_ref, q_ref, k_ref, vt_ref, inner_ref, *refs):
    pieces = refs[: len(offs)]
    lse_ref, qb_s, lo_s, all_s, start_s, q2_s, acc_s, top_s, slot_a, slot_b = refs[len(offs) :]
    h = idx_ref[1]
    width = lh * HD
    rw = pieces[0].shape[0] - 16
    per_piece = rw // TQ
    n_t = len(offs) * per_piece
    factor = SCORE_SCALE * LOG2E
    cols = lh * TQ
    column = lax.broadcasted_iota(jnp.int32, (1, cols), 1) % TQ
    all_s[...] = document_starts(seg_ref[...])
    n_pairs = 0
    for t in range(n_t):
        qb = (h ^ offs[t // per_piece]) * per_piece + t % per_piece
        at = pl.ds(pl.multiple_of(qb * TQ, TQ), TQ)
        start = all_s[:, at]
        lo = (jnp.min(start) * (1.0 / TK)).astype(jnp.int32)
        qb_s[t] = qb * (TQ // TK) + (TQ // TK - 1)
        lo_s[t] = lo
        n_pairs = n_pairs + qb_s[t] + 1 - lo
        start_s[t] = jnp.concatenate([start.astype(jnp.int32)] * lh, axis=1)
        q2_s[t] = lane_mask_stack(q_ref[at, :], lh)
    acc_s[...] = jnp.zeros_like(acc_s)
    top_s[...] = jnp.full(top_s.shape, NEG_LARGE, F32)

    def scores(t, kb, slot):
        keys = pl.ds(pl.multiple_of(kb * TK, TK), TK)
        slot[...] = dot(k_ref[keys, :], q2_s[t], 1, 1)

    def mix(t, kb, slot, least):
        c0 = pl.multiple_of(kb * TK, TK)
        key = lax.broadcasted_iota(jnp.int32, (TK, cols), 0)
        first = (qb_s[t] + 1) * TK - TQ
        ok = (key >= start_s[t] - c0 + least) & (key <= column + (first - c0))
        s = jnp.where(ok, slot[...], NEG_LARGE)
        old = top_s[t]
        top = jnp.maximum(old, jnp.max(s, axis=0, keepdims=True))
        p = jnp.exp2((s - top) * factor).astype(BF)
        acc_s[t] = acc_s[t] * jnp.exp2((old - top) * factor) + dot(vt_ref[:, pl.ds(c0, TK)], p, 1, 0)
        top_s[t] = top

    def following(t, kb):
        done = kb >= qb_s[t]
        nt = jnp.minimum(t + 1, n_t - 1)
        return jnp.where(done, nt, t), jnp.where(done, lo_s[nt], kb + 1)

    def two_pairs(i, carry):
        one = following(*carry)
        scores(*one, slot_b)
        mix(*carry, slot_a, 0)
        two = following(*one)
        scores(*two, slot_a)
        mix(*one, slot_b, jnp.where(2 * i + 1 < n_pairs, 0, 4 * q_ref.shape[0]))
        return two

    scores(0, lo_s[0], slot_a)
    lax.fori_loop(0, (n_pairs + 1) // 2, two_pairs, (jnp.int32(0), lo_s[0]))
    for t in range(n_t):
        total = acc_s[t, width : width + 1, :]
        out_t = head_rows_merge(acc_s[t, :width, :] / total, lh)
        inside = (t % per_piece) * TQ
        pieces[t // per_piece][inside : inside + TQ, :] = out_t.T.astype(BF)
        lse_ref[t] = jnp.broadcast_to(top_s[t] * factor + jnp.log2(total), (8, cols))
    for piece in pieces:
        piece[rw:, :] = inner_ref[...]


def document_starts(segment):
    seg = segment.astype(F32)
    start = jnp.zeros(seg.shape, F32)
    for s in range(HEADS):
        count = jnp.sum(jnp.where(seg == float(s), 1.0, 0.0), axis=1, keepdims=True)
        start = start + jnp.where(seg > float(s), count, 0.0)
    return start


def norm_back(grad, xhat, rstd, gain):
    g = grad * gain
    return rstd * (
        g - jnp.mean(g, axis=-1, keepdims=True) - xhat * jnp.mean(g * xhat, axis=-1, keepdims=True)
    )


def fold(v):
    return jnp.sum(v.reshape(v.shape[0] // 8, 8, v.shape[1]), axis=0)


def middle_kernel(lh, n_dp, n_h, e_steps, c_steps, es_steps, cs_steps, idx_ref, norm_ref, *refs):
    width = lh * HD
    mixed = refs[:n_h]
    e_parts, c_parts = refs[n_h : n_h + 4], refs[n_h + 4 : n_h + 8]
    post_in, dual_in, post_cot, dual_cot = refs[n_h + 8 : n_h + 12]
    outs = refs[n_h + 12 :]
    post_out, dual_out, gmid1_ref = outs[:3]
    gm = outs[3 : 3 + n_h]
    ge_keep, ge_send, gc_keep, gc_send, small_ref = outs[3 + n_h : 8 + n_h]
    (e_s, c_s, o_s, mix_s, bias_s, hid_s, acc_s, xh_s, rs_s, pn_s, xb_s, xt_s, gb_s, gmid2_s, ffb_s, gp_s, gt_s) = outs[
        8 + n_h :
    ]
    g, h = idx_ref[0], idx_ref[1]
    rw = post_in.shape[0]
    chunk = min(CHUNK, rw)
    ds_rows = D // n_dp
    units = hid_s.shape[1] // n_h
    row = lambda i: norm_ref[i : i + 1, :]

    e_dp, e_h = offsets(e_steps, "dp"), offsets(e_steps, "head")
    c_dp, c_h = offsets(c_steps, "dp"), offsets(c_steps, "head")
    quarter = n_dp * n_h // 4
    for p in range(n_dp * n_h):
        at = pl.ds(pl.multiple_of((g ^ e_dp[p]) * ds_rows, ds_rows), ds_rows)
        e_ref, c_ref, i = e_parts[p // quarter], c_parts[p // quarter], p % quarter
        e_s[at, e_h[p] * units : (e_h[p] + 1) * units] = e_ref[i]
        at = pl.ds(pl.multiple_of((g ^ c_dp[p]) * ds_rows, ds_rows), ds_rows)
        c_s[at, c_h[p] * units : (c_h[p] + 1) * units] = c_ref[i, :, :units]
        o_s[at, c_h[p] * width : (c_h[p] + 1) * width] = c_ref[i, :, units:]
    for off in range(n_h):
        mix_s[:, off * width : (off + 1) * width] = mixed[off][:rw, :]
        tail = mixed[off][rw : rw + 16, :].astype(F32)
        bias_s[off] = jnp.concatenate([tail[i : i + 1, :] for i in range(units // width)], axis=1)

    acc_s[...] = dot(mix_s[...], o_s[...], 1, 1)

    def chunk_one(i, carry):
        at = pl.ds(pl.multiple_of(i * chunk, chunk), chunk)
        attn_out = acc_s[at, :] + row(2)
        v = post_in[at, :] + attn_out
        centered = v - jnp.mean(v, axis=-1, keepdims=True)
        rstd = lax.rsqrt(jnp.mean(centered * centered, axis=-1, keepdims=True) + EPS_NORM)
        xhat = centered * rstd
        pn = xhat * row(0) + row(1)
        xh_s[at, :] = xhat
        rs_s[at, :] = jnp.broadcast_to(rstd, (chunk, 128))
        pn_s[at, :] = pn
        xb_s[at, :] = pn.astype(BF)
        dual_out[at, :] = dual_in[at, :] + attn_out
        return carry

    lax.fori_loop(0, rw // chunk, chunk_one, 0)
    xt_s[...] = xb_s[...].T
    for oh in range(n_h):
        part = slice(oh * units, (oh + 1) * units)
        pre = dot(xb_s[...], e_s[:, part], 1, 0) + bias_s[oh]
        hid_s[:, part] = jnp.maximum(pre, 0.0).astype(BF)
    acc_s[...] = dot(hid_s[...], c_s[...], 1, 1)

    def chunk_two(i, carry):
        gain_sum, shift_sum, ffn_sum = carry
        at = pl.ds(pl.multiple_of(i * chunk, chunk), chunk)
        ffn_out = acc_s[at, :] + row(5)
        v = pn_s[at, :] + ffn_out
        centered = v - jnp.mean(v, axis=-1, keepdims=True)
        rstd = lax.rsqrt(jnp.mean(centered * centered, axis=-1, keepdims=True) + EPS_NORM)
        xhat = centered * rstd
        post_out[at, :] = xhat * row(3) + row(4)
        dual_out[at, :] = dual_out[at, :] + ffn_out
        cot = post_cot[at, :]
        gmid2 = norm_back(cot, xhat, rstd, row(3))
        gffn = gmid2 + dual_cot[at, :]
        gmid2_s[at, :] = gmid2
        gb_s[at, :] = gffn.astype(BF)
        return gain_sum + fold(cot * xhat), shift_sum + fold(cot), ffn_sum + fold(gffn)

    zero = jnp.zeros((8, D), F32)
    gain2, shift2, ffn_sum = lax.fori_loop(0, rw // chunk, chunk_two, (zero, zero, zero))
    gt_s[...] = gb_s[...].T
    for oh in range(n_h):
        part = slice(oh * units, (oh + 1) * units)
        ge, gc = (ge_keep, gc_keep) if oh % 2 == 0 else (ge_send, gc_send)
        gh = dot(gb_s[...], c_s[:, part], 1, 0)
        gp = jnp.where(hid_s[:, part] > 0, gh, 0.0).astype(BF)
        gp_s[:, part] = gp
        ffb_s[oh] = jnp.sum(gp.astype(F32), axis=0, keepdims=True)
        grad_c = dot(gt_s[...], hid_s[:, part], 1, 0).astype(BF)
        grad_e = dot(xt_s[...], gp, 1, 0).astype(BF)
        e_at, c_at = place(es_steps, "head", oh - oh % 2), place(cs_steps, "head", oh - oh % 2)
        for b in range(n_dp):
            ge[place(es_steps, "dp", b ^ g) + e_at] = grad_e[b * ds_rows : (b + 1) * ds_rows]
            gc[place(cs_steps, "dp", b ^ g) + c_at, :, :units] = grad_c[b * ds_rows : (b + 1) * ds_rows]
    acc_s[...] = dot(gp_s[...], e_s[...], 1, 1)

    def chunk_three(i, carry):
        gain_sum, shift_sum, attn_sum = carry
        at = pl.ds(pl.multiple_of(i * chunk, chunk), chunk)
        grad = gmid2_s[at, :] + acc_s[at, :]
        xhat = xh_s[at, :]
        gmid1 = norm_back(grad, xhat, rs_s[at, :1], row(0))
        gmid1_ref[at, :] = gmid1
        gattn = gmid1 + dual_cot[at, :]
        gb_s[at, :] = gattn.astype(BF)
        return gain_sum + fold(grad * xhat), shift_sum + fold(grad), attn_sum + fold(gattn)

    gain1, shift1, attn_sum = lax.fori_loop(0, rw // chunk, chunk_three, (zero, zero, zero))
    grad_mixed = dot(gb_s[...], o_s[...], 1, 0).astype(BF)
    for off in range(n_h):
        gm[off][...] = grad_mixed[:, off * width : (off + 1) * width]
    grad_o = dot(gb_s[...].T, mix_s[...], 1, 0).astype(BF)
    for oh in range(n_h):
        gc = gc_keep if oh % 2 == 0 else gc_send
        for b in range(n_dp):
            gc[place(cs_steps, "dp", b ^ g) + place(cs_steps, "head", oh - oh % 2), :, units:] = grad_o[
                b * ds_rows : (b + 1) * ds_rows, oh * width : (oh + 1) * width
            ]
    for i, part in enumerate((gain1, shift1, attn_sum, gain2, shift2, ffn_sum)):
        line = jnp.sum(part, axis=0, keepdims=True)
        for j in range(D // 128):
            small_ref[4 * i + j : 4 * i + j + 1, :] = line[:, j * 128 : (j + 1) * 128]
    for oh in range(n_h):
        first = 24 + (h ^ oh) * (units // 128)
        for j in range(units // 128):
            small_ref[pl.ds(first + j, 1), :] = ffb_s[oh, :, j * 128 : (j + 1) * 128]


def first_key_blocks(start, lo_ref):
    total = 0
    for qb in range(start.shape[1] // TQ):
        lo = (jnp.min(start[:, qb * TQ : (qb + 1) * TQ]) * (1.0 / TK)).astype(jnp.int32)
        lo_ref[qb] = lo
        total = total + ((qb + 1) * (TQ // TK) - lo)
    return total


def next_pair(qb, kb, lo_ref, last):
    done = kb >= (qb + 1) * (TQ // TK) - 1
    following = jnp.minimum(qb + 1, last)
    return jnp.where(done, following, qb), jnp.where(done, lo_ref[following], kb + 1)


def attend_back_kernel(lh, n_h, idx_ref, seg_ref, q_ref, k_ref, v_ref, lse_near, lse_far, small_in, *refs):
    gm, pieces = refs[:n_h], refs[n_h : 2 * n_h]
    gqkv_ref, small_ref, lo_s, q2_s, do2_s, delta_s, lse_s, start_s, kt_s, dk_s, dv_s, dq_s = refs[
        2 * n_h : 2 * n_h + 12
    ]
    slots = (refs[2 * n_h + 12 : 2 * n_h + 14], refs[2 * n_h + 14 :])
    h = idx_ref[1]
    width = lh * HD
    rw = gm[0].shape[0]
    n_rows = q_ref.shape[0]
    n_q = n_rows // TQ
    cols = lh * TQ
    factor = SCORE_SCALE * LOG2E
    starts = document_starts(seg_ref[...])
    n_pairs = first_key_blocks(starts, lo_s)
    starts = starts.astype(jnp.int32)
    for qb in range(n_q):
        start_s[qb] = jnp.concatenate([starts[:, qb * TQ : (qb + 1) * TQ]] * lh, axis=1)
        q2_s[qb] = row_mask_stack(q_ref[qb * TQ : (qb + 1) * TQ, :].T, lh)
    for off in range(n_h):
        lse_part, n = (lse_near, off) if off < n_h // 2 else (lse_far, off - n_h // 2)
        for i in range(rw // TQ):
            qb = (h ^ off) * (rw // TQ) + i
            do = gm[off][i * TQ : (i + 1) * TQ, :]
            do2_s[qb] = row_mask_stack(do.T, lh)
            prod = (do.astype(F32) * pieces[off][i * TQ : (i + 1) * TQ, :].astype(F32)).T
            delta_s[qb] = jnp.concatenate(
                [jnp.sum(prod[l * HD : (l + 1) * HD, :], axis=0, keepdims=True) for l in range(lh)], axis=1
            )
            lse_s[qb] = lse_part[n * (rw // TQ) + i][:1]
    kt_s[...] = k_ref[...].T
    dk_s[...] = jnp.zeros_like(dk_s)
    dv_s[...] = jnp.zeros_like(dv_s)
    dq_s[...] = jnp.zeros_like(dq_s)
    column = lax.broadcasted_iota(jnp.int32, (1, cols), 1) % TQ

    def products(qb, kb, slot):
        keys = pl.ds(pl.multiple_of(kb * TK, TK), TK)
        slot[0][...] = dot(k_ref[keys, :], q2_s[qb], 1, 0)
        slot[1][...] = dot(v_ref[keys, :], do2_s[qb], 1, 0)

    def gradients(qb, kb, slot, least):
        c0 = pl.multiple_of(kb * TK, TK)
        keys = pl.ds(c0, TK)
        key = lax.broadcasted_iota(jnp.int32, (TK, cols), 0)
        ok = (key >= start_s[qb] - c0 + least) & (key <= column + (qb * TQ - c0))
        p = jnp.exp2(jnp.where(ok, slot[0][...], NEG_LARGE) * factor - lse_s[qb])
        grad = (p * (slot[1][...] - delta_s[qb])).astype(BF)
        dv_s[:, keys] += dot(do2_s[qb], p.astype(BF), 1, 1)
        dk_s[:, keys] += dot(q2_s[qb], grad, 1, 1)
        dq_s[qb] += dot(kt_s[:, keys], grad, 1, 0)

    products(0, 0, slots[0])

    def two_pairs(i, carry):
        qb, kb = carry
        one = next_pair(qb, kb, lo_s, n_q - 1)
        products(*one, slots[1])
        gradients(qb, kb, slots[0], 0)
        two = next_pair(*one, lo_s, n_q - 1)
        products(*two, slots[0])
        gradients(*one, slots[1], jnp.where(2 * i + 1 < n_pairs, 0, 2 * n_rows))
        return two

    lax.fori_loop(0, (n_pairs + 1) // 2, two_pairs, (jnp.int32(0), jnp.int32(0)))
    q_sum = jnp.zeros((1, width), F32)
    for qb in range(n_q):
        dq = (head_rows_merge(dq_s[qb], lh) * SCORE_SCALE).T.astype(BF)
        gqkv_ref[qb * TQ : (qb + 1) * TQ, :width] = dq
        q_sum = q_sum + jnp.sum(dq.astype(F32), axis=0, keepdims=True)
    gqkv_ref[:, width : 2 * width] = (dk_s[...] * SCORE_SCALE).astype(BF).T
    dv = dv_s[...].astype(BF).T
    gqkv_ref[:, 2 * width :] = dv
    v_sum = jnp.sum(dv.astype(F32), axis=0, keepdims=True)
    small_ref[:40, :] = small_in[...]
    small_ref[40:, :] = jnp.zeros((8, 128), F32)
    for l in range(lh):
        small_ref[pl.ds(40 + h * lh + l, 1), :] = jnp.concatenate(
            [q_sum[:, l * HD : (l + 1) * HD], v_sum[:, l * HD : (l + 1) * HD]], axis=1
        )


def rows_back_kernel(n_h, idx_ref, gqkv_ref, wg_ref, *outs):
    h = idx_ref[1]
    rw = outs[0].shape[0]
    for off in range(n_h):
        at = pl.ds(pl.multiple_of((h ^ off) * rw, rw), rw)
        outs[off][...] = dot(gqkv_ref[at, :], wg_ref[...], 1, 1).astype(BF)


def attend_grad_kernel(lh, n_dp, n_h, steps, idx_ref, gqkv_ref, *refs):
    rows = refs[:n_h]
    out_ref, acc_s = refs[n_h:]
    g, h = idx_ref[0], idx_ref[1]
    rw = rows[0].shape[0]
    ds_rows = D // n_dp
    width = lh * HD
    for off in range(n_h):
        at = pl.ds(pl.multiple_of((h ^ off) * rw, rw), rw)
        part = dot(rows[off][...], gqkv_ref[at, :], 0, 0)
        acc_s[...] = part if off == 0 else acc_s[...] + part
    full = acc_s[...]
    full = jnp.concatenate(
        [full[:, kind * width + l * HD : kind * width + (l + 1) * HD] for l in range(lh) for kind in range(3)],
        axis=1,
    ).astype(BF)
    for b in range(n_dp):
        out_ref[place(steps, "dp", b ^ g)] = full[b * ds_rows : (b + 1) * ds_rows]


def total_of_pair(keep_ref, got_ref):
    return keep_ref[0].astype(F32) + got_ref[0].astype(F32)


def squares_kernel(small_ref, *refs):
    out_ref = refs[-1]
    acc = jnp.zeros((8, 128), F32)
    for i in range(0, len(refs) - 1, 2):
        v = total_of_pair(refs[i], refs[i + 1])
        v = fold(v * v)
        if v.shape[1] % 128:
            v = jnp.concatenate([v, jnp.zeros((8, 128 - v.shape[1] % 128), F32)], axis=1)
        for j in range(v.shape[1] // 128):
            acc = acc + v[:, j * 128 : (j + 1) * 128]
    out_ref[:8, :] = acc
    out_ref[8:, :] = small_ref[...]


def adam_kernel(units, n_dp, lh, n_sums, idx_ref, clip_ref, *refs):
    sums, refs = [r[...] for r in refs[:n_sums]], refs[n_sums:]
    sums = [a + b for a, b in zip(sums[::2], sums[1::2])]
    sums = functools.reduce(lambda a, b: a + b, sums)
    params, momenta, variances = refs[6:12], refs[12:18], refs[18:24]
    norm_ref, clipped_ref = refs[24:26]
    outs, small_s = list(refs[26:-1]), refs[-1]
    g, h = idx_ref[0], idx_ref[1]
    small = sums[8:, :]
    small_s[...] = small
    squares = jnp.sum(sums[:8, :]) + jnp.sum(small * small)
    norm_grads = jnp.concatenate(
        [
            jnp.concatenate([small[4 * i + j : 4 * i + j + 1, :] for j in range(D // 128)], axis=1)
            for i in range(6)
        ],
        axis=0,
    )
    width = params[4].shape[1]
    bias_rows = []
    for l in range(lh):
        head = h * lh + l
        full = jnp.concatenate(
            [small_s[pl.ds(at, 1), :] for at in (40 + head, 24 + 2 * head, 25 + 2 * head)], axis=1
        )
        share = jnp.zeros((1, width), F32)
        for b in range(n_dp):
            share = share + jnp.where(g == b, full[:, b * width : (b + 1) * width], 0.0)
        bias_rows.append(share)
    share_bias = jnp.concatenate(bias_rows, axis=0)
    norm = jnp.sqrt(jnp.full((8, 128), squares))
    norm_ref[0] = jnp.max(norm)
    limit = clip_ref[0]
    factor = (limit / jnp.maximum(norm, limit))[:1, :1]
    shares = total_of_pair(refs[4], refs[5])
    grads = (
        total_of_pair(refs[0], refs[1]),
        shares[:, units:],
        total_of_pair(refs[2], refs[3]),
        shares[:, :units],
        share_bias,
        norm_grads,
    )
    for w, m, va, grad, rate in zip(params, momenta, variances, grads, RATES):
        clipped = factor * grad
        momentum_new = BETA * m[...] + (1.0 - BETA) * clipped
        variance_new = BETA * va[...] + (1.0 - BETA) * clipped * clipped
        step = momentum_new / BIAS_CORRECTION / (jnp.sqrt(variance_new / BIAS_CORRECTION) + ADAM_EPS)
        master_new = w[...] - rate * (step + DECAY * w[...])
        outs.pop(0)[...] = momentum_new
        outs.pop(0)[...] = variance_new
        outs.pop(0)[...] = master_new
        if len(outs) > 2:
            outs.pop(0)[...] = master_new.astype(BF)
    clipped_ref[...] = factor * norm_grads


def call(body, outs, scratch, n_smem, args, limit, us):
    return pl.pallas_call(
        body,
        out_shape=outs,
        in_specs=[SMEM] * n_smem + [VMEM] * (len(args) - n_smem),
        out_specs=jax.tree.map(lambda o: SMEM if o.shape == (1,) else VMEM, outs),
        scratch_shapes=scratch,
        compiler_params=pltpu.CompilerParams(vmem_limit_bytes=limit << 20),
        cost_estimate=pl.CostEstimate(flops=us * FLOPS_PER_US, bytes_accessed=1 << 20, transcendentals=0),
    )(*args)


def sds(shape, dtype):
    return jax.ShapeDtypeStruct(shape, dtype)


def per_device(
    post_in,
    dual_in,
    segment_ids,
    post_cot,
    dual_cot,
    attend_weight,
    output_weight,
    expand_weight,
    contract_weight,
    head_bias,
    norm_params,
    attend_momentum,
    output_momentum,
    expand_momentum,
    contract_momentum,
    bias_momentum,
    norm_momentum,
    attend_variance,
    output_variance,
    expand_variance,
    contract_variance,
    bias_variance,
    norm_variance,
    clip_limit,
):
    n_dp, n_h = lax.axis_size("dp"), lax.axis_size("head")
    g, h = lax.axis_index("dp"), lax.axis_index("head")
    idx = jnp.stack([g, h]).astype(jnp.int32)
    rw = post_in.shape[0]
    n_rows = rw * n_h
    lh = HEADS // n_h
    width = lh * HD
    ds_rows = attend_weight.shape[0]
    a_cols = attend_weight.shape[1]
    units = expand_weight.shape[1]
    shares = head_bias.shape[1]
    dp_bits, h_bits = bits_of(n_dp), bits_of(n_h)
    a_steps = [("dp", b) for b in dp_bits]
    dp_steps, h_steps = [("dp", b) for b in dp_bits], [("head", b) for b in h_bits]
    e_steps = dp_steps + h_steps
    c_steps = dp_steps[:-1] + h_steps[:-1] + dp_steps[-1:] + h_steps[-1:]
    es_steps = dp_steps[:-1] + h_steps[:-1] + dp_steps[-1:] + h_steps[-1:]
    cs_steps = dp_steps[:1] + h_steps[:-1] + dp_steps[-1:] + dp_steps[1:-1] + h_steps[-1:]
    g_steps = dp_steps[:1] + dp_steps[-1:] + dp_steps[1:-1]

    bias_block = jnp.pad(
        head_bias.astype(BF).reshape(1, lh * shares), ((0, 15), (0, a_cols - lh * shares))
    )
    a_msg = jnp.concatenate([attend_weight.astype(BF), bias_block], axis=0)
    m_msg = jnp.concatenate(
        [expand_weight.astype(BF), contract_weight.T.astype(BF), output_weight.T.astype(BF)], axis=1
    )
    rows_own = after(post_in, a_msg).astype(BF)

    n_d, n_s = len(dp_bits), len(e_steps)
    a_in, a_got = [a_msg[None]], []
    for i, step in enumerate(a_steps):
        a_got.append(swap(a_in[i], step))
        if i < n_d - 1:
            a_in.append(jnp.concatenate([a_in[i], a_got[i]], axis=0))
    m_in, m_got = m_msg[None], None
    for i in range(n_d - 1):
        if i > 0:
            m_in = jnp.concatenate([m_in, after(m_got, a_got[i - 1])], axis=0)
        m_got = swap(m_in, e_steps[i])
    e_in, c_in = m_in[..., :units], m_in[..., units:]
    e_got, c_got = m_got[..., :units], m_got[..., units:]

    def exchange(i, *ready):
        nonlocal e_in, c_in, e_got, c_got
        e_in = jnp.concatenate([e_in, after(e_got, *ready)], axis=0)
        c_in = jnp.concatenate([c_in, after(c_got, *ready)], axis=0)
        e_got, c_got = swap(e_in, e_steps[i]), swap(c_in, c_steps[i])

    rows = {0: rows_own}
    for bit in h_bits:
        for off in list(rows):
            rows[off ^ bit] = swap(rows[off], ("head", bit))
    rows = [rows[off] for off in range(n_h)]
    exchange(n_d - 1)
    n_q = n_rows // TQ
    cols = lh * TQ
    q, k, v, vt, wg, inner = call(
        functools.partial(qkv_kernel, lh, n_dp, n_h, offsets(a_steps, "dp")),
        [sds((n_rows, width), BF)] * 3
        + [sds((width + 16, n_rows), BF), sds((D, 3 * width), BF), sds((16, width), BF)],
        [pltpu.VMEM((D, a_cols), BF), pltpu.VMEM((n_dp, lh * shares), F32)],
        1,
        [idx, after(a_in[-1], e_in, c_in), a_got[-1]] + rows,
        24,
        4,
    )

    def attend(offs, q):
        out = call(
            functools.partial(attend_kernel, lh, offs),
            [sds((rw + 16, width), BF)] * len(offs) + [sds((n_q // 2, 8, cols), F32)],
            [
                pltpu.SMEM((n_q // 2,), jnp.int32),
                pltpu.SMEM((n_q // 2,), jnp.int32),
                pltpu.VMEM((1, n_rows), F32),
                pltpu.VMEM((n_q // 2, 1, cols), jnp.int32),
                pltpu.VMEM((n_q // 2, cols, width), BF),
                pltpu.VMEM((n_q // 2, width + 16, cols), F32),
                pltpu.VMEM((n_q // 2, 1, cols), F32),
                pltpu.VMEM((TK, cols), F32),
                pltpu.VMEM((TK, cols), F32),
            ],
            1,
            [idx, segment_ids, q, k, vt, inner],
            24,
            1,
        )
        return out[:-1], out[-1]

    far, lse_far = attend(range(n_h // 2, n_h), q)
    exchange(n_d, far[0])
    early = n_d + 1 == n_s - 1
    crossed = [swap(e_in, e_steps[-1]), swap(c_in, c_steps[-1])] if early else []
    near, lse_near = attend(range(n_h // 2), after(q, far[0], e_in, c_in))
    for i in range(n_d + 1, n_s - 1):
        exchange(i, near[0])
    pieces = list(near) + list(far)
    mixed = [pieces[0]] + [
        lax.ppermute(pieces[off], "head", [(i, i ^ off) for i in range(n_h)]) for off in range(1, n_h)
    ]
    arrived = [near[0]] + mixed[n_h // 2 :]
    if not early:
        crossed = [swap(e_in, e_steps[-1]), swap(c_in, c_steps[-1])]
    e_got, c_got = after(e_got, *arrived), after(c_got, *arrived)
    e_parts = [e_in, e_got, crossed[0], swap(e_got, e_steps[-1])]
    c_parts = [c_in, c_got, crossed[1], swap(c_got, c_steps[-1])]

    half = n_dp * n_h // 2
    middle_out = call(
        functools.partial(middle_kernel, lh, n_dp, n_h, e_steps, c_steps, es_steps, cs_steps),
        [sds((rw, D), F32)] * 3
        + [sds((rw, width), BF)] * n_h
        + [sds((half, ds_rows, units), BF)] * 2
        + [sds((half, ds_rows, units + width), BF)] * 2
        + [sds((40, 128), F32)],
        [
            pltpu.VMEM((D, n_h * units), BF),
            pltpu.VMEM((D, n_h * units), BF),
            pltpu.VMEM((D, n_h * width), BF),
            pltpu.VMEM((rw, n_h * width), BF),
            pltpu.VMEM((n_h, 1, units), F32),
            pltpu.VMEM((rw, n_h * units), BF),
            pltpu.VMEM((rw, D), F32),
            pltpu.VMEM((rw, D), F32),
            pltpu.VMEM((rw, 128), F32),
            pltpu.VMEM((rw, D), F32),
            pltpu.VMEM((rw, D), BF),
            pltpu.VMEM((D, rw), BF),
            pltpu.VMEM((rw, D), BF),
            pltpu.VMEM((rw, D), F32),
            pltpu.VMEM((n_h, 1, units), F32),
            pltpu.VMEM((rw, n_h * units), BF),
            pltpu.VMEM((D, rw), BF),
        ],
        1,
        [idx, norm_params] + mixed + e_parts + c_parts + [post_in, dual_in, post_cot, dual_cot],
        34,
        20,
    )
    post_out, dual_out, grad_mid1 = middle_out[:3]
    gm = middle_out[3 : 3 + n_h]
    ge_keep, ge_send, gc_keep, gc_send, small_mid = middle_out[3 + n_h :]
    gm = [gm[0]] + [
        lax.ppermute(gm[off], "head", [(i, i ^ off) for i in range(n_h)]) for off in range(1, n_h)
    ]
    ge, gc = Scatter(ge_keep, ge_send, es_steps), Scatter(gc_keep, gc_send, cs_steps)
    gm[0] = after(gm[0], *ge.advance(), *gc.advance())
    gqkv, small = call(
        functools.partial(attend_back_kernel, lh, n_h),
        [sds((n_rows, 3 * width), BF), sds((48, 128), F32)],
        [
            pltpu.SMEM((n_q,), jnp.int32),
            pltpu.VMEM((n_q, width, cols), BF),
            pltpu.VMEM((n_q, width, cols), BF),
            pltpu.VMEM((n_q, 1, cols), F32),
            pltpu.VMEM((n_q, 1, cols), F32),
            pltpu.VMEM((n_q, 1, cols), jnp.int32),
            pltpu.VMEM((width, n_rows), BF),
            pltpu.VMEM((width, n_rows), F32),
            pltpu.VMEM((width, n_rows), F32),
            pltpu.VMEM((n_q, width, cols), F32),
        ]
        + [pltpu.VMEM((TK, cols), F32)] * 4,
        1,
        [idx, segment_ids, q, k, v, lse_near, lse_far, small_mid] + gm + pieces,
        32,
        15,
    )
    sent = ge.advance(gqkv) + gc.advance(gqkv)
    ga = call(
        functools.partial(attend_grad_kernel, lh, n_dp, n_h, g_steps),
        sds((n_dp, ds_rows, a_cols), BF),
        [pltpu.VMEM((D, 3 * width), F32)],
        1,
        [idx, after(gqkv, *sent)] + rows,
        24,
        2,
    )
    ga = Scatter(ga[: n_dp // 2], ga[n_dp // 2 :], g_steps)
    back = call(
        functools.partial(rows_back_kernel, n_h),
        [sds((rw, D), BF)] * n_h,
        [],
        1,
        [idx, after(gqkv, ga.send), wg],
        24,
        2,
    )
    sent = (back[0],)
    back = RowSums(back, sorted(h_bits, reverse=True))
    for i in range(n_s - 3):
        sent = ge.advance(*sent)
        sent = gc.advance(*sent)
        if i == 0:
            for _ in range(len(h_bits) - 1):
                sent = back.advance(*sent)
        if i < n_d - 1:
            sent = ga.advance(*sent)
    post_grad = back.finish(grad_mid1, *sent)
    pairs = [ga.keep, ga.got, ge.keep, ge.got, gc.keep, gc.got]
    squares = call(squares_kernel, sds((56, 128), F32), [], 0, [small] + pairs, 16, 1)
    order = h_steps[-1:] + [step for step in h_steps[:-1] + dp_steps[::-1]]
    groups = [order[:1]] + [order[i : i + 2] for i in range(1, len(order), 2)]
    sums = sum_groups(squares, groups, (post_grad,))
    flip = lambda arrays: [a.T if i in (1, 3) else a for i, a in enumerate(arrays)]
    params = flip([attend_weight, output_weight, expand_weight, contract_weight, head_bias, norm_params])
    momenta = flip(
        [attend_momentum, output_momentum, expand_momentum, contract_momentum, bias_momentum, norm_momentum]
    )
    variances = flip(
        [attend_variance, output_variance, expand_variance, contract_variance, bias_variance, norm_variance]
    )
    shapes = [sds((1,), F32), sds((6, D), F32)]
    for i, w in enumerate(params):
        shapes += [sds(w.shape, F32)] * 3 + ([sds(w.shape, BF)] if i < 5 else [])
    norm, norm_clipped, *results = call(
        functools.partial(adam_kernel, units, n_dp, lh, len(sums)),
        shapes,
        [pltpu.VMEM((48, 128), F32)],
        2,
        [idx, clip_limit] + sums + pairs + params + momenta + variances,
        24,
        2,
    )
    results = [a.T if i // 4 in (1, 3) else a for i, a in enumerate(results)]
    return (post_out, dual_out, post_grad, norm, *results, norm_clipped)


def solution(mesh):
    rows = P(("dp", "head"), None)
    tall, flat, rep = P("dp", "head"), P("head", "dp"), P()
    weights = (tall, flat, tall, flat, flat, rep)
    in_specs = (rows, rows, P("dp", None), rows, rows) + weights * 3 + (rep,)
    out_specs = (rows, rows, rows, rep)
    for spec in (tall, flat, tall, flat, flat):
        out_specs += (spec,) * 4
    out_specs += (rep,) * 4
    return jax.shard_map(per_device, mesh=mesh, in_specs=in_specs, out_specs=out_specs, check_vma=False)
```

```python
import functools

import jax
import jax.numpy as jnp
from jax import lax
from jax.experimental import pallas as pl
from jax.experimental.pallas import tpu as pltpu
from jax.sharding import PartitionSpec as P

D = 512
HEADS = 8
HD = 64
TQ = 256
TK = 256
CHUNK = 512

EPS_NORM = 1e-05
NEG_LARGE = -1e30
LOG2E = 1.4426950408889634
SCORE_SCALE = HD ** (-0.5)
RATES = (0.04, 0.12, 0.04, 0.04, 0.16, 0.3)
DECAY = 0.01
ADAM_EPS = 1e-08
BETA = 0.5
BIAS_CORRECTION = 0.875
BF = jnp.bfloat16
FLOPS_PER_US = 10**9
F32 = jnp.float32
VMEM = pl.BlockSpec(memory_space=pltpu.VMEM)
SMEM = pl.BlockSpec(memory_space=pltpu.SMEM)


def dot(a, b, ca, cb):
    return lax.dot_general(a, b, (((ca,), (cb,)), ((), ())), preferred_element_type=F32)


def bits_of(count):
    bits = []
    while count > 1:
        count //= 2
        bits.append(count)
    return bits


def swap(v, step):
    axis, bit = step
    count = lax.axis_size(axis)
    return lax.ppermute(v, axis, [(i, i ^ bit) for i in range(count)])


def offsets(steps, axis):
    offs = [0]
    for name, bit in steps:
        offs = offs + [o ^ (bit if name == axis else 0) for o in offs]
    return offs


def after(v, *ready):
    return lax.optimization_barrier((v, *ready))[0]


def place(steps, axis, off):
    pos = 0
    for k, (name, bit) in enumerate(steps):
        if name == axis:
            pos = pos + ((off // bit) % 2) * (1 << k)
    return pos


class Scatter:
    def __init__(self, keep, send, steps):
        self.keep, self.steps = keep, list(steps)
        self.got = swap(send, self.steps[-1])
        self.send = send

    def advance(self, *ready):
        self.keep, self.send = self.take(*ready)
        self.steps.pop()
        self.got = swap(self.send, self.steps[-1])
        return (self.send,)

    def take(self, *ready):
        half = self.keep.shape[0] // 2
        total = self.keep.astype(F32) + after(self.got, *ready).astype(F32)
        return total[:half].astype(BF), total[half:].astype(BF)


def swap_both(v, one, two):
    n_h = lax.axis_size("head")
    flip = sum(bit * (n_h if axis == "dp" else 1) for axis, bit in (one, two))
    return lax.ppermute(v, ("dp", "head"), [(i, i ^ flip) for i in range(n_h * lax.axis_size("dp"))])


def sum_groups(value, groups, ready):
    for i, group in enumerate(groups):
        got = [value] + [swap(value, step) for step in group]
        if len(group) == 2:
            got.append(swap_both(value, *group))
        if i == len(groups) - 1:
            return got
        if i == 1:
            got[1] = after(got[1], *ready)
        pairs = [a + b for a, b in zip(got[::2], got[1::2])]
        value = functools.reduce(lambda a, b: a + b, pairs)


class RowSums:
    def __init__(self, pieces, bits):
        self.parts, self.bits = {off: [piece] for off, piece in enumerate(pieces)}, list(bits)
        self.flights = []
        self.start()

    def start(self, *ready):
        bit = self.bits.pop()
        sends = []
        for off in [off for off in self.parts if off & bit]:
            parts = self.parts.pop(off)
            total = parts[0]
            if len(parts) > 1:
                total = functools.reduce(
                    lambda a, b: a + b, [parts[0].astype(F32)] + [after(p, *ready).astype(F32) for p in parts[1:]]
                ).astype(BF)
            self.parts[off ^ bit].append(swap(total, ("head", bit)))
            sends.append(total)
        return tuple(sends)

    def advance(self, *ready):
        return self.start(*ready) if self.bits else ()

    def finish(self, value, *ready):
        return functools.reduce(lambda a, b: a + b, [after(p, *ready).astype(F32) for p in self.parts[0]], value)


def lane_mask_stack(v, lh):
    if lh == 1:
        return v
    lane = lax.broadcasted_iota(jnp.int32, v.shape, 1)
    zero = jnp.zeros_like(v)
    return jnp.concatenate(
        [jnp.where((lane >= l * HD) & (lane < (l + 1) * HD), v, zero) for l in range(lh)], axis=0
    )


def row_mask_stack(vt, lh):
    if lh == 1:
        return vt
    row = lax.broadcasted_iota(jnp.int32, vt.shape, 0)
    zero = jnp.zeros_like(vt)
    return jnp.concatenate(
        [jnp.where((row >= l * HD) & (row < (l + 1) * HD), vt, zero) for l in range(lh)], axis=1
    )


def head_rows_merge(vt, lh):
    return jnp.concatenate(
        [vt[l * HD : (l + 1) * HD, l * TQ : (l + 1) * TQ] for l in range(lh)], axis=0
    )


def qkv_kernel(lh, n_dp, n_h, dp_offs, idx_ref, w_own, w_got, *refs):
    rows = refs[:n_h]
    q_ref, k_ref, v_ref, vt_ref, wg_ref, inner_ref, w_s, b_s = refs[n_h:]
    g, h = idx_ref[0], idx_ref[1]
    width = lh * HD
    ds_rows = D // n_dp
    rw = rows[0].shape[0]
    shares = b_s.shape[1] // lh
    for p in range(n_dp):
        block = g ^ dp_offs[p]
        w_ref, p = (w_own, p) if p < n_dp // 2 else (w_got, p - n_dp // 2)
        w_s[pl.ds(pl.multiple_of(block * ds_rows, ds_rows), ds_rows), :] = w_ref[p, :ds_rows, :]
        b_s[pl.ds(block, 1), :] = w_ref[p, ds_rows : ds_rows + 16, : lh * shares][:1].astype(F32)
    wide = w_s[...].astype(F32)
    wg = jnp.concatenate(
        [
            wide[:, l * 3 * HD + kind * HD : l * 3 * HD + (kind + 1) * HD]
            for kind in range(3)
            for l in range(lh)
        ],
        axis=1,
    ).astype(BF)
    wg_ref[...] = wg
    per_head = [
        jnp.concatenate([b_s[b : b + 1, l * shares : (l + 1) * shares] for b in range(n_dp)], axis=1)
        for l in range(lh)
    ]
    q_bias = jnp.concatenate([r[:, :HD] for r in per_head], axis=1)
    v_bias = jnp.concatenate([r[:, HD : 2 * HD] for r in per_head], axis=1)
    inner = jnp.concatenate([r[:, 2 * HD :] for r in per_head], axis=1)
    inner_ref[...] = jnp.concatenate(
        [inner[:, i * width : (i + 1) * width] for i in range(inner.shape[1] // width)]
        + [jnp.zeros((16 - inner.shape[1] // width, width), F32)],
        axis=0,
    ).astype(BF)
    for off in range(n_h):
        base = pl.multiple_of((h ^ off) * rw, rw)
        qkv = dot(rows[off][...], wg_ref[...], 1, 0)
        q_ref[pl.ds(base, rw), :] = (qkv[:, :width] + q_bias).astype(BF)
        k_ref[pl.ds(base, rw), :] = qkv[:, width : 2 * width].astype(BF)
        v_ref[pl.ds(base, rw), :] = (qkv[:, 2 * width :] + v_bias).astype(BF)
    vt_ref[:width, :] = v_ref[...].T
    vt_ref[width:, :] = jnp.ones((16, v_ref.shape[0]), BF)


def attend_kernel(lh, offs, idx_ref, seg_ref, q_ref, k_ref, vt_ref, inner_ref, *refs):
    pieces = refs[: len(offs)]
    lse_ref, qb_s, lo_s, all_s, start_s, q2_s, acc_s, top_s, slot_a, slot_b = refs[len(offs) :]
    h = idx_ref[1]
    width = lh * HD
    rw = pieces[0].shape[0] - 16
    per_piece = rw // TQ
    n_t = len(offs) * per_piece
    factor = SCORE_SCALE * LOG2E
    cols = lh * TQ
    column = lax.broadcasted_iota(jnp.int32, (1, cols), 1) % TQ
    all_s[...] = document_starts(seg_ref[...])
    n_pairs = 0
    for t in range(n_t):
        qb = (h ^ offs[t // per_piece]) * per_piece + t % per_piece
        at = pl.ds(pl.multiple_of(qb * TQ, TQ), TQ)
        start = all_s[:, at]
        lo = (jnp.min(start) * (1.0 / TK)).astype(jnp.int32)
        qb_s[t] = qb * (TQ // TK) + (TQ // TK - 1)
        lo_s[t] = lo
        n_pairs = n_pairs + qb_s[t] + 1 - lo
        start_s[t] = jnp.concatenate([start.astype(jnp.int32)] * lh, axis=1)
        q2_s[t] = lane_mask_stack(q_ref[at, :], lh)
    acc_s[...] = jnp.zeros_like(acc_s)
    top_s[...] = jnp.full(top_s.shape, NEG_LARGE, F32)

    def scores(t, kb, slot):
        keys = pl.ds(pl.multiple_of(kb * TK, TK), TK)
        slot[...] = dot(k_ref[keys, :], q2_s[t], 1, 1)

    def mix(t, kb, slot, least):
        c0 = pl.multiple_of(kb * TK, TK)
        key = lax.broadcasted_iota(jnp.int32, (TK, cols), 0)
        first = (qb_s[t] + 1) * TK - TQ
        ok = (key >= start_s[t] - c0 + least) & (key <= column + (first - c0))
        s = jnp.where(ok, slot[...], NEG_LARGE)
        old = top_s[t]
        top = jnp.maximum(old, jnp.max(s, axis=0, keepdims=True))
        p = jnp.exp2((s - top) * factor).astype(BF)
        acc_s[t] = acc_s[t] * jnp.exp2((old - top) * factor) + dot(vt_ref[:, pl.ds(c0, TK)], p, 1, 0)
        top_s[t] = top

    def following(t, kb):
        done = kb >= qb_s[t]
        nt = jnp.minimum(t + 1, n_t - 1)
        return jnp.where(done, nt, t), jnp.where(done, lo_s[nt], kb + 1)

    def two_pairs(i, carry):
        one = following(*carry)
        scores(*one, slot_b)
        mix(*carry, slot_a, 0)
        two = following(*one)
        scores(*two, slot_a)
        mix(*one, slot_b, jnp.where(2 * i + 1 < n_pairs, 0, 4 * q_ref.shape[0]))
        return two

    scores(0, lo_s[0], slot_a)
    lax.fori_loop(0, (n_pairs + 1) // 2, two_pairs, (jnp.int32(0), lo_s[0]))
    for t in range(n_t):
        total = acc_s[t, width : width + 1, :]
        out_t = head_rows_merge(acc_s[t, :width, :] / total, lh)
        inside = (t % per_piece) * TQ
        pieces[t // per_piece][inside : inside + TQ, :] = out_t.T.astype(BF)
        lse_ref[t] = jnp.broadcast_to(top_s[t] * factor + jnp.log2(total), (8, cols))
    for piece in pieces:
        piece[rw:, :] = inner_ref[...]


def document_starts(segment):
    seg = segment.astype(F32)
    start = jnp.zeros(seg.shape, F32)
    for s in range(HEADS):
        count = jnp.sum(jnp.where(seg == float(s), 1.0, 0.0), axis=1, keepdims=True)
        start = start + jnp.where(seg > float(s), count, 0.0)
    return start


def norm_back(grad, xhat, rstd, gain):
    g = grad * gain
    return rstd * (
        g - jnp.mean(g, axis=-1, keepdims=True) - xhat * jnp.mean(g * xhat, axis=-1, keepdims=True)
    )


def fold(v):
    return jnp.sum(v.reshape(v.shape[0] // 8, 8, v.shape[1]), axis=0)


def middle_kernel(lh, n_dp, n_h, e_steps, c_steps, es_steps, cs_steps, idx_ref, norm_ref, *refs):
    width = lh * HD
    mixed = refs[:n_h]
    e_parts, c_parts = refs[n_h : n_h + 4], refs[n_h + 4 : n_h + 8]
    post_in, dual_in, post_cot, dual_cot = refs[n_h + 8 : n_h + 12]
    outs = refs[n_h + 12 :]
    post_out, dual_out, gmid1_ref = outs[:3]
    gm = outs[3 : 3 + n_h]
    ge_keep, ge_send, gc_keep, gc_send, small_ref = outs[3 + n_h : 8 + n_h]
    (e_s, c_s, o_s, mix_s, bias_s, hid_s, acc_s, xh_s, rs_s, pn_s, xb_s, xt_s, gb_s, gmid2_s, ffb_s, gp_s, gt_s) = outs[
        8 + n_h :
    ]
    g, h = idx_ref[0], idx_ref[1]
    rw = post_in.shape[0]
    chunk = min(CHUNK, rw)
    ds_rows = D // n_dp
    units = hid_s.shape[1] // n_h
    row = lambda i: norm_ref[i : i + 1, :]

    e_dp, e_h = offsets(e_steps, "dp"), offsets(e_steps, "head")
    c_dp, c_h = offsets(c_steps, "dp"), offsets(c_steps, "head")
    quarter = n_dp * n_h // 4
    for p in range(n_dp * n_h):
        at = pl.ds(pl.multiple_of((g ^ e_dp[p]) * ds_rows, ds_rows), ds_rows)
        e_ref, c_ref, i = e_parts[p // quarter], c_parts[p // quarter], p % quarter
        e_s[at, e_h[p] * units : (e_h[p] + 1) * units] = e_ref[i]
        at = pl.ds(pl.multiple_of((g ^ c_dp[p]) * ds_rows, ds_rows), ds_rows)
        c_s[at, c_h[p] * units : (c_h[p] + 1) * units] = c_ref[i, :, :units]
        o_s[at, c_h[p] * width : (c_h[p] + 1) * width] = c_ref[i, :, units:]
    for off in range(n_h):
        mix_s[:, off * width : (off + 1) * width] = mixed[off][:rw, :]
        tail = mixed[off][rw : rw + 16, :].astype(F32)
        bias_s[off] = jnp.concatenate([tail[i : i + 1, :] for i in range(units // width)], axis=1)

    acc_s[...] = dot(mix_s[...], o_s[...], 1, 1)

    def chunk_one(i, carry):
        at = pl.ds(pl.multiple_of(i * chunk, chunk), chunk)
        attn_out = acc_s[at, :] + row(2)
        v = post_in[at, :] + attn_out
        centered = v - jnp.mean(v, axis=-1, keepdims=True)
        rstd = lax.rsqrt(jnp.mean(centered * centered, axis=-1, keepdims=True) + EPS_NORM)
        xhat = centered * rstd
        pn = xhat * row(0) + row(1)
        xh_s[at, :] = xhat
        rs_s[at, :] = jnp.broadcast_to(rstd, (chunk, 128))
        pn_s[at, :] = pn
        xb_s[at, :] = pn.astype(BF)
        dual_out[at, :] = dual_in[at, :] + attn_out
        return carry

    lax.fori_loop(0, rw // chunk, chunk_one, 0)
    xt_s[...] = xb_s[...].T
    for oh in range(n_h):
        part = slice(oh * units, (oh + 1) * units)
        pre = dot(xb_s[...], e_s[:, part], 1, 0) + bias_s[oh]
        hid_s[:, part] = jnp.maximum(pre, 0.0).astype(BF)
    acc_s[...] = dot(hid_s[...], c_s[...], 1, 1)

    def chunk_two(i, carry):
        gain_sum, shift_sum, ffn_sum = carry
        at = pl.ds(pl.multiple_of(i * chunk, chunk), chunk)
        ffn_out = acc_s[at, :] + row(5)
        v = pn_s[at, :] + ffn_out
        centered = v - jnp.mean(v, axis=-1, keepdims=True)
        rstd = lax.rsqrt(jnp.mean(centered * centered, axis=-1, keepdims=True) + EPS_NORM)
        xhat = centered * rstd
        post_out[at, :] = xhat * row(3) + row(4)
        dual_out[at, :] = dual_out[at, :] + ffn_out
        cot = post_cot[at, :]
        gmid2 = norm_back(cot, xhat, rstd, row(3))
        gffn = gmid2 + dual_cot[at, :]
        gmid2_s[at, :] = gmid2
        gb_s[at, :] = gffn.astype(BF)
        return gain_sum + fold(cot * xhat), shift_sum + fold(cot), ffn_sum + fold(gffn)

    zero = jnp.zeros((8, D), F32)
    gain2, shift2, ffn_sum = lax.fori_loop(0, rw // chunk, chunk_two, (zero, zero, zero))
    gt_s[...] = gb_s[...].T
    for oh in range(n_h):
        part = slice(oh * units, (oh + 1) * units)
        ge, gc = (ge_keep, gc_keep) if oh % 2 == 0 else (ge_send, gc_send)
        gh = dot(gb_s[...], c_s[:, part], 1, 0)
        gp = jnp.where(hid_s[:, part] > 0, gh, 0.0).astype(BF)
        gp_s[:, part] = gp
        ffb_s[oh] = jnp.sum(gp.astype(F32), axis=0, keepdims=True)
        grad_c = dot(gt_s[...], hid_s[:, part], 1, 0).astype(BF)
        grad_e = dot(xt_s[...], gp, 1, 0).astype(BF)
        e_at, c_at = place(es_steps, "head", oh - oh % 2), place(cs_steps, "head", oh - oh % 2)
        for b in range(n_dp):
            ge[place(es_steps, "dp", b ^ g) + e_at] = grad_e[b * ds_rows : (b + 1) * ds_rows]
            gc[place(cs_steps, "dp", b ^ g) + c_at, :, :units] = grad_c[b * ds_rows : (b + 1) * ds_rows]
    acc_s[...] = dot(gp_s[...], e_s[...], 1, 1)

    def chunk_three(i, carry):
        gain_sum, shift_sum, attn_sum = carry
        at = pl.ds(pl.multiple_of(i * chunk, chunk), chunk)
        grad = gmid2_s[at, :] + acc_s[at, :]
        xhat = xh_s[at, :]
        gmid1 = norm_back(grad, xhat, rs_s[at, :1], row(0))
        gmid1_ref[at, :] = gmid1
        gattn = gmid1 + dual_cot[at, :]
        gb_s[at, :] = gattn.astype(BF)
        return gain_sum + fold(grad * xhat), shift_sum + fold(grad), attn_sum + fold(gattn)

    gain1, shift1, attn_sum = lax.fori_loop(0, rw // chunk, chunk_three, (zero, zero, zero))
    grad_mixed = dot(gb_s[...], o_s[...], 1, 0).astype(BF)
    for off in range(n_h):
        gm[off][...] = grad_mixed[:, off * width : (off + 1) * width]
    grad_o = dot(gb_s[...].T, mix_s[...], 1, 0).astype(BF)
    for oh in range(n_h):
        gc = gc_keep if oh % 2 == 0 else gc_send
        for b in range(n_dp):
            gc[place(cs_steps, "dp", b ^ g) + place(cs_steps, "head", oh - oh % 2), :, units:] = grad_o[
                b * ds_rows : (b + 1) * ds_rows, oh * width : (oh + 1) * width
            ]
    for i, part in enumerate((gain1, shift1, attn_sum, gain2, shift2, ffn_sum)):
        line = jnp.sum(part, axis=0, keepdims=True)
        for j in range(D // 128):
            small_ref[4 * i + j : 4 * i + j + 1, :] = line[:, j * 128 : (j + 1) * 128]
    for oh in range(n_h):
        first = 24 + (h ^ oh) * (units // 128)
        for j in range(units // 128):
            small_ref[pl.ds(first + j, 1), :] = ffb_s[oh, :, j * 128 : (j + 1) * 128]


def first_key_blocks(start, lo_ref):
    total = 0
    for qb in range(start.shape[1] // TQ):
        lo = (jnp.min(start[:, qb * TQ : (qb + 1) * TQ]) * (1.0 / TK)).astype(jnp.int32)
        lo_ref[qb] = lo
        total = total + ((qb + 1) * (TQ // TK) - lo)
    return total


def next_pair(qb, kb, lo_ref, last):
    done = kb >= (qb + 1) * (TQ // TK) - 1
    following = jnp.minimum(qb + 1, last)
    return jnp.where(done, following, qb), jnp.where(done, lo_ref[following], kb + 1)


def attend_back_kernel(lh, n_h, idx_ref, seg_ref, q_ref, k_ref, v_ref, lse_near, lse_far, small_in, *refs):
    gm, pieces = refs[:n_h], refs[n_h : 2 * n_h]
    gqkv_ref, small_ref, lo_s, q2_s, do2_s, delta_s, lse_s, start_s, kt_s, dk_s, dv_s, dq_s = refs[
        2 * n_h : 2 * n_h + 12
    ]
    slots = (refs[2 * n_h + 12 : 2 * n_h + 14], refs[2 * n_h + 14 :])
    h = idx_ref[1]
    width = lh * HD
    rw = gm[0].shape[0]
    n_rows = q_ref.shape[0]
    n_q = n_rows // TQ
    cols = lh * TQ
    factor = SCORE_SCALE * LOG2E
    starts = document_starts(seg_ref[...])
    n_pairs = first_key_blocks(starts, lo_s)
    starts = starts.astype(jnp.int32)
    for qb in range(n_q):
        start_s[qb] = jnp.concatenate([starts[:, qb * TQ : (qb + 1) * TQ]] * lh, axis=1)
        q2_s[qb] = row_mask_stack(q_ref[qb * TQ : (qb + 1) * TQ, :].T, lh)
    for off in range(n_h):
        lse_part, n = (lse_near, off) if off < n_h // 2 else (lse_far, off - n_h // 2)
        for i in range(rw // TQ):
            qb = (h ^ off) * (rw // TQ) + i
            do = gm[off][i * TQ : (i + 1) * TQ, :]
            do2_s[qb] = row_mask_stack(do.T, lh)
            prod = (do.astype(F32) * pieces[off][i * TQ : (i + 1) * TQ, :].astype(F32)).T
            delta_s[qb] = jnp.concatenate(
                [jnp.sum(prod[l * HD : (l + 1) * HD, :], axis=0, keepdims=True) for l in range(lh)], axis=1
            )
            lse_s[qb] = lse_part[n * (rw // TQ) + i][:1]
    kt_s[...] = k_ref[...].T
    dk_s[...] = jnp.zeros_like(dk_s)
    dv_s[...] = jnp.zeros_like(dv_s)
    dq_s[...] = jnp.zeros_like(dq_s)
    column = lax.broadcasted_iota(jnp.int32, (1, cols), 1) % TQ

    def products(qb, kb, slot):
        keys = pl.ds(pl.multiple_of(kb * TK, TK), TK)
        slot[0][...] = dot(k_ref[keys, :], q2_s[qb], 1, 0)
        slot[1][...] = dot(v_ref[keys, :], do2_s[qb], 1, 0)

    def gradients(qb, kb, slot, least):
        c0 = pl.multiple_of(kb * TK, TK)
        keys = pl.ds(c0, TK)
        key = lax.broadcasted_iota(jnp.int32, (TK, cols), 0)
        ok = (key >= start_s[qb] - c0 + least) & (key <= column + (qb * TQ - c0))
        p = jnp.exp2(jnp.where(ok, slot[0][...], NEG_LARGE) * factor - lse_s[qb])
        grad = (p * (slot[1][...] - delta_s[qb])).astype(BF)
        dv_s[:, keys] += dot(do2_s[qb], p.astype(BF), 1, 1)
        dk_s[:, keys] += dot(q2_s[qb], grad, 1, 1)
        dq_s[qb] += dot(kt_s[:, keys], grad, 1, 0)

    products(0, 0, slots[0])

    def two_pairs(i, carry):
        qb, kb = carry
        one = next_pair(qb, kb, lo_s, n_q - 1)
        products(*one, slots[1])
        gradients(qb, kb, slots[0], 0)
        two = next_pair(*one, lo_s, n_q - 1)
        products(*two, slots[0])
        gradients(*one, slots[1], jnp.where(2 * i + 1 < n_pairs, 0, 2 * n_rows))
        return two

    lax.fori_loop(0, (n_pairs + 1) // 2, two_pairs, (jnp.int32(0), jnp.int32(0)))
    q_sum = jnp.zeros((1, width), F32)
    for qb in range(n_q):
        dq = (head_rows_merge(dq_s[qb], lh) * SCORE_SCALE).T.astype(BF)
        gqkv_ref[qb * TQ : (qb + 1) * TQ, :width] = dq
        q_sum = q_sum + jnp.sum(dq.astype(F32), axis=0, keepdims=True)
    gqkv_ref[:, width : 2 * width] = (dk_s[...] * SCORE_SCALE).astype(BF).T
    dv = dv_s[...].astype(BF).T
    gqkv_ref[:, 2 * width :] = dv
    v_sum = jnp.sum(dv.astype(F32), axis=0, keepdims=True)
    small_ref[:40, :] = small_in[...]
    small_ref[40:, :] = jnp.zeros((8, 128), F32)
    for l in range(lh):
        small_ref[pl.ds(40 + h * lh + l, 1), :] = jnp.concatenate(
            [q_sum[:, l * HD : (l + 1) * HD], v_sum[:, l * HD : (l + 1) * HD]], axis=1
        )


def rows_back_kernel(n_h, idx_ref, gqkv_ref, wg_ref, *outs):
    h = idx_ref[1]
    rw = outs[0].shape[0]
    for off in range(n_h):
        at = pl.ds(pl.multiple_of((h ^ off) * rw, rw), rw)
        outs[off][...] = dot(gqkv_ref[at, :], wg_ref[...], 1, 1).astype(BF)


def attend_grad_kernel(lh, n_dp, n_h, steps, idx_ref, gqkv_ref, *refs):
    rows = refs[:n_h]
    out_ref, acc_s = refs[n_h:]
    g, h = idx_ref[0], idx_ref[1]
    rw = rows[0].shape[0]
    ds_rows = D // n_dp
    width = lh * HD
    for off in range(n_h):
        at = pl.ds(pl.multiple_of((h ^ off) * rw, rw), rw)
        part = dot(rows[off][...], gqkv_ref[at, :], 0, 0)
        acc_s[...] = part if off == 0 else acc_s[...] + part
    full = acc_s[...]
    full = jnp.concatenate(
        [full[:, kind * width + l * HD : kind * width + (l + 1) * HD] for l in range(lh) for kind in range(3)],
        axis=1,
    ).astype(BF)
    for b in range(n_dp):
        out_ref[place(steps, "dp", b ^ g)] = full[b * ds_rows : (b + 1) * ds_rows]


def total_of_pair(keep_ref, got_ref):
    return keep_ref[0].astype(F32) + got_ref[0].astype(F32)


def squares_kernel(small_ref, *refs):
    out_ref = refs[-1]
    acc = jnp.zeros((8, 128), F32)
    for i in range(0, len(refs) - 1, 2):
        v = total_of_pair(refs[i], refs[i + 1])
        v = fold(v * v)
        if v.shape[1] % 128:
            v = jnp.concatenate([v, jnp.zeros((8, 128 - v.shape[1] % 128), F32)], axis=1)
        for j in range(v.shape[1] // 128):
            acc = acc + v[:, j * 128 : (j + 1) * 128]
    out_ref[:8, :] = acc
    out_ref[8:, :] = small_ref[...]


def adam_kernel(units, n_dp, lh, n_sums, idx_ref, clip_ref, *refs):
    sums, refs = [r[...] for r in refs[:n_sums]], refs[n_sums:]
    sums = [a + b for a, b in zip(sums[::2], sums[1::2])]
    sums = functools.reduce(lambda a, b: a + b, sums)
    params, momenta, variances = refs[6:12], refs[12:18], refs[18:24]
    norm_ref, clipped_ref = refs[24:26]
    outs, small_s = list(refs[26:-1]), refs[-1]
    g, h = idx_ref[0], idx_ref[1]
    small = sums[8:, :]
    small_s[...] = small
    squares = jnp.sum(sums[:8, :]) + jnp.sum(small * small)
    norm_grads = jnp.concatenate(
        [
            jnp.concatenate([small[4 * i + j : 4 * i + j + 1, :] for j in range(D // 128)], axis=1)
            for i in range(6)
        ],
        axis=0,
    )
    width = params[4].shape[1]
    bias_rows = []
    for l in range(lh):
        head = h * lh + l
        full = jnp.concatenate(
            [small_s[pl.ds(at, 1), :] for at in (40 + head, 24 + 2 * head, 25 + 2 * head)], axis=1
        )
        share = jnp.zeros((1, width), F32)
        for b in range(n_dp):
            share = share + jnp.where(g == b, full[:, b * width : (b + 1) * width], 0.0)
        bias_rows.append(share)
    share_bias = jnp.concatenate(bias_rows, axis=0)
    norm = jnp.sqrt(jnp.full((8, 128), squares))
    norm_ref[0] = jnp.max(norm)
    limit = clip_ref[0]
    factor = (limit / jnp.maximum(norm, limit))[:1, :1]
    shares = total_of_pair(refs[4], refs[5])
    grads = (
        total_of_pair(refs[0], refs[1]),
        shares[:, units:],
        total_of_pair(refs[2], refs[3]),
        shares[:, :units],
        share_bias,
        norm_grads,
    )
    for w, m, va, grad, rate in zip(params, momenta, variances, grads, RATES):
        clipped = factor * grad
        momentum_new = BETA * m[...] + (1.0 - BETA) * clipped
        variance_new = BETA * va[...] + (1.0 - BETA) * clipped * clipped
        step = momentum_new / BIAS_CORRECTION / (jnp.sqrt(variance_new / BIAS_CORRECTION) + ADAM_EPS)
        master_new = w[...] - rate * (step + DECAY * w[...])
        outs.pop(0)[...] = momentum_new
        outs.pop(0)[...] = variance_new
        outs.pop(0)[...] = master_new
        if len(outs) > 2:
            outs.pop(0)[...] = master_new.astype(BF)
    clipped_ref[...] = factor * norm_grads


def call(body, outs, scratch, n_smem, args, limit, us):
    return pl.pallas_call(
        body,
        out_shape=outs,
        in_specs=[SMEM] * n_smem + [VMEM] * (len(args) - n_smem),
        out_specs=jax.tree.map(lambda o: SMEM if o.shape == (1,) else VMEM, outs),
        scratch_shapes=scratch,
        compiler_params=pltpu.CompilerParams(vmem_limit_bytes=limit << 20),
        cost_estimate=pl.CostEstimate(flops=us * FLOPS_PER_US, bytes_accessed=1 << 20, transcendentals=0),
    )(*args)


def sds(shape, dtype):
    return jax.ShapeDtypeStruct(shape, dtype)


def per_device(
    post_in,
    dual_in,
    segment_ids,
    post_cot,
    dual_cot,
    attend_weight,
    output_weight,
    expand_weight,
    contract_weight,
    head_bias,
    norm_params,
    attend_momentum,
    output_momentum,
    expand_momentum,
    contract_momentum,
    bias_momentum,
    norm_momentum,
    attend_variance,
    output_variance,
    expand_variance,
    contract_variance,
    bias_variance,
    norm_variance,
    clip_limit,
):
    n_dp, n_h = lax.axis_size("dp"), lax.axis_size("head")
    g, h = lax.axis_index("dp"), lax.axis_index("head")
    idx = jnp.stack([g, h]).astype(jnp.int32)
    rw = post_in.shape[0]
    n_rows = rw * n_h
    lh = HEADS // n_h
    width = lh * HD
    ds_rows = attend_weight.shape[0]
    a_cols = attend_weight.shape[1]
    units = expand_weight.shape[1]
    shares = head_bias.shape[1]
    dp_bits, h_bits = bits_of(n_dp), bits_of(n_h)
    a_steps = [("dp", b) for b in dp_bits]
    dp_steps, h_steps = [("dp", b) for b in dp_bits], [("head", b) for b in h_bits]
    e_steps = dp_steps + h_steps
    c_steps = dp_steps[:-1] + h_steps[:-1] + dp_steps[-1:] + h_steps[-1:]
    es_steps = dp_steps[:-1] + h_steps[:-1] + dp_steps[-1:] + h_steps[-1:]
    cs_steps = dp_steps[:1] + h_steps[:-1] + dp_steps[-1:] + dp_steps[1:-1] + h_steps[-1:]
    g_steps = dp_steps[:1] + dp_steps[-1:] + dp_steps[1:-1]

    bias_block = jnp.pad(
        head_bias.astype(BF).reshape(1, lh * shares), ((0, 15), (0, a_cols - lh * shares))
    )
    a_msg = jnp.concatenate([attend_weight.astype(BF), bias_block], axis=0)
    m_msg = jnp.concatenate(
        [expand_weight.astype(BF), contract_weight.T.astype(BF), output_weight.T.astype(BF)], axis=1
    )
    rows_own = after(post_in, a_msg).astype(BF)

    n_d, n_s = len(dp_bits), len(e_steps)
    a_in, a_got = [a_msg[None]], []
    for i, step in enumerate(a_steps):
        a_got.append(swap(a_in[i], step))
        if i < n_d - 1:
            a_in.append(jnp.concatenate([a_in[i], a_got[i]], axis=0))
    m_in, m_got = m_msg[None], None
    for i in range(n_d - 1):
        if i > 0:
            m_in = jnp.concatenate([m_in, after(m_got, a_got[i - 1])], axis=0)
        m_got = swap(m_in, e_steps[i])
    e_in, c_in = m_in[..., :units], m_in[..., units:]
    e_got, c_got = m_got[..., :units], m_got[..., units:]

    def exchange(i, *ready):
        nonlocal e_in, c_in, e_got, c_got
        e_in = jnp.concatenate([e_in, after(e_got, *ready)], axis=0)
        c_in = jnp.concatenate([c_in, after(c_got, *ready)], axis=0)
        e_got, c_got = swap(e_in, e_steps[i]), swap(c_in, c_steps[i])

    rows = {0: rows_own}
    for bit in h_bits:
        for off in list(rows):
            rows[off ^ bit] = swap(rows[off], ("head", bit))
    rows = [rows[off] for off in range(n_h)]
    exchange(n_d - 1)
    n_q = n_rows // TQ
    cols = lh * TQ
    q, k, v, vt, wg, inner = call(
        functools.partial(qkv_kernel, lh, n_dp, n_h, offsets(a_steps, "dp")),
        [sds((n_rows, width), BF)] * 3
        + [sds((width + 16, n_rows), BF), sds((D, 3 * width), BF), sds((16, width), BF)],
        [pltpu.VMEM((D, a_cols), BF), pltpu.VMEM((n_dp, lh * shares), F32)],
        1,
        [idx, after(a_in[-1], e_in, c_in), a_got[-1]] + rows,
        24,
        4,
    )

    def attend(offs, q):
        out = call(
            functools.partial(attend_kernel, lh, offs),
            [sds((rw + 16, width), BF)] * len(offs) + [sds((n_q // 2, 8, cols), F32)],
            [
                pltpu.SMEM((n_q // 2,), jnp.int32),
                pltpu.SMEM((n_q // 2,), jnp.int32),
                pltpu.VMEM((1, n_rows), F32),
                pltpu.VMEM((n_q // 2, 1, cols), jnp.int32),
                pltpu.VMEM((n_q // 2, cols, width), BF),
                pltpu.VMEM((n_q // 2, width + 16, cols), F32),
                pltpu.VMEM((n_q // 2, 1, cols), F32),
                pltpu.VMEM((TK, cols), F32),
                pltpu.VMEM((TK, cols), F32),
            ],
            1,
            [idx, segment_ids, q, k, vt, inner],
            24,
            1,
        )
        return out[:-1], out[-1]

    far, lse_far = attend(range(n_h // 2, n_h), q)
    exchange(n_d, far[0])
    early = n_d + 1 == n_s - 1
    crossed = [swap(e_in, e_steps[-1]), swap(c_in, c_steps[-1])] if early else []
    near, lse_near = attend(range(n_h // 2), after(q, far[0], e_in, c_in))
    for i in range(n_d + 1, n_s - 1):
        exchange(i, near[0])
    pieces = list(near) + list(far)
    mixed = [pieces[0]] + [
        lax.ppermute(pieces[off], "head", [(i, i ^ off) for i in range(n_h)]) for off in range(1, n_h)
    ]
    arrived = [near[0]] + mixed[n_h // 2 :]
    if not early:
        crossed = [swap(e_in, e_steps[-1]), swap(c_in, c_steps[-1])]
    e_got, c_got = after(e_got, *arrived), after(c_got, near[0])
    e_parts = [e_in, e_got, crossed[0], swap(e_got, e_steps[-1])]
    c_parts = [c_in, c_got, crossed[1], swap(c_got, c_steps[-1])]

    half = n_dp * n_h // 2
    middle_out = call(
        functools.partial(middle_kernel, lh, n_dp, n_h, e_steps, c_steps, es_steps, cs_steps),
        [sds((rw, D), F32)] * 3
        + [sds((rw, width), BF)] * n_h
        + [sds((half, ds_rows, units), BF)] * 2
        + [sds((half, ds_rows, units + width), BF)] * 2
        + [sds((40, 128), F32)],
        [
            pltpu.VMEM((D, n_h * units), BF),
            pltpu.VMEM((D, n_h * units), BF),
            pltpu.VMEM((D, n_h * width), BF),
            pltpu.VMEM((rw, n_h * width), BF),
            pltpu.VMEM((n_h, 1, units), F32),
            pltpu.VMEM((rw, n_h * units), BF),
            pltpu.VMEM((rw, D), F32),
            pltpu.VMEM((rw, D), F32),
            pltpu.VMEM((rw, 128), F32),
            pltpu.VMEM((rw, D), F32),
            pltpu.VMEM((rw, D), BF),
            pltpu.VMEM((D, rw), BF),
            pltpu.VMEM((rw, D), BF),
            pltpu.VMEM((rw, D), F32),
            pltpu.VMEM((n_h, 1, units), F32),
            pltpu.VMEM((rw, n_h * units), BF),
            pltpu.VMEM((D, rw), BF),
        ],
        1,
        [idx, norm_params] + mixed + e_parts + c_parts + [post_in, dual_in, post_cot, dual_cot],
        34,
        20,
    )
    post_out, dual_out, grad_mid1 = middle_out[:3]
    gm = middle_out[3 : 3 + n_h]
    ge_keep, ge_send, gc_keep, gc_send, small_mid = middle_out[3 + n_h :]
    gm = [gm[0]] + [
        lax.ppermute(gm[off], "head", [(i, i ^ off) for i in range(n_h)]) for off in range(1, n_h)
    ]
    ge, gc = Scatter(ge_keep, ge_send, es_steps), Scatter(gc_keep, gc_send, cs_steps)
    gm[0] = after(gm[0], *ge.advance(), *gc.advance())
    gqkv, small = call(
        functools.partial(attend_back_kernel, lh, n_h),
        [sds((n_rows, 3 * width), BF), sds((48, 128), F32)],
        [
            pltpu.SMEM((n_q,), jnp.int32),
            pltpu.VMEM((n_q, width, cols), BF),
            pltpu.VMEM((n_q, width, cols), BF),
            pltpu.VMEM((n_q, 1, cols), F32),
            pltpu.VMEM((n_q, 1, cols), F32),
            pltpu.VMEM((n_q, 1, cols), jnp.int32),
            pltpu.VMEM((width, n_rows), BF),
            pltpu.VMEM((width, n_rows), F32),
            pltpu.VMEM((width, n_rows), F32),
            pltpu.VMEM((n_q, width, cols), F32),
        ]
        + [pltpu.VMEM((TK, cols), F32)] * 4,
        1,
        [idx, segment_ids, q, k, v, lse_near, lse_far, small_mid] + gm + pieces,
        32,
        15,
    )
    sent = ge.advance(gqkv) + gc.advance(gqkv)
    ga = call(
        functools.partial(attend_grad_kernel, lh, n_dp, n_h, g_steps),
        sds((n_dp, ds_rows, a_cols), BF),
        [pltpu.VMEM((D, 3 * width), F32)],
        1,
        [idx, after(gqkv, *sent)] + rows,
        24,
        2,
    )
    ga = Scatter(ga[: n_dp // 2], ga[n_dp // 2 :], g_steps)
    back = call(
        functools.partial(rows_back_kernel, n_h),
        [sds((rw, D), BF)] * n_h,
        [],
        1,
        [idx, after(gqkv, ga.send), wg],
        24,
        2,
    )
    sent = (back[0],)
    back = RowSums(back, sorted(h_bits, reverse=True))
    for i in range(n_s - 3):
        sent = ge.advance(*sent)
        sent = gc.advance(*sent)
        if i == 0:
            for _ in range(len(h_bits) - 1):
                sent = back.advance(*sent)
        if i < n_d - 1:
            sent = ga.advance(*sent)
    post_grad = back.finish(grad_mid1, *sent)
    pairs = [ga.keep, ga.got, ge.keep, ge.got, gc.keep, gc.got]
    squares = call(squares_kernel, sds((56, 128), F32), [], 0, [small] + pairs, 16, 1)
    order = h_steps[-1:] + [step for step in h_steps[:-1] + dp_steps[::-1]]
    groups = [order[:1]] + [order[i : i + 2] for i in range(1, len(order), 2)]
    sums = sum_groups(squares, groups, (post_grad,))
    flip = lambda arrays: [a.T if i in (1, 3) else a for i, a in enumerate(arrays)]
    params = flip([attend_weight, output_weight, expand_weight, contract_weight, head_bias, norm_params])
    momenta = flip(
        [attend_momentum, output_momentum, expand_momentum, contract_momentum, bias_momentum, norm_momentum]
    )
    variances = flip(
        [attend_variance, output_variance, expand_variance, contract_variance, bias_variance, norm_variance]
    )
    shapes = [sds((1,), F32), sds((6, D), F32)]
    for i, w in enumerate(params):
        shapes += [sds(w.shape, F32)] * 3 + ([sds(w.shape, BF)] if i < 5 else [])
    norm, norm_clipped, *results = call(
        functools.partial(adam_kernel, units, n_dp, lh, len(sums)),
        shapes,
        [pltpu.VMEM((48, 128), F32)],
        2,
        [idx, clip_limit] + sums + pairs + params + momenta + variances,
        24,
        2,
    )
    results = [a.T if i // 4 in (1, 3) else a for i, a in enumerate(results)]
    return (post_out, dual_out, post_grad, norm, *results, norm_clipped)


def solution(mesh):
    rows = P(("dp", "head"), None)
    tall, flat, rep = P("dp", "head"), P("head", "dp"), P()
    weights = (tall, flat, tall, flat, flat, rep)
    in_specs = (rows, rows, P("dp", None), rows, rows) + weights * 3 + (rep,)
    out_specs = (rows, rows, rows, rep)
    for spec in (tall, flat, tall, flat, flat):
        out_specs += (spec,) * 4
    out_specs += (rep,) * 4
    return jax.shard_map(per_device, mesh=mesh, in_specs=in_specs, out_specs=out_specs, check_vma=False)
```
